32 devices in a mesh: fsdp: 32 (over z, y, x, core).
Axes of the slice: x: 2, y: 2, z: 4, core: 2. Of those that a mesh axis runs over, the one named last changes fastest.
Arguments:
- inputs: bfloat16 [8192, 384], P('fsdp'), may hold values from -6 to 6
- attn_blocks: bfloat16 [32, 18560], P('fsdp')
- mlp_blocks: bfloat16 [32, 36992], P('fsdp')
- image_id: int32 [8192], P('fsdp'), may hold values from 0 to 42, as said below
- bias_id: int32 [8192], P('fsdp'), may hold values from 0 to 15
- out_grad: bfloat16 [8192, 384], P('fsdp'), may hold values from -6 to 6
Outputs:
- output: bfloat16 [8192, 384], P('fsdp')
- grad_inputs: float32 [8192, 384], P('fsdp')
- grad_attn: float32 [32, 18560], P('fsdp')
- grad_mlp: float32 [32, 36992], P('fsdp')
The draws below stay inside these ranges and needn't reach their ends.
Inputs may be any that keep to these rules, and one draw needn't show every extreme that they name: `image_id`: tokens of one image are contiguous and image numbers rise by one from image to image, starting at 0 and ending at (42); every image holds 197 tokens except the first and the last, which may hold fewer.
All inputs are finite; a program needn't handle non-finite values.
Results may differ from the reference program's by a relative error of at most 0.009.
Values may be sent and summed in bfloat16 or wider, within the bound.
No kernel may reach another device: no remote copies, remote signals or barrier semaphores. Data moves between devices by JAX's collectives and lax.ppermute only.
A program may use at most 128 MiB of HBM per device.

```python
import math
import jax
import jax.numpy as jnp
from jax import lax

D = 384
FF = 1536
HEADS = 6
HEAD_DIM = 64
IMG = 197
NB = 16
TOKENS = 8192
BLOCK_A = 18560
BLOCK_M = 36992
N_FSDP = 32


def layered_values(noise_values, layout):
    position = jnp.arange(noise_values.shape[0], dtype=jnp.int32)
    spread = jnp.zeros(noise_values.shape, jnp.float32)
    centre = jnp.zeros(noise_values.shape, jnp.float32)
    offset = 0
    for amount, deviation, middle in layout:
        inside = (position >= offset) & (position < offset + amount)
        spread = jnp.where(inside, deviation, spread)
        centre = jnp.where(inside, middle, centre)
        offset += amount
    return noise_values * spread + centre


def draw_attn_blocks(key, part):
    key = jax.random.fold_in(key, 1)
    entries = N_FSDP * BLOCK_A
    noise_values = jax.random.normal(key, (entries,), jnp.float32)
    layout = [(D, 0.1, 1.0), (D, 0.2, 0.0), (3 * D * D, D ** (-0.5), 0.0), (D, 0.2, 0.0), (D, 0.2, 0.0), (D * D, math.sqrt(IMG / (3.0 * D)), 0.0), (D, 0.2, 0.0), (NB * HEADS, 1.0, 0.0)]
    return layered_values(noise_values, layout).reshape(N_FSDP, BLOCK_A).astype(jnp.bfloat16)


def draw_mlp_blocks(key, part):
    key = jax.random.fold_in(key, 2)
    entries = N_FSDP * BLOCK_M
    noise_values = jax.random.normal(key, (entries,), jnp.float32)
    layout = [(D, 0.1, 1.0), (D, 0.2, 0.0), (D * FF, D ** (-0.5), 0.0), (FF, 0.2, 0.0), (FF * D, FF ** (-0.5), 0.0), (D, 0.2, 0.0)]
    return layered_values(noise_values, layout).reshape(N_FSDP, BLOCK_M).astype(jnp.bfloat16)


def draw_image_id(key, part):
    key = jax.random.fold_in(key, 3)
    last_image = (TOKENS + IMG - 2) // IMG
    lowest_offset = last_image * IMG - TOKENS + 1
    first_offset = jax.random.randint(key, (), lowest_offset, IMG, dtype=jnp.int32)
    return ((jnp.arange(TOKENS, dtype=jnp.int32) + first_offset) // IMG).astype(jnp.int32)


def set_ends(values, own_key, least, top_value):
    dims = values.shape
    spot = [jax.random.randint(jax.random.fold_in(own_key, axis), (), 0, dims[axis]) for axis in range(len(dims))]
    values = values.at[tuple(spot)].set(least)
    longest = dims.index(max(dims))
    spot[longest] = (spot[longest] + 1) % dims[longest]
    return values.at[tuple(spot)].set(top_value)


def shard_levels(own_key, dims, shards, least, high):
    def one(dim, shards_of):
        steps = jax.random.uniform(jax.random.fold_in(jax.random.fold_in(own_key, 6), dim), (shards_of,), jnp.float32, least / len(shards), high / len(shards))
        return jnp.repeat(jnp.exp(steps), dims[dim] // shards_of).reshape((-1,) + (1,) * (len(dims) - dim - 1))

    gain = one(*shards[0])
    for cut in shards[1:]:
        gain = gain * one(*cut)
    return gain


def bell_draw(own_key, dims, scale, limit, split=(), kind=jnp.bfloat16):
    values = scale * jax.random.normal(own_key, dims, jnp.float32)
    if split:
        values = values * shard_levels(own_key, dims, split, -0.22, 0.18)
    return jnp.clip(values, -limit, limit).astype(kind)


def setup_inputs(seed: int = 0) -> dict:
    key_list = jax.random.split(jax.random.key(seed), 7)
    inputs = bell_draw(key_list[0], (TOKENS, D), 1.0, 6.0, ((0, 32),))
    attn_blocks = draw_attn_blocks(jax.random.fold_in(key_list[6], 71), 0)
    mlp_blocks = draw_mlp_blocks(jax.random.fold_in(key_list[6], 71), 0)
    image_id = draw_image_id(jax.random.fold_in(key_list[6], 71), 0)
    bias_id = set_ends(jax.random.randint(key_list[4], (TOKENS,), 0, NB), jax.random.fold_in(key_list[4], 1), 0, NB - 1).astype(jnp.int32)
    out_grad = bell_draw(key_list[5], (TOKENS, D), 1.0, 6.0, ((0, 32),))
    return {"inputs": inputs, "attn_blocks": attn_blocks, "mlp_blocks": mlp_blocks, "image_id": image_id, "bias_id": bias_id, "out_grad": out_grad}


@jax.custom_vjp
def low(v):
    return lax.optimization_barrier(v.astype(jnp.bfloat16)).astype(jnp.float32)

@jax.custom_vjp
def low_back(v):
    return v

def low_keep(v):
    return (low(v), None)

def low_pass(kept, grad):
    return (grad,)

def back_keep(v):
    return (v, None)

def back_low(kept, grad):
    return (low(grad),)
low.defvjp(low_keep, low_pass)
low_back.defvjp(back_keep, back_low)
epsilon = 1e-06
highest = lax.Precision.HIGHEST

def attention_shapes():
    return [(D,), (D,), (D, 3 * D), (D,), (D,), (D, D), (D,), (NB, HEADS)]

def feed_shapes():
    return [(D,), (D,), (D, FF), (FF,), (FF, D), (D,)]

def cut_pieces(flat, shapes):
    pieces = []
    offset = 0
    for piece_shape in shapes:
        amount = math.prod(piece_shape)
        pieces.append(flat[offset:offset + amount].reshape(piece_shape))
        offset += amount
    return pieces

def layer_norm(values, norm_gain, norm_shift):
    average = lax.optimization_barrier(jnp.mean(values, axis=-1, keepdims=True))
    centred = values - average
    variance = lax.optimization_barrier(jnp.mean(centred * centred, axis=-1, keepdims=True))
    return centred * lax.rsqrt(variance + epsilon) * norm_gain + norm_shift

def product(left, right):
    return jnp.dot(left, right, precision=highest, preferred_element_type=jnp.float32)

def forward(inputs, attn_flat, feed_flat, image_id, bias_id):
    gain_one, shift_one, w_qkv, bias_query, bias_value, w_out, bias_out, bias_table = cut_pieces(attn_flat.reshape(-1), attention_shapes())
    gain_two, shift_two, w_up, bias_up, w_down, bias_down = cut_pieces(feed_flat.reshape(-1), feed_shapes())
    rows_block = math.gcd(TOKENS, 4096)
    block_count = TOKENS // rows_block
    qkv_bias = jnp.concatenate([bias_query, jnp.zeros((D,), jnp.float32), bias_value])

    def project(row_group):
        normed = low(layer_norm(row_group, gain_one, shift_one))
        return product(normed, w_qkv) + qkv_bias
    projected = lax.map(jax.checkpoint(project), inputs.reshape(block_count, rows_block, D)).reshape(TOKENS, 3 * D)
    query_rows = low_back(low(projected[:, :D]))
    key_rows = low_back(low(projected[:, D:2 * D]))
    value_rows = low_back(low(projected[:, 2 * D:]))
    classes = (bias_id[:, None] == jnp.arange(NB, dtype=jnp.int32)[None, :]).astype(jnp.float32)
    key_bias = product(classes, bias_table)
    keys_pad = jnp.pad(key_rows, ((IMG, IMG), (0, 0)))
    values_pad = jnp.pad(value_rows, ((IMG, IMG), (0, 0)))
    bias_pad = jnp.pad(key_bias, ((IMG, IMG), (0, 0)))
    ids_pad = jnp.pad(image_id, (IMG, IMG), constant_values=-1)
    query_block = math.gcd(TOKENS, 512)
    window = query_block + 2 * IMG
    score_scale = HEAD_DIM ** (-0.5)

    def attend(start):
        queries = lax.dynamic_slice_in_dim(query_rows, start, query_block, 0).reshape(query_block, HEADS, HEAD_DIM)
        query_ids = lax.dynamic_slice_in_dim(image_id, start, query_block, 0)
        keys_win = lax.dynamic_slice_in_dim(keys_pad, start, window, 0).reshape(window, HEADS, HEAD_DIM)
        values_win = lax.dynamic_slice_in_dim(values_pad, start, window, 0).reshape(window, HEADS, HEAD_DIM)
        bias_win = lax.dynamic_slice_in_dim(bias_pad, start, window, 0)
        ids_win = lax.dynamic_slice_in_dim(ids_pad, start, window, 0)
        raw_scores = low_back(jnp.einsum('qhd,khd->hqk', queries, keys_win, precision=highest))
        scores = raw_scores * score_scale + bias_win.T[:, None, :]
        same_image = query_ids[:, None] == ids_win[None, :]
        scores = jnp.where(same_image[None], scores, -1e+30)
        row_peak = lax.optimization_barrier(jnp.max(scores, axis=-1, keepdims=True))
        weights = jnp.exp(scores - row_peak)
        probability = low(weights / lax.optimization_barrier(jnp.sum(weights, axis=-1, keepdims=True)))
        mixed_heads = jnp.einsum('hqk,khd->qhd', probability, values_win, precision=highest)
        return mixed_heads.reshape(query_block, D)
    starts = jnp.arange(TOKENS // query_block, dtype=jnp.int32) * query_block
    context = low_back(low(lax.map(jax.checkpoint(attend), starts).reshape(TOKENS, D)))
    middle = inputs + low_back(product(context, w_out) + bias_out)

    def feed_block(row_group):
        normed = low(layer_norm(row_group, gain_two, shift_two))
        hidden = low_back(product(normed, w_up) + bias_up)
        active = low(jax.nn.gelu(hidden, approximate=True))
        return row_group + product(active, w_down) + bias_down
    return lax.map(jax.checkpoint(feed_block), middle.reshape(block_count, rows_block, D)).reshape(TOKENS, D)

def reference(inputs, attn_blocks, mlp_blocks, image_id, bias_id, out_grad):

    def closed(values, attn_flat, feed_flat):
        return forward(values, attn_flat, feed_flat, image_id, bias_id)
    result, pullback = jax.vjp(closed, inputs.astype(jnp.float32), attn_blocks.astype(jnp.float32), mlp_blocks.astype(jnp.float32))
    grad_inputs, grad_attn, grad_mlp = pullback(out_grad.astype(jnp.float32))
    return (result.astype(jnp.bfloat16), grad_inputs, grad_attn, grad_mlp)
```

```python
import math

import jax
import jax.numpy as jnp
from jax import lax
from jax.sharding import PartitionSpec as P

D = 384
FF = 1536
HEADS = 6
HEAD_DIM = 64
IMG = 197
NB = 16


epsilon = 1e-06
highest = lax.Precision.HIGHEST
contract_rows = (((0,), (0,)), ((), ()))
contract_cols = (((1,), (1,)), ((), ()))


def shifted_2(value, axis, by):
    devices = lax.axis_size(axis)
    pairs = [(i, i + by) for i in range(devices) if 0 <= i + by < devices]
    return lax.ppermute(value, axis, pairs)


def attention_shapes():
    return [(D,), (D,), (D, 3 * D), (D,), (D,), (D, D), (D,), (NB, HEADS)]


def feed_shapes():
    return [(D,), (D,), (D, FF), (FF,), (FF, D), (D,)]


LANES = 128
CORES = 2
SQUARE = 4


def groups_of(devices):
    inner = CORES * SQUARE
    chips = [
        [base + CORES * spot + core for spot in range(SQUARE)]
        for base in range(0, devices, inner)
        for core in range(CORES)
    ]
    columns = [[base + inner * spot for spot in range(devices // inner)] for base in range(inner)]
    planes = [list(range(base, base + inner)) for base in range(0, devices, inner)]
    return (chips, columns, planes)


def gather_planes(block, devices):
    chips, columns, planes = groups_of(devices)
    rows = block.shape[1] // LANES
    part = lax.all_gather(block.reshape(rows, LANES), "fsdp", axis_index_groups=columns)
    part = lax.all_gather(part, "fsdp", axis_index_groups=planes)
    return jnp.transpose(part, (1, 0, 2, 3)).reshape(devices * rows, LANES)


def swap_cores(value, devices):
    return lax.ppermute(value, "fsdp", [(i, i ^ 1) for i in range(devices)])


def gather_exchange(block, devices):
    chips, columns, planes = groups_of(devices)
    rows = block.shape[1] // LANES
    depth = devices // (CORES * SQUARE)
    part = jnp.broadcast_to(block.reshape(1, rows, LANES), (depth, rows, LANES))
    part = lax.all_to_all(part, "fsdp", 0, 0, axis_index_groups=columns, tiled=True)
    part = jnp.broadcast_to(part[None], (SQUARE, depth, rows, LANES))
    part = lax.all_to_all(part, "fsdp", 0, 0, axis_index_groups=chips, tiled=True)
    other = swap_cores(part, devices)
    core = lax.axis_index("fsdp") % CORES
    pair = jnp.where(core == 0, jnp.stack([part, other], 1), jnp.stack([other, part], 1))
    return jnp.transpose(pair, (2, 0, 1, 3, 4)).reshape(devices * rows, LANES)


def scatter_exchange(terms, devices):
    chips, columns, planes = groups_of(devices)
    rows = terms.shape[0] // devices
    depth = devices // (CORES * SQUARE)
    core = lax.axis_index("fsdp") % CORES
    terms = terms.astype(jnp.bfloat16).reshape(depth * SQUARE, CORES, rows, LANES)
    other = swap_cores(lax.dynamic_index_in_dim(terms, 1 - core, 1, False), devices)
    mine = lax.dynamic_index_in_dim(terms, core, 1, False)
    part = (mine.astype(jnp.float32) + other.astype(jnp.float32)).astype(jnp.bfloat16)
    part = part.reshape(depth, SQUARE, rows, LANES)
    part = lax.all_to_all(part, "fsdp", 1, 1, axis_index_groups=chips, tiled=True)
    part = jnp.sum(part.astype(jnp.float32), axis=1).astype(jnp.bfloat16)
    part = lax.all_to_all(part, "fsdp", 0, 0, axis_index_groups=columns, tiled=True)
    return jnp.sum(part.astype(jnp.float32), axis=0).reshape(1, rows * LANES)


def scatter_planes(terms, devices):
    chips, columns, planes = groups_of(devices)
    rows = terms.shape[0] // devices
    inner = CORES * SQUARE
    depth = devices // inner
    part = terms.reshape(depth, inner, rows, LANES).transpose(1, 0, 2, 3).astype(jnp.bfloat16)
    part = lax.psum_scatter(part, "fsdp", scatter_dimension=0, axis_index_groups=planes)
    part = lax.psum_scatter(part, "fsdp", scatter_dimension=0, axis_index_groups=columns)
    return part.astype(jnp.float32).reshape(1, rows * LANES)


def cut_pieces(flat, shapes):
    pieces = []
    offset = 0
    for piece_shape in shapes:
        amount = math.prod(piece_shape)
        pieces.append(flat[offset : offset + amount].reshape(piece_shape))
        offset += amount
    return pieces


def flatten_terms(pieces, devices, block_width):
    flat = jnp.concatenate(
        [piece.reshape(-1, LANES) for piece in pieces if piece.size % LANES == 0]
        + [
            jnp.pad(piece.reshape(-1), (0, -piece.size % LANES)).reshape(-1, LANES)
            for piece in pieces
            if piece.size % LANES
        ]
    )
    rows = devices * block_width // LANES
    return jnp.pad(flat, ((0, rows - flat.shape[0]), (0, 0)))


def layer_norm(values, norm_gain, norm_shift):
    average = jnp.mean(values, axis=-1, keepdims=True)
    centred = values - average
    variance = jnp.mean(centred * centred, axis=-1, keepdims=True)
    return centred * lax.rsqrt(variance + epsilon) * norm_gain + norm_shift


def tanh_gelu(values):
    return jax.nn.gelu(values, approximate=True)


def row_sums(left, right):
    return lax.dot_general(left, right, contract_rows, preferred_element_type=jnp.float32)


def back_product(left, right):
    return lax.dot_general(left, right, contract_cols, preferred_element_type=jnp.float32)


def shards(inputs, attn_blocks, mlp_blocks, image_id, bias_id, out_grad):
    token_rows = inputs.shape[0]
    devices = lax.axis_size("fsdp")
    reach_shards = (IMG - 2) // token_rows + 1
    total_shards = 2 * reach_shards + 1
    span_keys = token_rows + 2 * IMG - 2
    first_key = reach_shards * token_rows - (IMG - 1)
    score_scale = HEAD_DIM ** (-0.5)
    attn_flat = gather_planes(attn_blocks, devices)
    gain_one, shift_one, w_qkv, bias_query, bias_value, w_out, bias_out, bias_table = cut_pieces(
        attn_flat.reshape(-1), attention_shapes()
    )
    inputs_wide = inputs.astype(jnp.float32)
    normed_one, norm_one_back = jax.vjp(
        layer_norm, inputs_wide, gain_one.astype(jnp.float32), shift_one.astype(jnp.float32)
    )
    normed_one = normed_one.astype(jnp.bfloat16)
    projected = jnp.dot(normed_one, w_qkv, preferred_element_type=jnp.float32)
    query_rows = (projected[:, :D] + bias_query.astype(jnp.float32)).astype(jnp.bfloat16)
    key_values = jnp.concatenate(
        [projected[:, D : 2 * D], projected[:, 2 * D :] + bias_value.astype(jnp.float32)], axis=1
    ).astype(jnp.bfloat16)
    image_tag = image_id % 128 + 1
    key_tags = jnp.stack([image_tag, bias_id]).astype(jnp.bfloat16)
    lower_kv, lower_tags, upper_kv, upper_tags = ([], [], [], [])
    distance = 1
    moved_kv, moved_tags = shifted_2((key_values, key_tags), "fsdp", distance)
    lower_kv.append(moved_kv)
    lower_tags.append(moved_tags)
    moved_kv, moved_tags = shifted_2((key_values, key_tags), "fsdp", -distance)
    upper_kv.append(moved_kv)
    upper_tags.append(moved_tags)
    window_kv = jnp.stack(lower_kv[::-1] + [key_values] + upper_kv)
    window_tags = jnp.stack(lower_tags[::-1] + [key_tags] + upper_tags)
    flat_kv = window_kv.reshape(-1, 2 * D)[first_key : first_key + span_keys]
    flat_tags = (
        jnp.transpose(window_tags, (1, 0, 2))
        .reshape(2, -1)[:, first_key : first_key + span_keys]
        .astype(jnp.float32)
    )
    keys_win = flat_kv[:, :D].reshape(span_keys, HEADS, HEAD_DIM)
    values_win = flat_kv[:, D:].reshape(span_keys, HEADS, HEAD_DIM)
    same_image = image_tag.astype(jnp.float32)[:, None] == flat_tags[0][None, :]
    key_class = (flat_tags[1][:, None] == jnp.arange(NB, dtype=jnp.float32)[None, :]).astype(
        jnp.float32
    )
    key_bias = jnp.dot(key_class, bias_table.astype(jnp.float32), precision=highest)
    queries = query_rows.reshape(token_rows, HEADS, HEAD_DIM)

    def scores_of():
        raw_scores = jnp.einsum(
            "qhd,khd->hqk", queries, keys_win, preferred_element_type=jnp.float32
        )
        shifted = raw_scores * score_scale + key_bias.T[:, None, :]
        return jnp.where(same_image[None], shifted, -1e30)

    scores = scores_of()
    row_peak = jnp.max(scores, axis=-1, keepdims=True)
    weights = jnp.exp(scores - row_peak)
    totals = jnp.sum(weights, axis=-1, keepdims=True)
    log_total = row_peak + jnp.log(totals)
    probability = (weights / totals).astype(jnp.bfloat16)
    context = jnp.einsum(
        "hqk,khd->qhd", probability, values_win, preferred_element_type=jnp.float32
    )
    context = context.reshape(token_rows, D).astype(jnp.bfloat16)
    middle = (
        inputs_wide
        + jnp.dot(context, w_out, preferred_element_type=jnp.float32)
        + bias_out.astype(jnp.float32)
    )
    feed_flat = gather_exchange(mlp_blocks, devices)
    gain_two, shift_two, w_up, bias_up, w_down, bias_down = cut_pieces(
        feed_flat.reshape(-1), feed_shapes()
    )
    normed_two, norm_two_back = jax.vjp(
        layer_norm, middle, gain_two.astype(jnp.float32), shift_two.astype(jnp.float32)
    )
    normed_two = normed_two.astype(jnp.bfloat16)
    hidden = jnp.dot(normed_two, w_up, preferred_element_type=jnp.float32) + bias_up.astype(
        jnp.float32
    )
    active, gelu_back = jax.vjp(tanh_gelu, hidden)
    active = active.astype(jnp.bfloat16)
    output = (
        middle
        + jnp.dot(active, w_down, preferred_element_type=jnp.float32)
        + bias_down.astype(jnp.float32)
    ).astype(jnp.bfloat16)
    attn_again = attn_flat
    feed_again = feed_flat
    w_qkv_back, w_out_back = cut_pieces(attn_again.reshape(-1), attention_shapes())[2::3]
    w_up_back, w_down_back = cut_pieces(feed_again.reshape(-1), feed_shapes())[2::2]
    grad_output = out_grad.astype(jnp.float32)
    grad_w_down = row_sums(active, out_grad)
    grad_bias_down = jnp.sum(grad_output, axis=0)
    grad_active = back_product(out_grad, w_down_back)
    grad_hidden = gelu_back(grad_active)[0].astype(jnp.bfloat16)
    grad_bias_up = jnp.sum(grad_hidden.astype(jnp.float32), axis=0)
    grad_w_up = row_sums(normed_two, grad_hidden)
    grad_normed_two = back_product(grad_hidden, w_up_back)
    grad_middle, grad_gain_two, grad_shift_two = norm_two_back(grad_normed_two)
    grad_middle = grad_output + grad_middle
    feed_terms = flatten_terms(
        [grad_gain_two, grad_shift_two, grad_w_up, grad_bias_up, grad_w_down, grad_bias_down],
        devices,
        mlp_blocks.shape[1],
    )
    grad_mlp = scatter_exchange(feed_terms, devices)
    grad_branch = grad_middle.astype(jnp.bfloat16)
    grad_bias_out = jnp.sum(grad_branch.astype(jnp.float32), axis=0)
    grad_w_out = row_sums(context, grad_branch)
    grad_context = (
        back_product(grad_branch, w_out_back)
        .astype(jnp.bfloat16)
        .reshape(token_rows, HEADS, HEAD_DIM)
    )
    probs_again = jnp.exp(scores_of() - log_total)
    grad_probs = jnp.einsum(
        "qhd,khd->hqk", grad_context, values_win, preferred_element_type=jnp.float32
    )
    grad_scores = probs_again * (
        grad_probs - jnp.sum(probs_again * grad_probs, axis=-1, keepdims=True)
    )
    grad_key_bias = jnp.sum(grad_scores, axis=1)
    grad_table = lax.dot_general(
        key_class,
        grad_key_bias,
        (((0,), (1,)), ((), ())),
        precision=highest,
        preferred_element_type=jnp.float32,
    )
    grad_raw = (grad_scores * score_scale).astype(jnp.bfloat16)
    grad_query = (
        jnp.einsum("hqk,khd->qhd", grad_raw, keys_win, preferred_element_type=jnp.float32)
        .reshape(token_rows, D)
        .astype(jnp.bfloat16)
    )
    grad_keys = jnp.einsum(
        "hqk,qhd->khd", grad_raw, queries, preferred_element_type=jnp.float32
    ).reshape(span_keys, D)
    grad_values = jnp.einsum(
        "hqk,qhd->khd", probability, grad_context, preferred_element_type=jnp.float32
    ).reshape(span_keys, D)
    grad_window = jnp.concatenate([grad_keys, grad_values], axis=1)
    grad_window = jnp.pad(
        grad_window, ((first_key, total_shards * token_rows - first_key - span_keys), (0, 0))
    )
    grad_window = grad_window.reshape(total_shards, token_rows, 2 * D)
    gathered_grad = grad_window[reach_shards]
    distance = 1
    gathered_grad = gathered_grad + shifted_2(
        grad_window[reach_shards - distance].astype(jnp.bfloat16), "fsdp", -distance
    ).astype(jnp.float32)
    gathered_grad = gathered_grad + shifted_2(
        grad_window[reach_shards + distance], "fsdp", distance
    )
    grad_kv = gathered_grad.astype(jnp.bfloat16)
    grad_qkv = jnp.concatenate([grad_query, grad_kv], axis=1)
    grad_bias_query = jnp.sum(grad_query.astype(jnp.float32), axis=0)
    grad_bias_value = jnp.sum(grad_kv[:, D:].astype(jnp.float32), axis=0)
    grad_w_qkv = row_sums(normed_one, grad_qkv)
    grad_normed_one = back_product(grad_qkv, w_qkv_back)
    grad_from_norm, grad_gain_one, grad_shift_one = norm_one_back(grad_normed_one)
    grad_inputs = grad_middle + grad_from_norm
    attn_terms = flatten_terms(
        [
            grad_gain_one,
            grad_shift_one,
            grad_w_qkv,
            grad_bias_query,
            grad_bias_value,
            grad_w_out,
            grad_bias_out,
            grad_table,
        ],
        devices,
        attn_blocks.shape[1],
    )
    grad_attn = scatter_planes(attn_terms, devices)
    return (output, grad_inputs, grad_attn, grad_mlp)


def solution(mesh):
    return jax.shard_map(
        shards,
        mesh=mesh,
        in_specs=(
            P("fsdp", None),
            P("fsdp", None),
            P("fsdp", None),
            P("fsdp"),
            P("fsdp"),
            P("fsdp", None),
        ),
        out_specs=(P("fsdp", None), P("fsdp", None), P("fsdp", None), P("fsdp", None)),
        check_vma=False,
    )
```

```python
import functools
import math

import jax
import jax.numpy as jnp
from jax import lax
from jax.experimental import pallas as pl
from jax.experimental.pallas import tpu as pltpu
from jax.sharding import PartitionSpec as P

D = 384
FF = 1536
HEADS = 6
HEAD_DIM = 64
IMG = 197
NB = 16

LANES = 128
CORES = 2
SQUARE = 4
SLOT = 208
SPAN = 2 * SLOT
HALO = 112
WIDE = 2 * D + LANES
D_ROWS = D // LANES
FF_ROWS = FF // LANES
QKV_ROWS = 3 * D // LANES

GAIN_AT = 0
SHIFT_AT = D_ROWS
W_QKV_AT = 2 * D_ROWS
BIAS_QUERY_AT = W_QKV_AT + D * QKV_ROWS
BIAS_VALUE_AT = BIAS_QUERY_AT + D_ROWS
W_OUT_AT = BIAS_VALUE_AT + D_ROWS
BIAS_OUT_AT = W_OUT_AT + D * D_ROWS
TABLE_AT = BIAS_OUT_AT + D_ROWS
W_UP_AT = 2 * D_ROWS
BIAS_UP_AT = W_UP_AT + D * FF_ROWS
W_DOWN_AT = BIAS_UP_AT + FF_ROWS
BIAS_DOWN_AT = W_DOWN_AT + FF * D_ROWS
FEED_END = BIAS_DOWN_AT + D_ROWS

epsilon = 1e-06
score_scale = HEAD_DIM ** (-0.5)
masked_score = -1e30
f32 = jnp.float32
bf16 = jnp.bfloat16


def dot(left, right):
    return lax.dot_general(left, right, (((1,), (0,)), ((), ())), preferred_element_type=f32)


def dot_rows(left, right):
    return lax.dot_general(left, right, (((0,), (0,)), ((), ())), preferred_element_type=f32)


def dot_cols(left, right):
    return lax.dot_general(left, right, (((1,), (1,)), ((), ())), preferred_element_type=f32)


def groups_of(devices):
    inner = CORES * SQUARE
    chips = [
        [base + CORES * spot + core for spot in range(SQUARE)]
        for base in range(0, devices, inner)
        for core in range(CORES)
    ]
    columns = [[base + inner * spot for spot in range(devices // inner)] for base in range(inner)]
    return (chips, columns)


def swap_cores(value, devices):
    return lax.ppermute(value, "fsdp", [(i, i ^ 1) for i in range(devices)])


def gather_blocks(block, devices):
    chips, columns = groups_of(devices)
    rows = block.shape[1] // LANES
    depth = devices // (CORES * SQUARE)
    part = jnp.broadcast_to(block.reshape(1, rows, LANES), (depth, rows, LANES))
    part = lax.all_to_all(part, "fsdp", 0, 0, axis_index_groups=columns, tiled=True)
    part = jnp.broadcast_to(part[None], (SQUARE, depth, rows, LANES))
    part = lax.all_to_all(part, "fsdp", 0, 0, axis_index_groups=chips, tiled=True)
    return (part, swap_cores(part, devices))


def add_cores(keep, send, devices):
    other = swap_cores(send, devices)
    return (keep.astype(f32) + other.astype(f32)).astype(bf16)


def add_chips(part, devices):
    chips, columns = groups_of(devices)
    part = lax.all_to_all(part, "fsdp", 1, 1, axis_index_groups=chips, tiled=True)
    return jnp.sum(part.astype(f32), axis=1).astype(bf16)


def add_columns(part, devices):
    chips, columns = groups_of(devices)
    part = lax.all_to_all(part, "fsdp", 0, 0, axis_index_groups=columns, tiled=True)
    return jnp.sum(part.astype(f32), axis=0).reshape(1, -1)


def lay_out_blocks(core, mine_ref, other_ref, flat_ref):
    spots, depth, rows, lanes = mine_ref.shape
    for layer in range(depth):
        for spot in range(spots):
            base = (layer * spots + spot) * CORES * rows
            mine = mine_ref[spot, layer].astype(f32)
            other = other_ref[spot, layer].astype(f32)
            flat_ref[base : base + rows] = jnp.where(core == 0, mine, other)
            flat_ref[base + rows : base + 2 * rows] = jnp.where(core == 0, other, mine)


def cut_blocks(core, flat_ref, keep_ref, send_ref):
    depth, spots, rows, lanes = keep_ref.shape
    for layer in range(depth):
        for spot in range(spots):
            base = (layer * spots + spot) * CORES * rows
            first = flat_ref[base : base + rows]
            second = flat_ref[base + rows : base + 2 * rows]
            keep_ref[layer, spot] = jnp.where(core == 0, first, second).astype(bf16)
            send_ref[layer, spot] = jnp.where(core == 0, second, first).astype(bf16)


def read_vector(flat_ref, at, amount):
    return jnp.concatenate([flat_ref[at + i : at + i + 1] for i in range(amount)], axis=1)


def write_vector(flat_ref, at, amount, value):
    for i in range(amount):
        flat_ref[at + i : at + i + 1] = value[:, i * LANES : (i + 1) * LANES]


def read_matrix(flat_ref, at, height, amount, out_ref):
    for i in range(amount):
        chunk = flat_ref[pl.ds(at + i, height, stride=amount), :]
        out_ref[:, i * LANES : (i + 1) * LANES] = chunk.astype(bf16)


def normalise(values):
    average = jnp.mean(values, axis=-1, keepdims=True)
    centred = values - average
    variance = jnp.mean(centred * centred, axis=-1, keepdims=True)
    inverse = lax.rsqrt(variance + epsilon)
    return (centred * inverse, inverse)


def norm_back(grad, unit, inverse, gain):
    scaled = grad * gain
    first = jnp.mean(scaled, axis=-1, keepdims=True)
    second = jnp.mean(scaled * unit, axis=-1, keepdims=True)
    return inverse * (scaled - first - unit * second)


def slot_mask(meta_ref, window, by_column):
    shape = (window, SPAN) if by_column else (SPAN, window)
    spot = lax.broadcasted_iota(jnp.int32, shape, 0 if by_column else 1)
    row = lax.broadcasted_iota(jnp.int32, shape, 1 if by_column else 0)
    start = jnp.where(row < SLOT, meta_ref[0], meta_ref[2] - SLOT)
    limit = jnp.where(row < SLOT, meta_ref[1], meta_ref[3] + SLOT)
    return jnp.where((spot == row + start) & (row < limit), 1.0, 0.0).astype(bf16)


def head_lanes(half):
    lane = lax.broadcasted_iota(jnp.int32, (1, LANES), 1)
    return (lane < HEAD_DIM) if half == 0 else (lane >= HEAD_DIM)


def attend_kernel(
    meta_ref, before_ref, own_ref, after_ref, mask_ref, mine_ref, other_ref,
    middle_ref, cotangent_ref, inputs_ref, normed_ref, qkv_ref, probability_ref,
    context_ref, classes_ref, w_qkv_ref, w_out_ref, gain_ref,
    flat_ref, window_ref,
):
    core = meta_ref[4]
    window = window_ref.shape[0]
    lay_out_blocks(core, mine_ref, other_ref, flat_ref)
    read_matrix(flat_ref, W_QKV_AT, D, QKV_ROWS, w_qkv_ref)
    read_matrix(flat_ref, W_OUT_AT, D, D_ROWS, w_out_ref)
    gain = read_vector(flat_ref, GAIN_AT, D_ROWS)
    shift = read_vector(flat_ref, SHIFT_AT, D_ROWS)
    gain_ref[...] = gain
    bias_query = read_vector(flat_ref, BIAS_QUERY_AT, D_ROWS)
    bias_value = read_vector(flat_ref, BIAS_VALUE_AT, D_ROWS)
    bias_out = read_vector(flat_ref, BIAS_OUT_AT, D_ROWS)
    table = (mask_ref[...] * flat_ref[TABLE_AT : TABLE_AT + 1]).astype(bf16)

    halo = before_ref.shape[0]
    own = own_ref.shape[0]
    window_ref[0:halo] = before_ref[...]
    window_ref[halo : halo + own] = own_ref[...]
    window_ref[halo + own : window] = after_ref[...]
    picked = dot(slot_mask(meta_ref, window, False), window_ref[...])
    inputs = picked[:, :D]
    inputs_ref[...] = inputs.astype(bf16)
    cotangent_ref[...] = picked[:, D : 2 * D].astype(bf16)
    classes_ref[...] = picked[:, 2 * D :].astype(bf16)

    unit, _ = normalise(inputs)
    normed_ref[...] = (unit * gain + shift).astype(bf16)
    normed = normed_ref[...]
    qkv_ref[:, :D] = (dot(normed, w_qkv_ref[:, :D]) + bias_query).astype(bf16)
    qkv_ref[:, D : 2 * D] = dot(normed, w_qkv_ref[:, D : 2 * D]).astype(bf16)
    qkv_ref[:, 2 * D :] = (dot(normed, w_qkv_ref[:, 2 * D :]) + bias_value).astype(bf16)

    for slot in range(2):
        rows = slice(slot * SLOT, (slot + 1) * SLOT)
        key = lax.broadcasted_iota(jnp.int32, (1, SLOT), 1)
        key_bias = dot_cols(table, classes_ref[rows])
        key_bias = jnp.where(key < meta_ref[2 * slot + 1], key_bias, masked_score)
        for pair in range(HEADS // 2):
            lanes = slice(pair * LANES, (pair + 1) * LANES)
            queries = qkv_ref[rows, lanes]
            keys = qkv_ref[rows, D + pair * LANES : D + (pair + 1) * LANES]
            values = qkv_ref[rows, 2 * D + pair * LANES : 2 * D + (pair + 1) * LANES]
            mixed = []
            for half in range(2):
                head = 2 * pair + half
                chosen = jnp.where(head_lanes(half), queries, jnp.zeros_like(queries))
                scores = dot_cols(chosen, keys) * score_scale + key_bias[head : head + 1]
                peak = jnp.max(scores, axis=-1, keepdims=True)
                weights = jnp.exp(scores - peak)
                total = jnp.sum(weights, axis=-1, keepdims=True)
                probability = (weights * (1.0 / total)).astype(bf16)
                probability_ref[slot * HEADS + head] = probability
                mixed.append(dot(probability, values))
            context_ref[rows, lanes] = jnp.where(head_lanes(0), mixed[0], mixed[1]).astype(bf16)
    middle_ref[...] = inputs + dot(context_ref[...], w_out_ref[...]) + bias_out


def feed_kernel(
    meta_ref, middle_ref, cotangent_ref, mine_ref, other_ref,
    output_ref, grad_middle_ref, keep_ref, send_ref,
    flat_ref, w_up_ref, w_down_ref, normed_ref,
):
    core = meta_ref[4]
    window = output_ref.shape[0]
    lay_out_blocks(core, mine_ref, other_ref, flat_ref)
    read_matrix(flat_ref, W_UP_AT, D, FF_ROWS, w_up_ref)
    read_matrix(flat_ref, W_DOWN_AT, FF, D_ROWS, w_down_ref)
    gain = read_vector(flat_ref, GAIN_AT, D_ROWS)
    shift = read_vector(flat_ref, SHIFT_AT, D_ROWS)
    bias_up = read_vector(flat_ref, BIAS_UP_AT, FF_ROWS)
    bias_down = read_vector(flat_ref, BIAS_DOWN_AT, D_ROWS)

    middle = middle_ref[...]
    cotangent = cotangent_ref[...]
    unit, inverse = normalise(middle)
    normed_ref[...] = (unit * gain + shift).astype(bf16)
    normed = normed_ref[...]
    output = middle + bias_down
    grad = jnp.zeros((SPAN, D), f32)
    slope = math.sqrt(2.0 / math.pi)
    for step in range(FF // D):
        cols = slice(step * D, (step + 1) * D)
        w_up = w_up_ref[:, cols]
        w_down = w_down_ref[cols]
        hidden = dot(normed, w_up) + bias_up[:, cols]
        square = hidden * hidden
        bend = jnp.tanh(slope * hidden * (1.0 + 0.044715 * square))
        half = 0.5 * (1.0 + bend)
        active = (hidden * half).astype(bf16)
        steep = half + 0.5 * hidden * (1.0 - bend * bend) * (
            slope * (1.0 + (3 * 0.044715) * square)
        )
        grad_hidden_wide = dot_cols(cotangent, w_down) * steep
        grad_hidden = grad_hidden_wide.astype(bf16)
        output = output + dot(active, w_down)
        grad = grad + dot_cols(grad_hidden, w_up)
        grad_down = dot_rows(active, cotangent)
        grad_up = dot_rows(normed, grad_hidden)
        grad_bias = jnp.sum(grad_hidden.astype(f32), axis=0, keepdims=True)
        write_vector(flat_ref, BIAS_UP_AT + step * D_ROWS, D_ROWS, grad_bias)
        for i in range(D_ROWS):
            lanes = slice(i * LANES, (i + 1) * LANES)
            flat_ref[pl.ds(W_UP_AT + step * D_ROWS + i, D, stride=FF_ROWS), :] = grad_up[:, lanes]
            flat_ref[pl.ds(W_DOWN_AT + step * D * D_ROWS + i, D, stride=D_ROWS), :] = grad_down[
                :, lanes
            ]
    output_ref[...] = dot(slot_mask(meta_ref, window, True), output.astype(bf16)).astype(bf16)
    grad_output = cotangent.astype(f32)
    write_vector(flat_ref, GAIN_AT, D_ROWS, jnp.sum(grad * unit, axis=0, keepdims=True))
    write_vector(flat_ref, SHIFT_AT, D_ROWS, jnp.sum(grad, axis=0, keepdims=True))
    write_vector(flat_ref, BIAS_DOWN_AT, D_ROWS, jnp.sum(grad_output, axis=0, keepdims=True))
    flat_ref[FEED_END:] = jnp.zeros((flat_ref.shape[0] - FEED_END, LANES), f32)
    grad_middle_ref[...] = grad_output + norm_back(grad, unit, inverse, gain)
    cut_blocks(core, flat_ref, keep_ref, send_ref)


def attend_back_kernel(
    meta_ref, grad_middle_ref, mask_ref, inputs_ref, normed_ref, qkv_ref, probability_ref,
    context_ref, classes_ref, w_qkv_ref, w_out_ref, gain_ref,
    grad_inputs_ref, keep_ref, send_ref,
    flat_ref, grad_qkv_ref, grad_context_ref,
):
    core = meta_ref[4]
    window = grad_inputs_ref.shape[0]
    grad_middle = grad_middle_ref[...]
    grad_branch = grad_middle.astype(bf16)
    grad_bias_out = jnp.sum(grad_branch.astype(f32), axis=0, keepdims=True)
    write_vector(flat_ref, BIAS_OUT_AT, D_ROWS, grad_bias_out)
    grad_w_out = dot_rows(context_ref[...], grad_branch)
    for i in range(D_ROWS):
        flat_ref[pl.ds(W_OUT_AT + i, D, stride=D_ROWS), :] = grad_w_out[
            :, i * LANES : (i + 1) * LANES
        ]
    grad_context_ref[...] = dot_cols(grad_branch, w_out_ref[...]).astype(bf16)
    grad_table = jnp.zeros((8, LANES), f32)
    for slot in range(2):
        rows = slice(slot * SLOT, (slot + 1) * SLOT)
        key_sums = []
        for pair in range(HEADS // 2):
            lanes = slice(pair * LANES, (pair + 1) * LANES)
            key_lanes = slice(D + pair * LANES, D + (pair + 1) * LANES)
            value_lanes = slice(2 * D + pair * LANES, 2 * D + (pair + 1) * LANES)
            queries = qkv_ref[rows, lanes]
            keys = qkv_ref[rows, key_lanes]
            values = qkv_ref[rows, value_lanes]
            grad_context = grad_context_ref[rows, lanes]
            parts = []
            for half in range(2):
                head = 2 * pair + half
                chosen = jnp.where(head_lanes(half), grad_context, jnp.zeros_like(grad_context))
                grad_probs = dot_cols(chosen, values)
                narrow = probability_ref[slot * HEADS + head]
                probability = narrow.astype(f32)
                weighted = probability * grad_probs
                grad_scores = weighted - probability * jnp.sum(weighted, axis=-1, keepdims=True)
                key_sums.append(jnp.sum(grad_scores, axis=0, keepdims=True))
                grad_raw = (grad_scores * score_scale).astype(bf16)
                parts.append(
                    (dot(grad_raw, keys), dot_rows(grad_raw, queries), dot_rows(narrow, grad_context))
                )
            low = head_lanes(0)
            for where, first, second in zip((lanes, key_lanes, value_lanes), *parts):
                grad_qkv_ref[rows, where] = jnp.where(low, first, second).astype(bf16)
        sums = jnp.concatenate(key_sums + [jnp.zeros((8 - HEADS, SLOT), f32)], axis=0)
        sums_high = sums.astype(bf16)
        sums_low = (sums - sums_high.astype(f32)).astype(bf16)
        classes = classes_ref[rows]
        grad_table = grad_table + dot(sums_high, classes) + dot(sums_low, classes)
    flat_ref[TABLE_AT:] = jnp.zeros((flat_ref.shape[0] - TABLE_AT, LANES), f32)
    flat_ref[TABLE_AT : TABLE_AT + 1] = jnp.sum(grad_table * mask_ref[...], axis=0, keepdims=True)

    grad_qkv = grad_qkv_ref[...]
    column_sums = jnp.sum(grad_qkv.astype(f32), axis=0, keepdims=True)
    write_vector(flat_ref, BIAS_QUERY_AT, D_ROWS, column_sums[:, :D])
    write_vector(flat_ref, BIAS_VALUE_AT, D_ROWS, column_sums[:, 2 * D :])
    normed = normed_ref[...]
    for part in range(3):
        grad_w = dot_rows(normed, grad_qkv_ref[:, part * D : (part + 1) * D])
        for i in range(D_ROWS):
            flat_ref[pl.ds(W_QKV_AT + part * D_ROWS + i, D, stride=QKV_ROWS), :] = grad_w[
                :, i * LANES : (i + 1) * LANES
            ]
    grad_normed = dot_cols(grad_qkv, w_qkv_ref[...])
    gain = gain_ref[...]
    unit, inverse = normalise(inputs_ref[...].astype(f32))
    write_vector(flat_ref, GAIN_AT, D_ROWS, jnp.sum(grad_normed * unit, axis=0, keepdims=True))
    write_vector(flat_ref, SHIFT_AT, D_ROWS, jnp.sum(grad_normed, axis=0, keepdims=True))
    grad_inputs = grad_middle + norm_back(grad_normed, unit, inverse, gain)
    high = grad_inputs.astype(bf16)
    low_part = (grad_inputs - high.astype(f32)).astype(bf16)
    back = slot_mask(meta_ref, window, True)
    grad_inputs_ref[...] = dot(back, high) + dot(back, low_part)
    cut_blocks(core, flat_ref, keep_ref, send_ref)


def call_kernel(kernel, out_shapes, scratch, flops, operands):
    vmem = pl.BlockSpec(memory_space=pltpu.VMEM)
    specs = [pl.BlockSpec(memory_space=pltpu.SMEM)] + [vmem] * (len(operands) - 1)
    moved = sum(math.prod(o.shape) * o.dtype.itemsize for o in list(operands) + list(out_shapes))
    return pl.pallas_call(
        kernel,
        out_shape=out_shapes,
        in_specs=specs,
        out_specs=[vmem] * len(out_shapes),
        scratch_shapes=scratch,
        compiler_params=pltpu.CompilerParams(vmem_limit_bytes=50 * 1024 * 1024),
        cost_estimate=pl.CostEstimate(flops=flops, bytes_accessed=moved, transcendentals=0),
    )(*operands)


def plan_slots(image_id, devices):
    token_rows = image_id.shape[0]
    device = lax.axis_index("fsdp")
    ends = jnp.sum((image_id == image_id[0]).astype(jnp.int32))
    first, last = device == 0, device == devices - 1
    holds = first | (ends >= IMG // 2 + 1)
    start = jnp.where(first, 0, jnp.where(holds, ends - IMG, ends))
    stop = jnp.where(last, token_rows, token_rows + IMG)
    stop_one = jnp.where(holds, ends, jnp.minimum(ends + IMG, stop))
    next_centre = stop_one + IMG // 2
    has_next = (stop_one < stop) & (last | (next_centre < token_rows))
    stop_two = jnp.where(has_next, jnp.minimum(stop_one + IMG, stop), stop_one)
    zero = jnp.zeros((), jnp.int32)
    return jnp.stack(
        [start + HALO, stop_one - start, stop_one + HALO, stop_two - stop_one, device % CORES]
        + [zero] * 3
    ).astype(jnp.int32)


def struct(shape, kind):
    return jax.ShapeDtypeStruct(shape, kind)


def shards(inputs, attn_blocks, mlp_blocks, image_id, bias_id, out_grad):
    token_rows = inputs.shape[0]
    devices = lax.axis_size("fsdp")
    depth = devices // (CORES * SQUARE)
    window = token_rows + 2 * HALO
    attn_rows = attn_blocks.shape[1] // LANES
    mlp_rows = mlp_blocks.shape[1] // LANES
    attn_mine, attn_other = gather_blocks(attn_blocks, devices)

    lane = jnp.arange(LANES, dtype=jnp.int32)
    classes = ((lane // HEADS)[None, :] == bias_id[:, None]) & (lane < NB * HEADS)[None, :]
    tokens = jnp.concatenate([inputs, out_grad, classes.astype(bf16)], axis=1)
    up = [(i, i + 1) for i in range(devices - 1)]
    down = [(i + 1, i) for i in range(devices - 1)]
    before = lax.ppermute(tokens[token_rows - HALO :], "fsdp", up)
    after = lax.ppermute(tokens[:HALO], "fsdp", down)
    meta = plan_slots(image_id, devices)
    head = jnp.arange(8, dtype=jnp.int32)
    head_mask = ((lane % HEADS)[None, :] == head[:, None]) & (lane < NB * HEADS)[None, :]
    head_mask = head_mask.astype(f32)
    mlp_mine, mlp_other = gather_blocks(mlp_blocks, devices)

    (
        middle, cotangent, inputs_span, normed, qkv, probability, context, classes_span,
        w_qkv, w_out, gain,
    ) = call_kernel(
        attend_kernel,
        [
            struct((SPAN, D), f32),
            struct((SPAN, D), bf16),
            struct((SPAN, D), bf16),
            struct((SPAN, D), bf16),
            struct((SPAN, 3 * D), bf16),
            struct((2 * HEADS, SLOT, SLOT), bf16),
            struct((SPAN, D), bf16),
            struct((SPAN, LANES), bf16),
            struct((D, 3 * D), bf16),
            struct((D, D), bf16),
            struct((1, D), f32),
        ],
        [pltpu.VMEM((devices * attn_rows, LANES), f32), pltpu.VMEM((window, WIDE), bf16)],
        2 * 10**9,
        [meta, before, tokens, after, head_mask, attn_mine, attn_other],
    )
    output, grad_middle, feed_keep, feed_send = call_kernel(
        feed_kernel,
        [
            struct((window, D), bf16),
            struct((SPAN, D), f32),
            struct((depth, SQUARE, mlp_rows, LANES), bf16),
            struct((depth, SQUARE, mlp_rows, LANES), bf16),
        ],
        [
            pltpu.VMEM((devices * mlp_rows, LANES), f32),
            pltpu.VMEM((D, FF), bf16),
            pltpu.VMEM((FF, D), bf16),
            pltpu.VMEM((SPAN, D), bf16),
        ],
        4 * 10**9,
        [meta, middle, cotangent, mlp_mine, mlp_other],
    )
    feed_part = add_chips(add_cores(feed_keep, feed_send, devices), devices)
    grad_mlp = add_columns(feed_part, devices)
    grad_inputs, attn_keep, attn_send = call_kernel(
        attend_back_kernel,
        [
            struct((window, D), f32),
            struct((depth, SQUARE, attn_rows, LANES), bf16),
            struct((depth, SQUARE, attn_rows, LANES), bf16),
        ],
        [
            pltpu.VMEM((devices * attn_rows, LANES), f32),
            pltpu.VMEM((SPAN, 3 * D), bf16),
            pltpu.VMEM((SPAN, D), bf16),
        ],
        3 * 10**9,
        [
            meta, grad_middle, head_mask, inputs_span, normed, qkv, probability, context,
            classes_span, w_qkv, w_out, gain,
        ],
    )
    attn_part = add_chips(add_cores(attn_keep, attn_send, devices), devices)
    grad_attn = add_columns(attn_part, devices)
    edges = jnp.concatenate([output, grad_inputs.astype(bf16)], axis=1)
    from_next = lax.ppermute(edges[:HALO], "fsdp", down)
    from_last = lax.ppermute(edges[window - HALO :], "fsdp", up)
    gap = jnp.zeros((token_rows - HALO, 2 * D), bf16)
    extra = jnp.concatenate([from_last, gap]) + jnp.concatenate([gap, from_next])
    own = slice(HALO, HALO + token_rows)
    output = output[own] + extra[:, :D]
    grad_inputs = grad_inputs[own] + extra[:, D:].astype(f32)
    return (output, grad_inputs, grad_attn, grad_mlp)


def solution(mesh):
    return jax.shard_map(
        shards,
        mesh=mesh,
        in_specs=(
            P("fsdp", None),
            P("fsdp", None),
            P("fsdp", None),
            P("fsdp"),
            P("fsdp"),
            P("fsdp", None),
        ),
        out_specs=(P("fsdp", None), P("fsdp", None), P("fsdp", None), P("fsdp", None)),
        check_vma=False,
    )
```

```python
import functools
import math

import jax
import jax.numpy as jnp
from jax import lax
from jax.experimental import pallas as pl
from jax.experimental.pallas import tpu as pltpu
from jax.sharding import PartitionSpec as P

D = 384
FF = 1536
HEADS = 6
HEAD_DIM = 64
IMG = 197
NB = 16

LANES = 128
CORES = 2
SQUARE = 4
SLOT = 208
SPAN = 2 * SLOT
HALO = 112
WIDE = 2 * D + LANES
D_ROWS = D // LANES
FF_ROWS = FF // LANES
QKV_ROWS = 3 * D // LANES

GAIN_AT = 0
SHIFT_AT = D_ROWS
W_QKV_AT = 2 * D_ROWS
BIAS_QUERY_AT = W_QKV_AT + D * QKV_ROWS
BIAS_VALUE_AT = BIAS_QUERY_AT + D_ROWS
W_OUT_AT = BIAS_VALUE_AT + D_ROWS
BIAS_OUT_AT = W_OUT_AT + D * D_ROWS
TABLE_AT = BIAS_OUT_AT + D_ROWS
W_UP_AT = 2 * D_ROWS
BIAS_UP_AT = W_UP_AT + D * FF_ROWS
W_DOWN_AT = BIAS_UP_AT + FF_ROWS
BIAS_DOWN_AT = W_DOWN_AT + FF * D_ROWS
FEED_END = BIAS_DOWN_AT + D_ROWS

epsilon = 1e-06
score_scale = HEAD_DIM ** (-0.5)
masked_score = -1e30
f32 = jnp.float32
bf16 = jnp.bfloat16


def dot(left, right):
    return lax.dot_general(left, right, (((1,), (0,)), ((), ())), preferred_element_type=f32)


def dot_rows(left, right):
    return lax.dot_general(left, right, (((0,), (0,)), ((), ())), preferred_element_type=f32)


def dot_cols(left, right):
    return lax.dot_general(left, right, (((1,), (1,)), ((), ())), preferred_element_type=f32)


def groups_of(devices):
    inner = CORES * SQUARE
    chips = [
        [base + CORES * spot + core for spot in range(SQUARE)]
        for base in range(0, devices, inner)
        for core in range(CORES)
    ]
    columns = [[base + inner * spot for spot in range(devices // inner)] for base in range(inner)]
    return (chips, columns)


def swap_cores(value, devices):
    return lax.ppermute(value, "fsdp", [(i, i ^ 1) for i in range(devices)])


def rounded(amount, step):
    return -(-amount // step) * step


def as_rows(block):
    rows = block.shape[1] // LANES
    return jnp.pad(block.reshape(rows, LANES), ((0, rounded(rows, 8) - rows), (0, 0)))


def exchange(part, groups):
    return lax.all_to_all(part, "fsdp", 0, 0, axis_index_groups=groups, tiled=True)


def gather_exchange(block, groups):
    return exchange(jnp.broadcast_to(block[None], (len(groups[0]),) + block.shape), groups)


def add_cores(keep, send, devices):
    other = swap_cores(send, devices)
    return (keep.astype(f32) + other.astype(f32)).astype(bf16)


def sum_exchange(part, groups):
    return jnp.sum(exchange(part, groups).astype(f32), axis=0)


def as_block(part, like):
    width = like.shape[1]
    return part.astype(f32)[: width // LANES].reshape(1, width)


def lay_out_blocks(core, mine_ref, other_ref, flat_ref):
    spots, depth, padded, lanes = mine_ref.shape
    rows = flat_ref.shape[0] // (CORES * spots * depth)
    for layer in range(depth):
        for spot in range(spots):
            base = (layer * spots + spot) * CORES * rows
            mine = mine_ref[spot, layer].astype(f32)[:rows]
            other = other_ref[spot, layer].astype(f32)[:rows]
            flat_ref[base : base + rows] = jnp.where(core == 0, mine, other)
            flat_ref[base + rows : base + 2 * rows] = jnp.where(core == 0, other, mine)


def cut_blocks(core, flat_ref, keep_ref, send_ref):
    spots, depth, padded, lanes = keep_ref.shape
    rows = flat_ref.shape[0] // (CORES * spots * depth)
    for layer in range(depth):
        for spot in range(spots):
            base = (layer * spots + spot) * CORES * rows
            first = flat_ref[base : base + padded]
            second = flat_ref[base + rows : base + rows + padded]
            keep_ref[spot, layer] = jnp.where(core == 0, first, second).astype(bf16)
            send_ref[spot, layer] = jnp.where(core == 0, second, first).astype(bf16)


def read_vector(flat_ref, at, amount):
    return jnp.concatenate([flat_ref[at + i : at + i + 1] for i in range(amount)], axis=1)


def write_vector(flat_ref, at, amount, value):
    for i in range(amount):
        flat_ref[at + i : at + i + 1] = value[:, i * LANES : (i + 1) * LANES]


def read_matrix(flat_ref, at, height, amount, out_ref):
    for i in range(amount):
        chunk = flat_ref[pl.ds(at + i, height, stride=amount), :]
        out_ref[:, i * LANES : (i + 1) * LANES] = chunk.astype(bf16)


def normalise(values):
    average = jnp.mean(values, axis=-1, keepdims=True)
    centred = values - average
    variance = jnp.mean(centred * centred, axis=-1, keepdims=True)
    inverse = lax.rsqrt(variance + epsilon)
    return (centred * inverse, inverse)


def norm_back(grad, unit, inverse, gain):
    scaled = grad * gain
    first = jnp.mean(scaled, axis=-1, keepdims=True)
    second = jnp.mean(scaled * unit, axis=-1, keepdims=True)
    return inverse * (scaled - first - unit * second)


def slot_mask(meta_ref, window, by_column):
    shape = (window, SPAN) if by_column else (SPAN, window)
    spot = lax.broadcasted_iota(jnp.int32, shape, 0 if by_column else 1)
    row = lax.broadcasted_iota(jnp.int32, shape, 1 if by_column else 0)
    start = jnp.where(row < SLOT, meta_ref[0], meta_ref[2] - SLOT)
    limit = jnp.where(row < SLOT, meta_ref[1], meta_ref[3] + SLOT)
    return jnp.where((spot == row + start) & (row < limit), 1.0, 0.0).astype(bf16)


def head_lanes(half):
    lane = lax.broadcasted_iota(jnp.int32, (1, LANES), 1)
    return (lane < HEAD_DIM) if half == 0 else (lane >= HEAD_DIM)


def attend_kernel(
    meta_ref, before_ref, own_ref, after_ref, mask_ref, mine_ref, other_ref,
    middle_ref, cotangent_ref, inputs_ref, normed_ref, qkv_ref, probability_ref,
    context_ref, classes_ref, w_qkv_ref, w_out_ref, gain_ref,
    flat_ref, window_ref,
):
    core = meta_ref[4]
    window = window_ref.shape[0]
    lay_out_blocks(core, mine_ref, other_ref, flat_ref)
    read_matrix(flat_ref, W_QKV_AT, D, QKV_ROWS, w_qkv_ref)
    read_matrix(flat_ref, W_OUT_AT, D, D_ROWS, w_out_ref)
    gain = read_vector(flat_ref, GAIN_AT, D_ROWS)
    shift = read_vector(flat_ref, SHIFT_AT, D_ROWS)
    gain_ref[...] = gain
    bias_query = read_vector(flat_ref, BIAS_QUERY_AT, D_ROWS)
    bias_value = read_vector(flat_ref, BIAS_VALUE_AT, D_ROWS)
    bias_out = read_vector(flat_ref, BIAS_OUT_AT, D_ROWS)
    table = (mask_ref[...] * flat_ref[TABLE_AT : TABLE_AT + 1]).astype(bf16)

    halo = before_ref.shape[0]
    own = own_ref.shape[0]
    window_ref[0:halo] = before_ref[...]
    window_ref[halo : halo + own] = own_ref[...]
    window_ref[halo + own : window] = after_ref[...]
    picked = dot(slot_mask(meta_ref, window, False), window_ref[...])
    inputs = picked[:, :D]
    inputs_ref[...] = inputs.astype(bf16)
    cotangent_ref[...] = picked[:, D : 2 * D].astype(bf16)
    classes_ref[...] = picked[:, 2 * D :].astype(bf16)

    unit, _ = normalise(inputs)
    normed_ref[...] = (unit * gain + shift).astype(bf16)
    normed = normed_ref[...]
    qkv_ref[:, :D] = (dot(normed, w_qkv_ref[:, :D]) + bias_query).astype(bf16)
    qkv_ref[:, D : 2 * D] = dot(normed, w_qkv_ref[:, D : 2 * D]).astype(bf16)
    qkv_ref[:, 2 * D :] = (dot(normed, w_qkv_ref[:, 2 * D :]) + bias_value).astype(bf16)

    for slot in range(2):
        rows = slice(slot * SLOT, (slot + 1) * SLOT)
        key = lax.broadcasted_iota(jnp.int32, (1, SLOT), 1)
        key_bias = dot_cols(table, classes_ref[rows])
        key_bias = jnp.where(key < meta_ref[2 * slot + 1], key_bias, masked_score)
        for pair in range(HEADS // 2):
            lanes = slice(pair * LANES, (pair + 1) * LANES)
            queries = qkv_ref[rows, lanes]
            keys = qkv_ref[rows, D + pair * LANES : D + (pair + 1) * LANES]
            values = qkv_ref[rows, 2 * D + pair * LANES : 2 * D + (pair + 1) * LANES]
            mixed = []
            for half in range(2):
                head = 2 * pair + half
                chosen = jnp.where(head_lanes(half), queries, jnp.zeros_like(queries))
                scores = dot_cols(chosen, keys) * score_scale + key_bias[head : head + 1]
                peak = jnp.max(scores, axis=-1, keepdims=True)
                weights = jnp.exp(scores - peak)
                total = jnp.sum(weights, axis=-1, keepdims=True)
                probability = (weights * (1.0 / total)).astype(bf16)
                probability_ref[slot * HEADS + head] = probability
                mixed.append(dot(probability, values))
            context_ref[rows, lanes] = jnp.where(head_lanes(0), mixed[0], mixed[1]).astype(bf16)
    middle_ref[...] = inputs + dot(context_ref[...], w_out_ref[...]) + bias_out


def feed_kernel(
    meta_ref, middle_ref, cotangent_ref, mine_ref, other_ref,
    output_ref, grad_middle_ref, keep_ref, send_ref,
    flat_ref, w_up_ref, w_down_ref, normed_ref,
):
    core = meta_ref[4]
    window = output_ref.shape[0]
    lay_out_blocks(core, mine_ref, other_ref, flat_ref)
    read_matrix(flat_ref, W_UP_AT, D, FF_ROWS, w_up_ref)
    read_matrix(flat_ref, W_DOWN_AT, FF, D_ROWS, w_down_ref)
    gain = read_vector(flat_ref, GAIN_AT, D_ROWS)
    shift = read_vector(flat_ref, SHIFT_AT, D_ROWS)
    bias_up = read_vector(flat_ref, BIAS_UP_AT, FF_ROWS)
    bias_down = read_vector(flat_ref, BIAS_DOWN_AT, D_ROWS)

    middle = middle_ref[...]
    cotangent = cotangent_ref[...]
    unit, inverse = normalise(middle)
    normed_ref[...] = (unit * gain + shift).astype(bf16)
    normed = normed_ref[...]
    output = middle + bias_down
    grad = jnp.zeros((SPAN, D), f32)
    slope = math.sqrt(2.0 / math.pi)
    for step in range(FF // D):
        cols = slice(step * D, (step + 1) * D)
        w_up = w_up_ref[:, cols]
        w_down = w_down_ref[cols]
        hidden = dot(normed, w_up) + bias_up[:, cols]
        square = hidden * hidden
        bend = jnp.tanh(slope * hidden * (1.0 + 0.044715 * square))
        half = 0.5 * (1.0 + bend)
        active = (hidden * half).astype(bf16)
        steep = half + 0.5 * hidden * (1.0 - bend * bend) * (
            slope * (1.0 + (3 * 0.044715) * square)
        )
        grad_hidden_wide = dot_cols(cotangent, w_down) * steep
        grad_hidden = grad_hidden_wide.astype(bf16)
        output = output + dot(active, w_down)
        grad = grad + dot_cols(grad_hidden, w_up)
        grad_down = dot_rows(active, cotangent)
        grad_up = dot_rows(normed, grad_hidden)
        grad_bias = jnp.sum(grad_hidden.astype(f32), axis=0, keepdims=True)
        write_vector(flat_ref, BIAS_UP_AT + step * D_ROWS, D_ROWS, grad_bias)
        for i in range(D_ROWS):
            lanes = slice(i * LANES, (i + 1) * LANES)
            flat_ref[pl.ds(W_UP_AT + step * D_ROWS + i, D, stride=FF_ROWS), :] = grad_up[:, lanes]
            flat_ref[pl.ds(W_DOWN_AT + step * D * D_ROWS + i, D, stride=D_ROWS), :] = grad_down[
                :, lanes
            ]
    output_ref[...] = dot(slot_mask(meta_ref, window, True), output.astype(bf16)).astype(bf16)
    grad_output = cotangent.astype(f32)
    write_vector(flat_ref, GAIN_AT, D_ROWS, jnp.sum(grad * unit, axis=0, keepdims=True))
    write_vector(flat_ref, SHIFT_AT, D_ROWS, jnp.sum(grad, axis=0, keepdims=True))
    write_vector(flat_ref, BIAS_DOWN_AT, D_ROWS, jnp.sum(grad_output, axis=0, keepdims=True))
    flat_ref[FEED_END:] = jnp.zeros((flat_ref.shape[0] - FEED_END, LANES), f32)
    grad_middle_ref[...] = grad_output + norm_back(grad, unit, inverse, gain)
    cut_blocks(core, flat_ref, keep_ref, send_ref)


def attend_back_kernel(
    meta_ref, grad_middle_ref, mask_ref, qkv_ref, probability_ref, context_ref, classes_ref,
    w_out_ref,
    grad_qkv_ref, grad_w_out_ref, grad_bias_out_ref, grad_table_ref,
    grad_context_ref,
):
    grad_branch = grad_middle_ref[...].astype(bf16)
    grad_bias_out_ref[...] = jnp.sum(grad_branch.astype(f32), axis=0, keepdims=True)
    grad_w_out_ref[...] = dot_rows(context_ref[...], grad_branch)
    grad_context_ref[...] = dot_cols(grad_branch, w_out_ref[...]).astype(bf16)
    grad_table = jnp.zeros((8, LANES), f32)
    for slot in range(2):
        rows = slice(slot * SLOT, (slot + 1) * SLOT)
        key_sums = []
        for pair in range(HEADS // 2):
            lanes = slice(pair * LANES, (pair + 1) * LANES)
            key_lanes = slice(D + pair * LANES, D + (pair + 1) * LANES)
            value_lanes = slice(2 * D + pair * LANES, 2 * D + (pair + 1) * LANES)
            queries = qkv_ref[rows, lanes]
            keys = qkv_ref[rows, key_lanes]
            values = qkv_ref[rows, value_lanes]
            grad_context = grad_context_ref[rows, lanes]
            parts = []
            for half in range(2):
                head = 2 * pair + half
                chosen = jnp.where(head_lanes(half), grad_context, jnp.zeros_like(grad_context))
                grad_probs = dot_cols(chosen, values)
                narrow = probability_ref[slot * HEADS + head]
                probability = narrow.astype(f32)
                weighted = probability * grad_probs
                grad_scores = weighted - probability * jnp.sum(weighted, axis=-1, keepdims=True)
                key_sums.append(jnp.sum(grad_scores, axis=0, keepdims=True))
                grad_raw = (grad_scores * score_scale).astype(bf16)
                parts.append(
                    (dot(grad_raw, keys), dot_rows(grad_raw, queries), dot_rows(narrow, grad_context))
                )
            low = head_lanes(0)
            for where, first, second in zip((lanes, key_lanes, value_lanes), *parts):
                grad_qkv_ref[rows, where] = jnp.where(low, first, second).astype(bf16)
        sums = jnp.concatenate(key_sums + [jnp.zeros((8 - HEADS, SLOT), f32)], axis=0)
        sums_high = sums.astype(bf16)
        sums_low = (sums - sums_high.astype(f32)).astype(bf16)
        classes = classes_ref[rows]
        grad_table = grad_table + dot(sums_high, classes) + dot(sums_low, classes)
    grad_table_ref[...] = jnp.sum(grad_table * mask_ref[...], axis=0, keepdims=True)


def inputs_back_kernel(
    meta_ref, grad_middle_ref, inputs_ref, normed_ref, w_qkv_ref, gain_ref,
    grad_qkv_ref, grad_w_out_ref, grad_bias_out_ref, grad_table_ref,
    grad_inputs_ref, keep_ref, send_ref,
    flat_ref,
):
    core = meta_ref[4]
    window = grad_inputs_ref.shape[0]
    flat_ref[TABLE_AT:] = jnp.zeros((flat_ref.shape[0] - TABLE_AT, LANES), f32)
    flat_ref[TABLE_AT : TABLE_AT + 1] = grad_table_ref[...]
    write_vector(flat_ref, BIAS_OUT_AT, D_ROWS, grad_bias_out_ref[...])
    for i in range(D_ROWS):
        flat_ref[pl.ds(W_OUT_AT + i, D, stride=D_ROWS), :] = grad_w_out_ref[
            :, i * LANES : (i + 1) * LANES
        ]
    grad_qkv = grad_qkv_ref[...]
    column_sums = jnp.sum(grad_qkv.astype(f32), axis=0, keepdims=True)
    write_vector(flat_ref, BIAS_QUERY_AT, D_ROWS, column_sums[:, :D])
    write_vector(flat_ref, BIAS_VALUE_AT, D_ROWS, column_sums[:, 2 * D :])
    normed = normed_ref[...]
    for part in range(3):
        grad_w = dot_rows(normed, grad_qkv_ref[:, part * D : (part + 1) * D])
        for i in range(D_ROWS):
            flat_ref[pl.ds(W_QKV_AT + part * D_ROWS + i, D, stride=QKV_ROWS), :] = grad_w[
                :, i * LANES : (i + 1) * LANES
            ]
    grad_normed = dot_cols(grad_qkv, w_qkv_ref[...])
    gain = gain_ref[...]
    unit, inverse = normalise(inputs_ref[...].astype(f32))
    write_vector(flat_ref, GAIN_AT, D_ROWS, jnp.sum(grad_normed * unit, axis=0, keepdims=True))
    write_vector(flat_ref, SHIFT_AT, D_ROWS, jnp.sum(grad_normed, axis=0, keepdims=True))
    grad_inputs = grad_middle_ref[...] + norm_back(grad_normed, unit, inverse, gain)
    high = grad_inputs.astype(bf16)
    low_part = (grad_inputs - high.astype(f32)).astype(bf16)
    back = slot_mask(meta_ref, window, True)
    grad_inputs_ref[...] = dot(back, high) + dot(back, low_part)
    cut_blocks(core, flat_ref, keep_ref, send_ref)


def call_kernel(kernel, out_shapes, scratch, flops, operands):
    vmem = pl.BlockSpec(memory_space=pltpu.VMEM)
    specs = [pl.BlockSpec(memory_space=pltpu.SMEM)] + [vmem] * (len(operands) - 1)
    moved = sum(math.prod(o.shape) * o.dtype.itemsize for o in list(operands) + list(out_shapes))
    return pl.pallas_call(
        kernel,
        out_shape=out_shapes,
        in_specs=specs,
        out_specs=[vmem] * len(out_shapes),
        scratch_shapes=scratch,
        compiler_params=pltpu.CompilerParams(vmem_limit_bytes=50 * 1024 * 1024),
        cost_estimate=pl.CostEstimate(flops=flops, bytes_accessed=moved, transcendentals=0),
    )(*operands)


def plan_slots(image_id, devices):
    token_rows = image_id.shape[0]
    device = lax.axis_index("fsdp")
    ends = jnp.sum((image_id == image_id[0]).astype(jnp.int32))
    first, last = device == 0, device == devices - 1
    holds = first | (ends >= IMG // 2 + 1)
    start = jnp.where(first, 0, jnp.where(holds, ends - IMG, ends))
    stop = jnp.where(last, token_rows, token_rows + IMG)
    stop_one = jnp.where(holds, ends, jnp.minimum(ends + IMG, stop))
    next_centre = stop_one + IMG // 2
    has_next = (stop_one < stop) & (last | (next_centre < token_rows))
    stop_two = jnp.where(has_next, jnp.minimum(stop_one + IMG, stop), stop_one)
    zero = jnp.zeros((), jnp.int32)
    return jnp.stack(
        [start + HALO, stop_one - start, stop_one + HALO, stop_two - stop_one, device % CORES]
        + [zero] * 3
    ).astype(jnp.int32)


def struct(shape, kind):
    return jax.ShapeDtypeStruct(shape, kind)


def shards(inputs, attn_blocks, mlp_blocks, image_id, bias_id, out_grad):
    token_rows = inputs.shape[0]
    devices = lax.axis_size("fsdp")
    chips, columns = groups_of(devices)
    depth = devices // (CORES * SQUARE)
    window = token_rows + 2 * HALO
    attn_flat = devices * attn_blocks.shape[1] // LANES
    mlp_flat = devices * mlp_blocks.shape[1] // LANES
    barrier = lax.optimization_barrier

    lane = jnp.arange(LANES, dtype=jnp.int32)
    classes = ((lane // HEADS)[None, :] == bias_id[:, None]) & (lane < NB * HEADS)[None, :]
    tokens = jnp.concatenate([inputs, out_grad, classes.astype(bf16)], axis=1)
    up = [(i, i + 1) for i in range(devices - 1)]
    down = [(i + 1, i) for i in range(devices - 1)]
    meta = plan_slots(image_id, devices)
    head = jnp.arange(8, dtype=jnp.int32)
    head_mask = ((lane % HEADS)[None, :] == head[:, None]) & (lane < NB * HEADS)[None, :]
    head_mask = head_mask.astype(f32)

    mlp_column = lax.all_gather(as_rows(mlp_blocks), "fsdp", axis_index_groups=columns)
    attn_column = gather_exchange(as_rows(attn_blocks), columns)
    before = lax.ppermute(tokens[token_rows - HALO :], "fsdp", up)
    after = lax.ppermute(tokens[:HALO], "fsdp", down)
    attn_column, before, after = barrier((attn_column, before, after))
    attn_mine = gather_exchange(attn_column, chips)
    mlp_column, attn_mine = barrier((mlp_column, attn_mine))
    mlp_mine = gather_exchange(mlp_column, chips)
    attn_other = swap_cores(attn_mine, devices)
    mlp_other = swap_cores(mlp_mine, devices)

    (
        middle, cotangent, inputs_span, normed, qkv, probability, context, classes_span,
        w_qkv, w_out, gain,
    ) = call_kernel(
        attend_kernel,
        [
            struct((SPAN, D), f32),
            struct((SPAN, D), bf16),
            struct((SPAN, D), bf16),
            struct((SPAN, D), bf16),
            struct((SPAN, 3 * D), bf16),
            struct((2 * HEADS, SLOT, SLOT), bf16),
            struct((SPAN, D), bf16),
            struct((SPAN, LANES), bf16),
            struct((D, 3 * D), bf16),
            struct((D, D), bf16),
            struct((1, D), f32),
        ],
        [pltpu.VMEM((attn_flat, LANES), f32), pltpu.VMEM((window, WIDE), bf16)],
        5 * 10**9,
        [meta, before, tokens, after, head_mask, attn_mine, attn_other],
    )
    feed_blocks = struct((SQUARE, depth, mlp_column.shape[1], LANES), bf16)
    output, grad_middle, feed_keep, feed_send = call_kernel(
        feed_kernel,
        [struct((window, D), bf16), struct((SPAN, D), f32), feed_blocks, feed_blocks],
        [
            pltpu.VMEM((mlp_flat + 8, LANES), f32),
            pltpu.VMEM((D, FF), bf16),
            pltpu.VMEM((FF, D), bf16),
            pltpu.VMEM((SPAN, D), bf16),
        ],
        9 * 10**9,
        [meta, middle, cotangent, mlp_mine, mlp_other],
    )
    feed_part = add_cores(feed_keep, feed_send, devices)
    grad_qkv, grad_w_out, grad_bias_out, grad_table = call_kernel(
        attend_back_kernel,
        [
            struct((SPAN, 3 * D), bf16),
            struct((D, D), f32),
            struct((1, D), f32),
            struct((1, LANES), f32),
        ],
        [pltpu.VMEM((SPAN, D), bf16)],
        5 * 10**9,
        [meta, grad_middle, head_mask, qkv, probability, context, classes_span, w_out],
    )
    feed_part, grad_qkv = barrier((feed_part, grad_qkv))
    feed_part = sum_exchange(feed_part, chips).astype(bf16)
    attn_blocks_out = struct((SQUARE, depth, attn_column.shape[1], LANES), bf16)
    grad_inputs, attn_keep, attn_send = call_kernel(
        inputs_back_kernel,
        [struct((window, D), f32), attn_blocks_out, attn_blocks_out],
        [pltpu.VMEM((attn_flat + 8, LANES), f32)],
        5 * 10**9,
        [
            meta, grad_middle, inputs_span, normed, w_qkv, gain,
            grad_qkv, grad_w_out, grad_bias_out, grad_table,
        ],
    )
    attn_part = add_cores(attn_keep, attn_send, devices)
    attn_part, feed_part = barrier((attn_part, feed_part))
    feed_sum = lax.psum_scatter(feed_part, "fsdp", scatter_dimension=0, axis_index_groups=columns)
    feed_sum = barrier(feed_sum)
    attn_part = sum_exchange(attn_part, chips).astype(bf16)
    attn_sum = sum_exchange(attn_part, columns)
    edges = jnp.concatenate([output, grad_inputs.astype(bf16)], axis=1)
    from_next = lax.ppermute(edges[:HALO], "fsdp", down)
    from_last = lax.ppermute(edges[window - HALO :], "fsdp", up)
    gap = jnp.zeros((token_rows - HALO, 2 * D), bf16)
    extra = jnp.concatenate([from_last, gap]) + jnp.concatenate([gap, from_next])
    own = slice(HALO, HALO + token_rows)
    output = output[own] + extra[:, :D]
    grad_inputs = grad_inputs[own] + extra[:, D:].astype(f32)
    return (output, grad_inputs, as_block(attn_sum, attn_blocks), as_block(feed_sum, mlp_blocks))


def solution(mesh):
    return jax.shard_map(
        shards,
        mesh=mesh,
        in_specs=(
            P("fsdp", None),
            P("fsdp", None),
            P("fsdp", None),
            P("fsdp"),
            P("fsdp"),
            P("fsdp", None),
        ),
        out_specs=(P("fsdp", None), P("fsdp", None), P("fsdp", None), P("fsdp", None)),
        check_vma=False,
    )
```

```python
import functools
import math

import jax
import jax.numpy as jnp
from jax import lax
from jax.experimental import pallas as pl
from jax.experimental.pallas import tpu as pltpu
from jax.sharding import PartitionSpec as P

D = 384
FF = 1536
HEADS = 6
HEAD_DIM = 64
IMG = 197
NB = 16

LANES = 128
CORES = 2
SQUARE = 4
SLOT = 208
SPAN = 2 * SLOT
HALO = 112
WIDE = 2 * D + LANES
D_ROWS = D // LANES
FF_ROWS = FF // LANES
QKV_ROWS = 3 * D // LANES

GAIN_AT = 0
SHIFT_AT = D_ROWS
W_QKV_AT = 2 * D_ROWS
BIAS_QUERY_AT = W_QKV_AT + D * QKV_ROWS
BIAS_VALUE_AT = BIAS_QUERY_AT + D_ROWS
W_OUT_AT = BIAS_VALUE_AT + D_ROWS
BIAS_OUT_AT = W_OUT_AT + D * D_ROWS
TABLE_AT = BIAS_OUT_AT + D_ROWS
W_UP_AT = 2 * D_ROWS
BIAS_UP_AT = W_UP_AT + D * FF_ROWS
W_DOWN_AT = BIAS_UP_AT + FF_ROWS
BIAS_DOWN_AT = W_DOWN_AT + FF * D_ROWS
FEED_END = BIAS_DOWN_AT + D_ROWS

epsilon = 1e-06
score_scale = HEAD_DIM ** (-0.5)
masked_score = -1e30
f32 = jnp.float32
bf16 = jnp.bfloat16


def dot(left, right):
    return lax.dot_general(left, right, (((1,), (0,)), ((), ())), preferred_element_type=f32)


def dot_rows(left, right):
    return lax.dot_general(left, right, (((0,), (0,)), ((), ())), preferred_element_type=f32)


def dot_cols(left, right):
    return lax.dot_general(left, right, (((1,), (1,)), ((), ())), preferred_element_type=f32)


def groups_of(devices):
    inner = CORES * SQUARE
    chips = [
        [base + CORES * spot + core for spot in range(SQUARE)]
        for base in range(0, devices, inner)
        for core in range(CORES)
    ]
    columns = [[base + inner * spot for spot in range(devices // inner)] for base in range(inner)]
    return (chips, columns)


def pass_column(value, step, devices):
    inner = CORES * SQUARE
    return lax.ppermute(value, "fsdp", [(i, i ^ (step * inner)) for i in range(devices)])


def swap_cores(value, devices):
    return lax.ppermute(value, "fsdp", [(i, i ^ 1) for i in range(devices)])


def rounded(amount, step):
    return -(-amount // step) * step


def as_rows(block):
    rows = block.shape[1] // LANES
    return jnp.pad(block.reshape(rows, LANES), ((0, rounded(rows, 8) - rows), (0, 0)))


def exchange(part, groups):
    return lax.all_to_all(part, "fsdp", 0, 0, axis_index_groups=groups, tiled=True)


def gather_exchange(block, groups):
    return exchange(jnp.broadcast_to(block[None], (len(groups[0]),) + block.shape), groups)


def add_cores(keep, send, devices):
    other = swap_cores(send, devices)
    return (keep.astype(f32) + other.astype(f32)).astype(bf16)


def sum_exchange(part, groups):
    return jnp.sum(exchange(part, groups).astype(f32), axis=0)


def as_block(part, like):
    width = like.shape[1]
    return part.astype(f32)[: width // LANES].reshape(1, width)


def lay_out_blocks(core, mine_ref, other_ref, flat_ref):
    spots, depth, padded, lanes = mine_ref.shape
    rows = flat_ref.shape[0] // (CORES * spots * depth)
    for layer in range(depth):
        for spot in range(spots):
            base = (layer * spots + spot) * CORES * rows
            mine = mine_ref[spot, layer].astype(f32)[:rows]
            other = other_ref[spot, layer].astype(f32)[:rows]
            flat_ref[base : base + rows] = jnp.where(core == 0, mine, other)
            flat_ref[base + rows : base + 2 * rows] = jnp.where(core == 0, other, mine)


def cut_blocks(core, flat_ref, keep_ref, send_ref):
    spots, depth, padded, lanes = keep_ref.shape
    rows = flat_ref.shape[0] // (CORES * spots * depth)
    for layer in range(depth):
        for spot in range(spots):
            base = (layer * spots + spot) * CORES * rows
            first = flat_ref[base : base + padded]
            second = flat_ref[base + rows : base + rows + padded]
            keep_ref[spot, layer] = jnp.where(core == 0, first, second).astype(bf16)
            send_ref[spot, layer] = jnp.where(core == 0, second, first).astype(bf16)


def spread_kernel(meta_ref, *refs):
    spread_ref = refs[-1]
    for step, part_ref in enumerate(refs[:-1]):
        block = part_ref[...]
        for spot in range(SQUARE):
            spread_ref[spot, meta_ref[5] ^ step] = block


def sum_chips_kernel(meta_ref, parts_ref, *out_refs):
    for step, out_ref in enumerate(out_refs):
        layer = meta_ref[5] ^ step
        total = parts_ref[0, layer].astype(f32)
        for spot in range(1, SQUARE):
            total = total + parts_ref[spot, layer].astype(f32)
        out_ref[...] = total.astype(bf16)


def read_vector(flat_ref, at, amount):
    return jnp.concatenate([flat_ref[at + i : at + i + 1] for i in range(amount)], axis=1)


def write_vector(flat_ref, at, amount, value):
    for i in range(amount):
        flat_ref[at + i : at + i + 1] = value[:, i * LANES : (i + 1) * LANES]


def read_matrix(flat_ref, at, height, amount, out_ref):
    for i in range(amount):
        chunk = flat_ref[pl.ds(at + i, height, stride=amount), :]
        out_ref[:, i * LANES : (i + 1) * LANES] = chunk.astype(bf16)


def normalise(values):
    average = jnp.mean(values, axis=-1, keepdims=True)
    centred = values - average
    variance = jnp.mean(centred * centred, axis=-1, keepdims=True)
    inverse = lax.rsqrt(variance + epsilon)
    return (centred * inverse, inverse)


def norm_back(grad, unit, inverse, gain):
    scaled = grad * gain
    first = jnp.mean(scaled, axis=-1, keepdims=True)
    second = jnp.mean(scaled * unit, axis=-1, keepdims=True)
    return inverse * (scaled - first - unit * second)


def slot_mask(meta_ref, window, by_column):
    shape = (window, SPAN) if by_column else (SPAN, window)
    spot = lax.broadcasted_iota(jnp.int32, shape, 0 if by_column else 1)
    row = lax.broadcasted_iota(jnp.int32, shape, 1 if by_column else 0)
    start = jnp.where(row < SLOT, meta_ref[0], meta_ref[2] - SLOT)
    limit = jnp.where(row < SLOT, meta_ref[1], meta_ref[3] + SLOT)
    return jnp.where((spot == row + start) & (row < limit), 1.0, 0.0).astype(bf16)


def head_lanes(half):
    lane = lax.broadcasted_iota(jnp.int32, (1, LANES), 1)
    return (lane < HEAD_DIM) if half == 0 else (lane >= HEAD_DIM)


def attend_kernel(
    meta_ref, before_ref, own_ref, after_ref, mask_ref, mine_ref, other_ref,
    middle_ref, cotangent_ref, inputs_ref, normed_ref, qkv_ref, probability_ref,
    context_ref, classes_ref, w_qkv_ref, w_out_ref, gain_ref,
    flat_ref, window_ref,
):
    core = meta_ref[4]
    window = window_ref.shape[0]
    lay_out_blocks(core, mine_ref, other_ref, flat_ref)
    read_matrix(flat_ref, W_QKV_AT, D, QKV_ROWS, w_qkv_ref)
    read_matrix(flat_ref, W_OUT_AT, D, D_ROWS, w_out_ref)
    gain = read_vector(flat_ref, GAIN_AT, D_ROWS)
    shift = read_vector(flat_ref, SHIFT_AT, D_ROWS)
    gain_ref[...] = gain
    bias_query = read_vector(flat_ref, BIAS_QUERY_AT, D_ROWS)
    bias_value = read_vector(flat_ref, BIAS_VALUE_AT, D_ROWS)
    bias_out = read_vector(flat_ref, BIAS_OUT_AT, D_ROWS)
    table = (mask_ref[...] * flat_ref[TABLE_AT : TABLE_AT + 1]).astype(bf16)

    halo = before_ref.shape[0]
    own = own_ref.shape[0]
    window_ref[0:halo] = before_ref[...]
    window_ref[halo : halo + own] = own_ref[...]
    window_ref[halo + own : window] = after_ref[...]
    picked = dot(slot_mask(meta_ref, window, False), window_ref[...])
    inputs = picked[:, :D]
    inputs_ref[...] = inputs.astype(bf16)
    cotangent_ref[...] = picked[:, D : 2 * D].astype(bf16)
    classes_ref[...] = picked[:, 2 * D :].astype(bf16)

    unit, _ = normalise(inputs)
    normed_ref[...] = (unit * gain + shift).astype(bf16)
    normed = normed_ref[...]
    qkv_ref[:, :D] = (dot(normed, w_qkv_ref[:, :D]) + bias_query).astype(bf16)
    qkv_ref[:, D : 2 * D] = dot(normed, w_qkv_ref[:, D : 2 * D]).astype(bf16)
    qkv_ref[:, 2 * D :] = (dot(normed, w_qkv_ref[:, 2 * D :]) + bias_value).astype(bf16)

    for slot in range(2):
        rows = slice(slot * SLOT, (slot + 1) * SLOT)
        key = lax.broadcasted_iota(jnp.int32, (1, SLOT), 1)
        key_bias = dot_cols(table, classes_ref[rows])
        key_bias = jnp.where(key < meta_ref[2 * slot + 1], key_bias, masked_score)
        for pair in range(HEADS // 2):
            lanes = slice(pair * LANES, (pair + 1) * LANES)
            queries = qkv_ref[rows, lanes]
            keys = qkv_ref[rows, D + pair * LANES : D + (pair + 1) * LANES]
            values = qkv_ref[rows, 2 * D + pair * LANES : 2 * D + (pair + 1) * LANES]
            mixed = []
            for half in range(2):
                head = 2 * pair + half
                chosen = jnp.where(head_lanes(half), queries, jnp.zeros_like(queries))
                scores = dot_cols(chosen, keys) * score_scale + key_bias[head : head + 1]
                peak = jnp.max(scores, axis=-1, keepdims=True)
                weights = jnp.exp(scores - peak)
                total = jnp.sum(weights, axis=-1, keepdims=True)
                probability = (weights * (1.0 / total)).astype(bf16)
                probability_ref[slot * HEADS + head] = probability
                mixed.append(dot(probability, values))
            context_ref[rows, lanes] = jnp.where(head_lanes(0), mixed[0], mixed[1]).astype(bf16)
    middle_ref[...] = inputs + dot(context_ref[...], w_out_ref[...]) + bias_out


def feed_kernel(
    meta_ref, middle_ref, cotangent_ref, mine_ref, other_ref,
    output_ref, grad_middle_ref, keep_ref, send_ref,
    flat_ref, w_up_ref, w_down_ref, normed_ref,
):
    core = meta_ref[4]
    window = output_ref.shape[0]
    lay_out_blocks(core, mine_ref, other_ref, flat_ref)
    read_matrix(flat_ref, W_UP_AT, D, FF_ROWS, w_up_ref)
    read_matrix(flat_ref, W_DOWN_AT, FF, D_ROWS, w_down_ref)
    gain = read_vector(flat_ref, GAIN_AT, D_ROWS)
    shift = read_vector(flat_ref, SHIFT_AT, D_ROWS)
    bias_up = read_vector(flat_ref, BIAS_UP_AT, FF_ROWS)
    bias_down = read_vector(flat_ref, BIAS_DOWN_AT, D_ROWS)

    middle = middle_ref[...]
    cotangent = cotangent_ref[...]
    unit, inverse = normalise(middle)
    normed_ref[...] = (unit * gain + shift).astype(bf16)
    normed = normed_ref[...]
    output = middle + bias_down
    grad = jnp.zeros((SPAN, D), f32)
    slope = math.sqrt(2.0 / math.pi)
    for step in range(FF // D):
        cols = slice(step * D, (step + 1) * D)
        w_up = w_up_ref[:, cols]
        w_down = w_down_ref[cols]
        hidden = dot(normed, w_up) + bias_up[:, cols]
        square = hidden * hidden
        bend = jnp.tanh(slope * hidden * (1.0 + 0.044715 * square))
        half = 0.5 * (1.0 + bend)
        active = (hidden * half).astype(bf16)
        steep = half + 0.5 * hidden * (1.0 - bend * bend) * (
            slope * (1.0 + (3 * 0.044715) * square)
        )
        grad_hidden_wide = dot_cols(cotangent, w_down) * steep
        grad_hidden = grad_hidden_wide.astype(bf16)
        output = output + dot(active, w_down)
        grad = grad + dot_cols(grad_hidden, w_up)
        grad_down = dot_rows(active, cotangent)
        grad_up = dot_rows(normed, grad_hidden)
        grad_bias = jnp.sum(grad_hidden.astype(f32), axis=0, keepdims=True)
        write_vector(flat_ref, BIAS_UP_AT + step * D_ROWS, D_ROWS, grad_bias)
        for i in range(D_ROWS):
            lanes = slice(i * LANES, (i + 1) * LANES)
            flat_ref[pl.ds(W_UP_AT + step * D_ROWS + i, D, stride=FF_ROWS), :] = grad_up[:, lanes]
            flat_ref[pl.ds(W_DOWN_AT + step * D * D_ROWS + i, D, stride=D_ROWS), :] = grad_down[
                :, lanes
            ]
    output_ref[...] = dot(slot_mask(meta_ref, window, True), output.astype(bf16)).astype(bf16)
    grad_output = cotangent.astype(f32)
    write_vector(flat_ref, GAIN_AT, D_ROWS, jnp.sum(grad * unit, axis=0, keepdims=True))
    write_vector(flat_ref, SHIFT_AT, D_ROWS, jnp.sum(grad, axis=0, keepdims=True))
    write_vector(flat_ref, BIAS_DOWN_AT, D_ROWS, jnp.sum(grad_output, axis=0, keepdims=True))
    flat_ref[FEED_END:] = jnp.zeros((flat_ref.shape[0] - FEED_END, LANES), f32)
    grad_middle_ref[...] = grad_output + norm_back(grad, unit, inverse, gain)
    cut_blocks(core, flat_ref, keep_ref, send_ref)


def slot_back(
    slot, qkv_ref, probability_ref, classes_ref, grad_context_ref, grad_qkv_ref
):
    rows = slice(slot * SLOT, (slot + 1) * SLOT)
    key_sums = []
    for pair in range(HEADS // 2):
        lanes = slice(pair * LANES, (pair + 1) * LANES)
        key_lanes = slice(D + pair * LANES, D + (pair + 1) * LANES)
        value_lanes = slice(2 * D + pair * LANES, 2 * D + (pair + 1) * LANES)
        queries = qkv_ref[rows, lanes]
        keys = qkv_ref[rows, key_lanes]
        values = qkv_ref[rows, value_lanes]
        grad_context = grad_context_ref[rows, lanes]
        parts = []
        for half in range(2):
            head = 2 * pair + half
            chosen = jnp.where(head_lanes(half), grad_context, jnp.zeros_like(grad_context))
            grad_probs = dot_cols(chosen, values)
            narrow = probability_ref[slot * HEADS + head]
            probability = narrow.astype(f32)
            weighted = probability * grad_probs
            grad_scores = weighted - probability * jnp.sum(weighted, axis=-1, keepdims=True)
            key_sums.append(jnp.sum(grad_scores, axis=0, keepdims=True))
            grad_raw = (grad_scores * score_scale).astype(bf16)
            parts.append(
                (dot(grad_raw, keys), dot_rows(grad_raw, queries), dot_rows(narrow, grad_context))
            )
        low = head_lanes(0)
        for where, first, second in zip((lanes, key_lanes, value_lanes), *parts):
            grad_qkv_ref[:, where] = jnp.where(low, first, second).astype(bf16)
    sums = jnp.concatenate(key_sums + [jnp.zeros((8 - HEADS, SLOT), f32)], axis=0)
    sums_high = sums.astype(bf16)
    sums_low = (sums - sums_high.astype(f32)).astype(bf16)
    classes = classes_ref[rows]
    return dot(sums_high, classes) + dot(sums_low, classes)


def attend_back_kernel(
    meta_ref, grad_middle_ref, qkv_ref, probability_ref, context_ref, classes_ref, w_out_ref,
    grad_qkv_ref, grad_w_out_ref, grad_bias_out_ref, grad_table_ref, grad_context_ref,
):
    grad_branch = grad_middle_ref[...].astype(bf16)
    grad_bias_out_ref[...] = jnp.sum(grad_branch.astype(f32), axis=0, keepdims=True)
    grad_w_out_ref[...] = dot_rows(context_ref[...], grad_branch)
    grad_context_ref[...] = dot_cols(grad_branch, w_out_ref[...]).astype(bf16)
    grad_table_ref[...] = slot_back(
        0, qkv_ref, probability_ref, classes_ref, grad_context_ref, grad_qkv_ref
    )


def inputs_back_kernel(
    meta_ref, grad_middle_ref, mask_ref, inputs_ref, normed_ref, qkv_ref, probability_ref,
    classes_ref, w_qkv_ref, gain_ref,
    grad_first_ref, grad_w_out_ref, grad_bias_out_ref, grad_table_ref, grad_context_ref,
    grad_inputs_ref, keep_ref, send_ref,
    flat_ref, grad_second_ref, grad_qkv_ref,
):
    core = meta_ref[4]
    window = grad_inputs_ref.shape[0]
    grad_table = grad_table_ref[...] + slot_back(
        1, qkv_ref, probability_ref, classes_ref, grad_context_ref, grad_second_ref
    )
    grad_qkv_ref[:SLOT] = grad_first_ref[...]
    grad_qkv_ref[SLOT:] = grad_second_ref[...]
    flat_ref[TABLE_AT:] = jnp.zeros((flat_ref.shape[0] - TABLE_AT, LANES), f32)
    flat_ref[TABLE_AT : TABLE_AT + 1] = jnp.sum(grad_table * mask_ref[...], axis=0, keepdims=True)
    write_vector(flat_ref, BIAS_OUT_AT, D_ROWS, grad_bias_out_ref[...])
    for i in range(D_ROWS):
        flat_ref[pl.ds(W_OUT_AT + i, D, stride=D_ROWS), :] = grad_w_out_ref[
            :, i * LANES : (i + 1) * LANES
        ]
    grad_qkv = grad_qkv_ref[...]
    column_sums = jnp.sum(grad_qkv.astype(f32), axis=0, keepdims=True)
    write_vector(flat_ref, BIAS_QUERY_AT, D_ROWS, column_sums[:, :D])
    write_vector(flat_ref, BIAS_VALUE_AT, D_ROWS, column_sums[:, 2 * D :])
    normed = normed_ref[...]
    for part in range(3):
        grad_w = dot_rows(normed, grad_qkv_ref[:, part * D : (part + 1) * D])
        for i in range(D_ROWS):
            flat_ref[pl.ds(W_QKV_AT + part * D_ROWS + i, D, stride=QKV_ROWS), :] = grad_w[
                :, i * LANES : (i + 1) * LANES
            ]
    grad_normed = dot_cols(grad_qkv, w_qkv_ref[...])
    gain = gain_ref[...]
    unit, inverse = normalise(inputs_ref[...].astype(f32))
    write_vector(flat_ref, GAIN_AT, D_ROWS, jnp.sum(grad_normed * unit, axis=0, keepdims=True))
    write_vector(flat_ref, SHIFT_AT, D_ROWS, jnp.sum(grad_normed, axis=0, keepdims=True))
    grad_inputs = grad_middle_ref[...] + norm_back(grad_normed, unit, inverse, gain)
    high = grad_inputs.astype(bf16)
    low_part = (grad_inputs - high.astype(f32)).astype(bf16)
    back = slot_mask(meta_ref, window, True)
    grad_inputs_ref[...] = dot(back, high) + dot(back, low_part)
    cut_blocks(core, flat_ref, keep_ref, send_ref)


def call_kernel(kernel, out_shapes, scratch, flops, operands):
    vmem = pl.BlockSpec(memory_space=pltpu.VMEM)
    specs = [pl.BlockSpec(memory_space=pltpu.SMEM)] + [vmem] * (len(operands) - 1)
    moved = sum(math.prod(o.shape) * o.dtype.itemsize for o in list(operands) + list(out_shapes))
    return pl.pallas_call(
        kernel,
        out_shape=out_shapes,
        in_specs=specs,
        out_specs=[vmem] * len(out_shapes),
        scratch_shapes=scratch,
        compiler_params=pltpu.CompilerParams(vmem_limit_bytes=32 * 1024 * 1024),
        cost_estimate=pl.CostEstimate(flops=flops, bytes_accessed=moved, transcendentals=0),
    )(*operands)


def plan_slots(image_id, devices):
    token_rows = image_id.shape[0]
    device = lax.axis_index("fsdp")
    ends = jnp.sum((image_id == image_id[0]).astype(jnp.int32))
    first, last = device == 0, device == devices - 1
    holds = first | (ends >= IMG // 2 + 1)
    start = jnp.where(first, 0, jnp.where(holds, ends - IMG, ends))
    stop = jnp.where(last, token_rows, token_rows + IMG)
    stop_one = jnp.where(holds, ends, jnp.minimum(ends + IMG, stop))
    next_centre = stop_one + IMG // 2
    has_next = (stop_one < stop) & (last | (next_centre < token_rows))
    stop_two = jnp.where(has_next, jnp.minimum(stop_one + IMG, stop), stop_one)
    zero = jnp.zeros((), jnp.int32)
    return jnp.stack(
        [
            start + HALO, stop_one - start, stop_one + HALO, stop_two - stop_one,
            device % CORES, device // (CORES * SQUARE), zero, zero,
        ]
    ).astype(jnp.int32)


def struct(shape, kind):
    return jax.ShapeDtypeStruct(shape, kind)


def shards(inputs, attn_blocks, mlp_blocks, image_id, bias_id, out_grad):
    token_rows = inputs.shape[0]
    devices = lax.axis_size("fsdp")
    chips, columns = groups_of(devices)
    depth = devices // (CORES * SQUARE)
    window = token_rows + 2 * HALO
    attn_flat = devices * attn_blocks.shape[1] // LANES
    mlp_flat = devices * mlp_blocks.shape[1] // LANES
    barrier = lax.optimization_barrier

    lane = jnp.arange(LANES, dtype=jnp.int32)
    classes = ((lane // HEADS)[None, :] == bias_id[:, None]) & (lane < NB * HEADS)[None, :]
    tokens = jnp.concatenate([inputs, out_grad, classes.astype(bf16)], axis=1)
    up = [(i, i + 1) for i in range(devices - 1)]
    down = [(i + 1, i) for i in range(devices - 1)]
    meta = plan_slots(image_id, devices)
    head = jnp.arange(8, dtype=jnp.int32)
    head_mask = ((lane % HEADS)[None, :] == head[:, None]) & (lane < NB * HEADS)[None, :]
    head_mask = head_mask.astype(f32)

    attn_column = gather_exchange(as_rows(attn_blocks), columns)
    before = lax.ppermute(tokens[token_rows - HALO :], "fsdp", up)
    after = lax.ppermute(tokens[:HALO], "fsdp", down)
    mlp_rows = as_rows(mlp_blocks)
    attn_column, before, after, meta, head_mask, mlp_rows = barrier(
        (attn_column, before, after, meta, head_mask, mlp_rows)
    )
    attn_mine = gather_exchange(attn_column, chips)
    mlp_parts = [mlp_rows] + [pass_column(mlp_rows, k, devices) for k in range(1, depth)]
    (mlp_spread,) = call_kernel(
        spread_kernel, [struct((SQUARE, depth) + mlp_rows.shape, bf16)], [], 10**6,
        [meta] + mlp_parts,
    )
    mlp_spread, attn_mine = barrier((mlp_spread, attn_mine))
    mlp_mine = exchange(mlp_spread, chips)
    attn_other = swap_cores(attn_mine, devices)
    mlp_other = swap_cores(mlp_mine, devices)

    (
        middle, cotangent, inputs_span, normed, qkv, probability, context, classes_span,
        w_qkv, w_out, gain,
    ) = call_kernel(
        attend_kernel,
        [
            struct((SPAN, D), f32),
            struct((SPAN, D), bf16),
            struct((SPAN, D), bf16),
            struct((SPAN, D), bf16),
            struct((SPAN, 3 * D), bf16),
            struct((2 * HEADS, SLOT, SLOT), bf16),
            struct((SPAN, D), bf16),
            struct((SPAN, LANES), bf16),
            struct((D, 3 * D), bf16),
            struct((D, D), bf16),
            struct((1, D), f32),
        ],
        [pltpu.VMEM((attn_flat, LANES), f32), pltpu.VMEM((window, WIDE), bf16)],
        5 * 10**9,
        [meta, before, tokens, after, head_mask, attn_mine, attn_other],
    )
    feed_blocks = struct((SQUARE, depth, mlp_rows.shape[0], LANES), bf16)
    output, grad_middle, feed_keep, feed_send = call_kernel(
        feed_kernel,
        [struct((window, D), bf16), struct((SPAN, D), f32), feed_blocks, feed_blocks],
        [
            pltpu.VMEM((mlp_flat + 8, LANES), f32),
            pltpu.VMEM((D, FF), bf16),
            pltpu.VMEM((FF, D), bf16),
            pltpu.VMEM((SPAN, D), bf16),
        ],
        9 * 10**9,
        [meta, middle, cotangent, mlp_mine, mlp_other],
    )
    feed_part = add_cores(feed_keep, feed_send, devices)
    grad_first, grad_w_out, grad_bias_out, grad_table, grad_context = call_kernel(
        attend_back_kernel,
        [
            struct((SLOT, 3 * D), bf16),
            struct((D, D), f32),
            struct((1, D), f32),
            struct((8, LANES), f32),
            struct((SPAN, D), bf16),
        ],
        [],
        4 * 10**9,
        [meta, grad_middle, qkv, probability, context, classes_span, w_out],
    )
    feed_part, grad_first = barrier((feed_part, grad_first))
    feed_part = exchange(feed_part, chips)
    attn_blocks_out = struct((SQUARE, depth, attn_column.shape[1], LANES), bf16)
    grad_inputs, attn_keep, attn_send = call_kernel(
        inputs_back_kernel,
        [struct((window, D), f32), attn_blocks_out, attn_blocks_out],
        [
            pltpu.VMEM((attn_flat + 8, LANES), f32),
            pltpu.VMEM((SLOT, 3 * D), bf16),
            pltpu.VMEM((SPAN, 3 * D), bf16),
        ],
        8 * 10**9,
        [
            meta, grad_middle, head_mask, inputs_span, normed, qkv, probability, classes_span,
            w_qkv, gain, grad_first, grad_w_out, grad_bias_out, grad_table, grad_context,
        ],
    )
    attn_part = add_cores(attn_keep, attn_send, devices)
    attn_part, feed_part = barrier((attn_part, feed_part))
    feed_sums = call_kernel(
        sum_chips_kernel, [struct(mlp_rows.shape, bf16)] * depth, [], 10**6, [meta, feed_part]
    )
    attn_part = exchange(attn_part, chips)
    feed_parts = [feed_sums[0]] + [
        pass_column(feed_sums[k], k, devices) for k in range(1, depth)
    ]
    feed_sum = sum(part.astype(f32) for part in feed_parts)
    attn_part = jnp.sum(attn_part.astype(f32), axis=0).astype(bf16)
    attn_sum = sum_exchange(attn_part, columns)
    edges = jnp.concatenate([output, grad_inputs.astype(bf16)], axis=1)
    from_next = lax.ppermute(edges[:HALO], "fsdp", down)
    from_last = lax.ppermute(edges[window - HALO :], "fsdp", up)
    gap = jnp.zeros((token_rows - HALO, 2 * D), bf16)
    extra = jnp.concatenate([from_last, gap]) + jnp.concatenate([gap, from_next])
    own = slice(HALO, HALO + token_rows)
    output = output[own] + extra[:, :D]
    grad_inputs = grad_inputs[own] + extra[:, D:].astype(f32)
    return (output, grad_inputs, as_block(attn_sum, attn_blocks), as_block(feed_sum, mlp_blocks))


def solution(mesh):
    return jax.shard_map(
        shards,
        mesh=mesh,
        in_specs=(
            P("fsdp", None),
            P("fsdp", None),
            P("fsdp", None),
            P("fsdp"),
            P("fsdp"),
            P("fsdp", None),
        ),
        out_specs=(P("fsdp", None), P("fsdp", None), P("fsdp", None), P("fsdp", None)),
        check_vma=False,
    )
```

```python
import functools
import math

import jax
import jax.numpy as jnp
from jax import lax
from jax.experimental import pallas as pl
from jax.experimental.pallas import tpu as pltpu
from jax.sharding import PartitionSpec as P

D = 384
FF = 1536
HEADS = 6
HEAD_DIM = 64
IMG = 197
NB = 16

LANES = 128
CORES = 2
SQUARE = 4
SLOT = 208
SPAN = 2 * SLOT
HALO = 112
WIDE = 2 * D + LANES
D_ROWS = D // LANES
FF_ROWS = FF // LANES
QKV_ROWS = 3 * D // LANES

GAIN_AT = 0
SHIFT_AT = D_ROWS
W_QKV_AT = 2 * D_ROWS
BIAS_QUERY_AT = W_QKV_AT + D * QKV_ROWS
BIAS_VALUE_AT = BIAS_QUERY_AT + D_ROWS
W_OUT_AT = BIAS_VALUE_AT + D_ROWS
BIAS_OUT_AT = W_OUT_AT + D * D_ROWS
TABLE_AT = BIAS_OUT_AT + D_ROWS
W_UP_AT = 2 * D_ROWS
BIAS_UP_AT = W_UP_AT + D * FF_ROWS
W_DOWN_AT = BIAS_UP_AT + FF_ROWS
BIAS_DOWN_AT = W_DOWN_AT + FF * D_ROWS
FEED_END = BIAS_DOWN_AT + D_ROWS

epsilon = 1e-06
score_scale = HEAD_DIM ** (-0.5)
masked_score = -1e30
f32 = jnp.float32
bf16 = jnp.bfloat16


def dot(left, right):
    return lax.dot_general(left, right, (((1,), (0,)), ((), ())), preferred_element_type=f32)


def dot_rows(left, right):
    return lax.dot_general(left, right, (((0,), (0,)), ((), ())), preferred_element_type=f32)


def dot_cols(left, right):
    return lax.dot_general(left, right, (((1,), (1,)), ((), ())), preferred_element_type=f32)


def pass_on(value, step, devices):
    return lax.ppermute(value, "fsdp", [(i, i ^ step) for i in range(devices)])


def pass_cores(value, devices):
    return pass_on(value, 1, devices)


def pass_chips(parts, devices):
    return [pass_on(part, q * CORES, devices) for q, part in enumerate(parts) if q]


def pass_layers(parts, devices):
    return [pass_on(part, k * CORES * SQUARE, devices) for k, part in enumerate(parts) if k]


def rounded(amount, step):
    return -(-amount // step) * step


def as_rows(block):
    rows = block.shape[1] // LANES
    return jnp.pad(block.reshape(rows, LANES), ((0, rounded(rows, 8) - rows), (0, 0)))


def as_block(part, like):
    width = like.shape[1]
    return part.astype(f32)[: width // LANES].reshape(1, width)


def block_row(meta_ref, step, spot, layer, rows):
    where = (meta_ref[5] ^ layer) * SQUARE + (meta_ref[6] ^ spot)
    return (where * CORES + (meta_ref[4] ^ step)) * rows


def lay_out_blocks(meta_ref, block_refs, flat_ref):
    depth, padded, lanes = block_refs[0].shape
    rows = flat_ref.shape[0] // (CORES * SQUARE * depth)
    for index, block_ref in enumerate(block_refs):
        step, spot = divmod(index, SQUARE)
        for layer in range(depth):
            base = block_row(meta_ref, step, spot, layer, rows)
            flat_ref[pl.ds(base, rows), :] = block_ref[layer].astype(f32)[:rows]


def cut_blocks(meta_ref, flat_ref, keep_ref, send_ref):
    spots, depth, padded, lanes = keep_ref.shape
    rows = flat_ref.shape[0] // (CORES * spots * depth)
    for step, out_ref in enumerate((keep_ref, send_ref)):
        for spot in range(spots):
            for layer in range(depth):
                base = block_row(meta_ref, step, spot, layer, rows)
                out_ref[spot, layer] = flat_ref[pl.ds(base, padded), :].astype(bf16)


def pack_kernel(*refs):
    for layer, part_ref in enumerate(refs[:-1]):
        refs[-1][layer] = part_ref[...]


def add_cores_kernel(keep_ref, other_ref, *out_refs):
    for spot, out_ref in enumerate(out_refs):
        total = keep_ref[spot].astype(f32) + other_ref[spot].astype(f32)
        out_ref[...] = total.astype(bf16)


def add_chips_kernel(*refs):
    parts = refs[:SQUARE]
    for layer, out_ref in enumerate(refs[SQUARE:]):
        total = parts[0][layer].astype(f32)
        for part_ref in parts[1:]:
            total = total + part_ref[layer].astype(f32)
        out_ref[...] = total.astype(bf16)


def read_vector(flat_ref, at, amount):
    return jnp.concatenate([flat_ref[at + i : at + i + 1] for i in range(amount)], axis=1)


def write_vector(flat_ref, at, amount, value):
    for i in range(amount):
        flat_ref[at + i : at + i + 1] = value[:, i * LANES : (i + 1) * LANES]


def read_matrix(flat_ref, at, height, amount, out_ref):
    for i in range(amount):
        chunk = flat_ref[pl.ds(at + i, height, stride=amount), :]
        out_ref[:, i * LANES : (i + 1) * LANES] = chunk.astype(bf16)


def normalise(values):
    average = jnp.mean(values, axis=-1, keepdims=True)
    centred = values - average
    variance = jnp.mean(centred * centred, axis=-1, keepdims=True)
    inverse = lax.rsqrt(variance + epsilon)
    return (centred * inverse, inverse)


def norm_back(grad, unit, inverse, gain):
    scaled = grad * gain
    first = jnp.mean(scaled, axis=-1, keepdims=True)
    second = jnp.mean(scaled * unit, axis=-1, keepdims=True)
    return inverse * (scaled - first - unit * second)


def slot_mask(meta_ref, window, by_column):
    shape = (window, SPAN) if by_column else (SPAN, window)
    spot = lax.broadcasted_iota(jnp.int32, shape, 0 if by_column else 1)
    row = lax.broadcasted_iota(jnp.int32, shape, 1 if by_column else 0)
    start = jnp.where(row < SLOT, meta_ref[0], meta_ref[2] - SLOT)
    limit = jnp.where(row < SLOT, meta_ref[1], meta_ref[3] + SLOT)
    return jnp.where((spot == row + start) & (row < limit), 1.0, 0.0).astype(bf16)


def head_lanes(half):
    lane = lax.broadcasted_iota(jnp.int32, (1, LANES), 1)
    return (lane < HEAD_DIM) if half == 0 else (lane >= HEAD_DIM)


def attend_kernel(
    meta_ref, before_ref, own_ref, after_ref, mask_ref,
    mine_0, mine_1, mine_2, mine_3, other_0, other_1, other_2, other_3,
    middle_ref, cotangent_ref, inputs_ref, normed_ref, qkv_ref, probability_ref,
    context_ref, classes_ref, w_qkv_ref, w_out_ref, gain_ref,
    flat_ref, window_ref,
):
    window = window_ref.shape[0]
    block_refs = (mine_0, mine_1, mine_2, mine_3, other_0, other_1, other_2, other_3)
    lay_out_blocks(meta_ref, block_refs, flat_ref)
    read_matrix(flat_ref, W_QKV_AT, D, QKV_ROWS, w_qkv_ref)
    read_matrix(flat_ref, W_OUT_AT, D, D_ROWS, w_out_ref)
    gain = read_vector(flat_ref, GAIN_AT, D_ROWS)
    shift = read_vector(flat_ref, SHIFT_AT, D_ROWS)
    gain_ref[...] = gain
    bias_query = read_vector(flat_ref, BIAS_QUERY_AT, D_ROWS)
    bias_value = read_vector(flat_ref, BIAS_VALUE_AT, D_ROWS)
    bias_out = read_vector(flat_ref, BIAS_OUT_AT, D_ROWS)
    table = (mask_ref[...] * flat_ref[TABLE_AT : TABLE_AT + 1]).astype(bf16)

    halo = before_ref.shape[0]
    own = own_ref.shape[0]
    window_ref[0:halo] = before_ref[...]
    window_ref[halo : halo + own] = own_ref[...]
    window_ref[halo + own : window] = after_ref[...]
    picked = dot(slot_mask(meta_ref, window, False), window_ref[...])
    inputs = picked[:, :D]
    inputs_ref[...] = inputs.astype(bf16)
    cotangent_ref[...] = picked[:, D : 2 * D].astype(bf16)
    classes_ref[...] = picked[:, 2 * D :].astype(bf16)

    unit, _ = normalise(inputs)
    normed_ref[...] = (unit * gain + shift).astype(bf16)
    normed = normed_ref[...]
    qkv_ref[:, :D] = (dot(normed, w_qkv_ref[:, :D]) + bias_query).astype(bf16)
    qkv_ref[:, D : 2 * D] = dot(normed, w_qkv_ref[:, D : 2 * D]).astype(bf16)
    qkv_ref[:, 2 * D :] = (dot(normed, w_qkv_ref[:, 2 * D :]) + bias_value).astype(bf16)

    for slot in range(2):
        rows = slice(slot * SLOT, (slot + 1) * SLOT)
        key = lax.broadcasted_iota(jnp.int32, (1, SLOT), 1)
        key_bias = dot_cols(table, classes_ref[rows])
        key_bias = jnp.where(key < meta_ref[2 * slot + 1], key_bias, masked_score)
        for pair in range(HEADS // 2):
            lanes = slice(pair * LANES, (pair + 1) * LANES)
            queries = qkv_ref[rows, lanes]
            keys = qkv_ref[rows, D + pair * LANES : D + (pair + 1) * LANES]
            values = qkv_ref[rows, 2 * D + pair * LANES : 2 * D + (pair + 1) * LANES]
            mixed = []
            for half in range(2):
                head = 2 * pair + half
                chosen = jnp.where(head_lanes(half), queries, jnp.zeros_like(queries))
                scores = dot_cols(chosen, keys) * score_scale + key_bias[head : head + 1]
                peak = jnp.max(scores, axis=-1, keepdims=True)
                weights = jnp.exp(scores - peak)
                total = jnp.sum(weights, axis=-1, keepdims=True)
                probability = (weights * (1.0 / total)).astype(bf16)
                probability_ref[slot * HEADS + head] = probability
                mixed.append(dot(probability, values))
            context_ref[rows, lanes] = jnp.where(head_lanes(0), mixed[0], mixed[1]).astype(bf16)
    middle_ref[...] = inputs + dot(context_ref[...], w_out_ref[...]) + bias_out


def feed_kernel(
    meta_ref, middle_ref, cotangent_ref,
    mine_0, mine_1, mine_2, mine_3, other_0, other_1, other_2, other_3,
    output_ref, grad_middle_ref, keep_ref, send_ref,
    flat_ref, w_up_ref, w_down_ref, normed_ref,
):
    window = output_ref.shape[0]
    block_refs = (mine_0, mine_1, mine_2, mine_3, other_0, other_1, other_2, other_3)
    lay_out_blocks(meta_ref, block_refs, flat_ref)
    read_matrix(flat_ref, W_UP_AT, D, FF_ROWS, w_up_ref)
    read_matrix(flat_ref, W_DOWN_AT, FF, D_ROWS, w_down_ref)
    gain = read_vector(flat_ref, GAIN_AT, D_ROWS)
    shift = read_vector(flat_ref, SHIFT_AT, D_ROWS)
    bias_up = read_vector(flat_ref, BIAS_UP_AT, FF_ROWS)
    bias_down = read_vector(flat_ref, BIAS_DOWN_AT, D_ROWS)

    middle = middle_ref[...]
    cotangent = cotangent_ref[...]
    unit, inverse = normalise(middle)
    normed_ref[...] = (unit * gain + shift).astype(bf16)
    normed = normed_ref[...]
    output = middle + bias_down
    grad = jnp.zeros((SPAN, D), f32)
    slope = math.sqrt(2.0 / math.pi)
    for step in range(FF // D):
        cols = slice(step * D, (step + 1) * D)
        w_up = w_up_ref[:, cols]
        w_down = w_down_ref[cols]
        hidden = dot(normed, w_up) + bias_up[:, cols]
        square = hidden * hidden
        bend = jnp.tanh(slope * hidden * (1.0 + 0.044715 * square))
        half = 0.5 * (1.0 + bend)
        active = (hidden * half).astype(bf16)
        steep = half + 0.5 * hidden * (1.0 - bend * bend) * (
            slope * (1.0 + (3 * 0.044715) * square)
        )
        grad_hidden_wide = dot_cols(cotangent, w_down) * steep
        grad_hidden = grad_hidden_wide.astype(bf16)
        output = output + dot(active, w_down)
        grad = grad + dot_cols(grad_hidden, w_up)
        grad_down = dot_rows(active, cotangent)
        grad_up = dot_rows(normed, grad_hidden)
        grad_bias = jnp.sum(grad_hidden.astype(f32), axis=0, keepdims=True)
        write_vector(flat_ref, BIAS_UP_AT + step * D_ROWS, D_ROWS, grad_bias)
        for i in range(D_ROWS):
            lanes = slice(i * LANES, (i + 1) * LANES)
            flat_ref[pl.ds(W_UP_AT + step * D_ROWS + i, D, stride=FF_ROWS), :] = grad_up[:, lanes]
            flat_ref[pl.ds(W_DOWN_AT + step * D * D_ROWS + i, D, stride=D_ROWS), :] = grad_down[
                :, lanes
            ]
    output_ref[...] = dot(slot_mask(meta_ref, window, True), output.astype(bf16)).astype(bf16)
    grad_output = cotangent.astype(f32)
    write_vector(flat_ref, GAIN_AT, D_ROWS, jnp.sum(grad * unit, axis=0, keepdims=True))
    write_vector(flat_ref, SHIFT_AT, D_ROWS, jnp.sum(grad, axis=0, keepdims=True))
    write_vector(flat_ref, BIAS_DOWN_AT, D_ROWS, jnp.sum(grad_output, axis=0, keepdims=True))
    flat_ref[FEED_END:] = jnp.zeros((flat_ref.shape[0] - FEED_END, LANES), f32)
    grad_middle_ref[...] = grad_output + norm_back(grad, unit, inverse, gain)
    cut_blocks(meta_ref, flat_ref, keep_ref, send_ref)


def slot_back(
    slot, qkv_ref, probability_ref, classes_ref, grad_context_ref, grad_qkv_ref
):
    rows = slice(slot * SLOT, (slot + 1) * SLOT)
    key_sums = []
    for pair in range(HEADS // 2):
        lanes = slice(pair * LANES, (pair + 1) * LANES)
        key_lanes = slice(D + pair * LANES, D + (pair + 1) * LANES)
        value_lanes = slice(2 * D + pair * LANES, 2 * D + (pair + 1) * LANES)
        queries = qkv_ref[rows, lanes]
        keys = qkv_ref[rows, key_lanes]
        values = qkv_ref[rows, value_lanes]
        grad_context = grad_context_ref[rows, lanes]
        parts = []
        for half in range(2):
            head = 2 * pair + half
            chosen = jnp.where(head_lanes(half), grad_context, jnp.zeros_like(grad_context))
            grad_probs = dot_cols(chosen, values)
            narrow = probability_ref[slot * HEADS + head]
            probability = narrow.astype(f32)
            weighted = probability * grad_probs
            grad_scores = weighted - probability * jnp.sum(weighted, axis=-1, keepdims=True)
            key_sums.append(jnp.sum(grad_scores, axis=0, keepdims=True))
            grad_raw = (grad_scores * score_scale).astype(bf16)
            parts.append(
                (dot(grad_raw, keys), dot_rows(grad_raw, queries), dot_rows(narrow, grad_context))
            )
        low = head_lanes(0)
        for where, first, second in zip((lanes, key_lanes, value_lanes), *parts):
            grad_qkv_ref[:, where] = jnp.where(low, first, second).astype(bf16)
    sums = jnp.concatenate(key_sums + [jnp.zeros((8 - HEADS, SLOT), f32)], axis=0)
    sums_high = sums.astype(bf16)
    sums_low = (sums - sums_high.astype(f32)).astype(bf16)
    classes = classes_ref[rows]
    return dot(sums_high, classes) + dot(sums_low, classes)


def attend_back_kernel(
    meta_ref, grad_middle_ref, qkv_ref, probability_ref, context_ref, classes_ref, w_out_ref,
    grad_qkv_ref, grad_w_out_ref, grad_bias_out_ref, grad_table_ref, grad_context_ref,
):
    grad_branch = grad_middle_ref[...].astype(bf16)
    grad_bias_out_ref[...] = jnp.sum(grad_branch.astype(f32), axis=0, keepdims=True)
    grad_w_out_ref[...] = dot_rows(context_ref[...], grad_branch)
    grad_context_ref[...] = dot_cols(grad_branch, w_out_ref[...]).astype(bf16)
    grad_table_ref[...] = slot_back(
        0, qkv_ref, probability_ref, classes_ref, grad_context_ref, grad_qkv_ref
    )


def inputs_back_kernel(
    meta_ref, grad_middle_ref, mask_ref, inputs_ref, normed_ref, qkv_ref, probability_ref,
    classes_ref, w_qkv_ref, gain_ref,
    grad_first_ref, grad_w_out_ref, grad_bias_out_ref, grad_table_ref, grad_context_ref,
    grad_inputs_ref, keep_ref, send_ref,
    flat_ref, grad_second_ref, grad_qkv_ref,
):
    window = grad_inputs_ref.shape[0]
    grad_table = grad_table_ref[...] + slot_back(
        1, qkv_ref, probability_ref, classes_ref, grad_context_ref, grad_second_ref
    )
    grad_qkv_ref[:SLOT] = grad_first_ref[...]
    grad_qkv_ref[SLOT:] = grad_second_ref[...]
    flat_ref[TABLE_AT:] = jnp.zeros((flat_ref.shape[0] - TABLE_AT, LANES), f32)
    flat_ref[TABLE_AT : TABLE_AT + 1] = jnp.sum(grad_table * mask_ref[...], axis=0, keepdims=True)
    write_vector(flat_ref, BIAS_OUT_AT, D_ROWS, grad_bias_out_ref[...])
    for i in range(D_ROWS):
        flat_ref[pl.ds(W_OUT_AT + i, D, stride=D_ROWS), :] = grad_w_out_ref[
            :, i * LANES : (i + 1) * LANES
        ]
    grad_qkv = grad_qkv_ref[...]
    column_sums = jnp.sum(grad_qkv.astype(f32), axis=0, keepdims=True)
    write_vector(flat_ref, BIAS_QUERY_AT, D_ROWS, column_sums[:, :D])
    write_vector(flat_ref, BIAS_VALUE_AT, D_ROWS, column_sums[:, 2 * D :])
    normed = normed_ref[...]
    for part in range(3):
        grad_w = dot_rows(normed, grad_qkv_ref[:, part * D : (part + 1) * D])
        for i in range(D_ROWS):
            flat_ref[pl.ds(W_QKV_AT + part * D_ROWS + i, D, stride=QKV_ROWS), :] = grad_w[
                :, i * LANES : (i + 1) * LANES
            ]
    grad_normed = dot_cols(grad_qkv, w_qkv_ref[...])
    gain = gain_ref[...]
    unit, inverse = normalise(inputs_ref[...].astype(f32))
    write_vector(flat_ref, GAIN_AT, D_ROWS, jnp.sum(grad_normed * unit, axis=0, keepdims=True))
    write_vector(flat_ref, SHIFT_AT, D_ROWS, jnp.sum(grad_normed, axis=0, keepdims=True))
    grad_inputs = grad_middle_ref[...] + norm_back(grad_normed, unit, inverse, gain)
    high = grad_inputs.astype(bf16)
    low_part = (grad_inputs - high.astype(f32)).astype(bf16)
    back = slot_mask(meta_ref, window, True)
    grad_inputs_ref[...] = dot(back, high) + dot(back, low_part)
    cut_blocks(meta_ref, flat_ref, keep_ref, send_ref)


def call_kernel(kernel, out_shapes, scratch, flops, operands):
    vmem = pl.BlockSpec(memory_space=pltpu.VMEM)
    smem = pl.BlockSpec(memory_space=pltpu.SMEM)
    specs = [smem if operand.dtype == jnp.int32 else vmem for operand in operands]
    moved = sum(math.prod(o.shape) * o.dtype.itemsize for o in list(operands) + list(out_shapes))
    return pl.pallas_call(
        kernel,
        out_shape=out_shapes,
        in_specs=specs,
        out_specs=[vmem] * len(out_shapes),
        scratch_shapes=scratch,
        compiler_params=pltpu.CompilerParams(vmem_limit_bytes=32 * 1024 * 1024),
        cost_estimate=pl.CostEstimate(flops=flops, bytes_accessed=moved, transcendentals=0),
    )(*operands)


def plan_slots(image_id, devices):
    token_rows = image_id.shape[0]
    device = lax.axis_index("fsdp")
    ends = jnp.sum((image_id == image_id[0]).astype(jnp.int32))
    first, last = device == 0, device == devices - 1
    holds = first | (ends >= IMG // 2 + 1)
    start = jnp.where(first, 0, jnp.where(holds, ends - IMG, ends))
    stop = jnp.where(last, token_rows, token_rows + IMG)
    stop_one = jnp.where(holds, ends, jnp.minimum(ends + IMG, stop))
    next_centre = stop_one + IMG // 2
    has_next = (stop_one < stop) & (last | (next_centre < token_rows))
    stop_two = jnp.where(has_next, jnp.minimum(stop_one + IMG, stop), stop_one)
    zero = jnp.zeros((), jnp.int32)
    return jnp.stack(
        [
            start + HALO, stop_one - start, stop_one + HALO, stop_two - stop_one,
            device % CORES, device // (CORES * SQUARE), (device // CORES) % SQUARE, zero,
        ]
    ).astype(jnp.int32)


def struct(shape, kind):
    return jax.ShapeDtypeStruct(shape, kind)


def gather_columns(rows, devices):
    depth = devices // (CORES * SQUARE)
    parts = [rows] + pass_layers([rows] * depth, devices)
    return call_kernel(pack_kernel, [struct((depth,) + rows.shape, bf16)], [], 10**6, parts)[0]


def gather_planes(column, devices):
    return [column] + pass_chips([column] * SQUARE, devices)


def add_cores(keep, send, devices):
    parts = [struct(keep.shape[1:], bf16)] * SQUARE
    return call_kernel(add_cores_kernel, parts, [], 10**6, [keep, pass_cores(send, devices)])


def add_chips(parts, passed):
    depth, padded, lanes = parts[0].shape
    sums = [struct((padded, lanes), bf16)] * depth
    return call_kernel(add_chips_kernel, sums, [], 10**6, [parts[0]] + passed)


def shards(inputs, attn_blocks, mlp_blocks, image_id, bias_id, out_grad):
    token_rows = inputs.shape[0]
    devices = lax.axis_size("fsdp")
    depth = devices // (CORES * SQUARE)
    window = token_rows + 2 * HALO
    attn_flat = devices * attn_blocks.shape[1] // LANES
    mlp_flat = devices * mlp_blocks.shape[1] // LANES
    barrier = lax.optimization_barrier

    lane = jnp.arange(LANES, dtype=jnp.int32)
    classes = ((lane // HEADS)[None, :] == bias_id[:, None]) & (lane < NB * HEADS)[None, :]
    tokens = jnp.concatenate([inputs, out_grad, classes.astype(bf16)], axis=1)
    up = [(i, i + 1) for i in range(devices - 1)]
    down = [(i + 1, i) for i in range(devices - 1)]
    meta = plan_slots(image_id, devices)
    head = jnp.arange(8, dtype=jnp.int32)
    head_mask = ((lane % HEADS)[None, :] == head[:, None]) & (lane < NB * HEADS)[None, :]
    head_mask = head_mask.astype(f32)

    attn_rows = as_rows(attn_blocks)
    mlp_rows = as_rows(mlp_blocks)
    attn_column = gather_columns(attn_rows, devices)
    before = lax.ppermute(tokens[token_rows - HALO :], "fsdp", up)
    after = lax.ppermute(tokens[:HALO], "fsdp", down)
    mlp_column = gather_columns(mlp_rows, devices)
    attn_mine = gather_planes(attn_column, devices)
    mlp_column, attn_mine, before, after, meta, head_mask = barrier(
        (mlp_column, attn_mine, before, after, meta, head_mask)
    )
    mlp_mine = gather_planes(mlp_column, devices)
    attn_other = [pass_cores(part, devices) for part in attn_mine]
    mlp_other = [pass_cores(part, devices) for part in mlp_mine]

    (
        middle, cotangent, inputs_span, normed, qkv, probability, context, classes_span,
        w_qkv, w_out, gain,
    ) = call_kernel(
        attend_kernel,
        [
            struct((SPAN, D), f32),
            struct((SPAN, D), bf16),
            struct((SPAN, D), bf16),
            struct((SPAN, D), bf16),
            struct((SPAN, 3 * D), bf16),
            struct((2 * HEADS, SLOT, SLOT), bf16),
            struct((SPAN, D), bf16),
            struct((SPAN, LANES), bf16),
            struct((D, 3 * D), bf16),
            struct((D, D), bf16),
            struct((1, D), f32),
        ],
        [pltpu.VMEM((attn_flat + 16, LANES), f32), pltpu.VMEM((window, WIDE), bf16)],
        5 * 10**9,
        [meta, before, tokens, after, head_mask] + attn_mine + attn_other,
    )
    feed_blocks = struct((SQUARE,) + mlp_column.shape, bf16)
    output, grad_middle, feed_keep, feed_send = call_kernel(
        feed_kernel,
        [struct((window, D), bf16), struct((SPAN, D), f32), feed_blocks, feed_blocks],
        [
            pltpu.VMEM((mlp_flat + 16, LANES), f32),
            pltpu.VMEM((D, FF), bf16),
            pltpu.VMEM((FF, D), bf16),
            pltpu.VMEM((SPAN, D), bf16),
        ],
        9 * 10**9,
        [meta, middle, cotangent] + mlp_mine + mlp_other,
    )
    feed_parts = add_cores(feed_keep, feed_send, devices)
    grad_first, grad_w_out, grad_bias_out, grad_table, grad_context = call_kernel(
        attend_back_kernel,
        [
            struct((SLOT, 3 * D), bf16),
            struct((D, D), f32),
            struct((1, D), f32),
            struct((8, LANES), f32),
            struct((SPAN, D), bf16),
        ],
        [],
        4 * 10**9,
        [meta, grad_middle, qkv, probability, context, classes_span, w_out],
    )
    feed_parts, grad_first = barrier((feed_parts, grad_first))
    feed_passed = pass_chips(feed_parts, devices)
    attn_blocks_out = struct((SQUARE,) + attn_column.shape, bf16)
    grad_inputs, attn_keep, attn_send = call_kernel(
        inputs_back_kernel,
        [struct((window, D), f32), attn_blocks_out, attn_blocks_out],
        [
            pltpu.VMEM((attn_flat + 16, LANES), f32),
            pltpu.VMEM((SLOT, 3 * D), bf16),
            pltpu.VMEM((SPAN, 3 * D), bf16),
        ],
        8 * 10**9,
        [
            meta, grad_middle, head_mask, inputs_span, normed, qkv, probability, classes_span,
            w_qkv, gain, grad_first, grad_w_out, grad_bias_out, grad_table, grad_context,
        ],
    )
    attn_parts = add_cores(attn_keep, attn_send, devices)
    attn_passed = pass_chips(attn_parts, devices)
    feed_sums = add_chips(feed_parts, feed_passed)
    feed_layers = [feed_sums[0]] + pass_layers(feed_sums, devices)
    attn_sums = add_chips(attn_parts, attn_passed)
    attn_layers = [attn_sums[0]] + pass_layers(attn_sums, devices)
    feed_sum = sum(part.astype(f32) for part in feed_layers)
    attn_sum = sum(part.astype(f32) for part in attn_layers)
    edges = jnp.concatenate([output, grad_inputs.astype(bf16)], axis=1)
    from_next = lax.ppermute(edges[:HALO], "fsdp", down)
    from_last = lax.ppermute(edges[window - HALO :], "fsdp", up)
    gap = jnp.zeros((token_rows - HALO, 2 * D), bf16)
    extra = jnp.concatenate([from_last, gap]) + jnp.concatenate([gap, from_next])
    own = slice(HALO, HALO + token_rows)
    output = output[own] + extra[:, :D]
    grad_inputs = grad_inputs[own] + extra[:, D:].astype(f32)
    return (output, grad_inputs, as_block(attn_sum, attn_blocks), as_block(feed_sum, mlp_blocks))


def solution(mesh):
    return jax.shard_map(
        shards,
        mesh=mesh,
        in_specs=(
            P("fsdp", None),
            P("fsdp", None),
            P("fsdp", None),
            P("fsdp"),
            P("fsdp"),
            P("fsdp", None),
        ),
        out_specs=(P("fsdp", None), P("fsdp", None), P("fsdp", None), P("fsdp", None)),
        check_vma=False,
    )
```

```python
import functools
import math

import jax
import jax.numpy as jnp
from jax import lax
from jax.experimental import pallas as pl
from jax.experimental.pallas import tpu as pltpu
from jax.sharding import PartitionSpec as P

D = 384
FF = 1536
HEADS = 6
HEAD_DIM = 64
IMG = 197
NB = 16

LANES = 128
CORES = 2
SQUARE = 4
SLOT = 208
SPAN = 2 * SLOT
HALO = 112
WIDE = 2 * D + LANES
D_ROWS = D // LANES
FF_ROWS = FF // LANES
QKV_ROWS = 3 * D // LANES

GAIN_AT = 0
SHIFT_AT = D_ROWS
W_QKV_AT = 2 * D_ROWS
BIAS_QUERY_AT = W_QKV_AT + D * QKV_ROWS
BIAS_VALUE_AT = BIAS_QUERY_AT + D_ROWS
W_OUT_AT = BIAS_VALUE_AT + D_ROWS
BIAS_OUT_AT = W_OUT_AT + D * D_ROWS
TABLE_AT = BIAS_OUT_AT + D_ROWS
W_UP_AT = 2 * D_ROWS
BIAS_UP_AT = W_UP_AT + D * FF_ROWS
W_DOWN_AT = BIAS_UP_AT + FF_ROWS
BIAS_DOWN_AT = W_DOWN_AT + FF * D_ROWS
FEED_END = BIAS_DOWN_AT + D_ROWS

epsilon = 1e-06
score_scale = HEAD_DIM ** (-0.5)
masked_score = -1e30
f32 = jnp.float32
bf16 = jnp.bfloat16


def dot(left, right):
    return lax.dot_general(left, right, (((1,), (0,)), ((), ())), preferred_element_type=f32)


def dot_rows(left, right):
    return lax.dot_general(left, right, (((0,), (0,)), ((), ())), preferred_element_type=f32)


def dot_cols(left, right):
    return lax.dot_general(left, right, (((1,), (1,)), ((), ())), preferred_element_type=f32)


def pass_on(value, step, devices):
    return lax.ppermute(value, "fsdp", [(i, i ^ step) for i in range(devices)])


def pass_cores(value, devices):
    return pass_on(value, 1, devices)


def pass_chips(parts, devices):
    return [pass_on(part, q * CORES, devices) for q, part in enumerate(parts) if q]


def pass_layers(parts, devices):
    return [pass_on(part, k * CORES * SQUARE, devices) for k, part in enumerate(parts) if k]


def rounded(amount, step):
    return -(-amount // step) * step


def as_rows(block):
    rows = block.shape[1] // LANES
    return jnp.pad(block.reshape(rows, LANES), ((0, rounded(rows, 8) - rows), (0, 0)))


def as_block(part, like):
    width = like.shape[1]
    return part.astype(f32)[: width // LANES].reshape(1, width)


def block_row(meta_ref, step, spot, layer, rows):
    where = (meta_ref[5] ^ layer) * SQUARE + (meta_ref[6] ^ spot)
    return (where * CORES + (meta_ref[4] ^ step)) * rows


def lay_out_blocks(meta_ref, mine_ref, other_ref, flat_ref):
    spots, depth, padded, lanes = mine_ref.shape
    rows = flat_ref.shape[0] // (CORES * spots * depth)
    for step, block_ref in enumerate((mine_ref, other_ref)):
        for spot in range(spots):
            for layer in range(depth):
                base = block_row(meta_ref, step, spot, layer, rows)
                flat_ref[pl.ds(base, rows), :] = block_ref[spot, layer].astype(f32)[:rows]


def cut_blocks(meta_ref, flat_ref, keep_ref, send_ref):
    spots, depth, padded, lanes = keep_ref.shape
    rows = flat_ref.shape[0] // (CORES * spots * depth)
    for step, out_ref in enumerate((keep_ref, send_ref)):
        for spot in range(spots):
            for layer in range(depth):
                base = block_row(meta_ref, step, spot, layer, rows)
                out_ref[spot, layer] = flat_ref[pl.ds(base, padded), :].astype(bf16)


def pack_kernel(*refs):
    for layer, part_ref in enumerate(refs[:-1]):
        refs[-1][layer] = part_ref[...]


def add_cores_kernel(keep_ref, other_ref, *out_refs):
    for spot, out_ref in enumerate(out_refs):
        total = keep_ref[spot].astype(f32) + other_ref[spot].astype(f32)
        out_ref[...] = total.astype(bf16)


def add_chips_kernel(*refs):
    parts = refs[:SQUARE]
    for layer, out_ref in enumerate(refs[SQUARE:]):
        total = parts[0][layer].astype(f32)
        for part_ref in parts[1:]:
            total = total + part_ref[layer].astype(f32)
        out_ref[...] = total.astype(bf16)


def read_vector(flat_ref, at, amount):
    return jnp.concatenate([flat_ref[at + i : at + i + 1] for i in range(amount)], axis=1)


def write_vector(flat_ref, at, amount, value):
    for i in range(amount):
        flat_ref[at + i : at + i + 1] = value[:, i * LANES : (i + 1) * LANES]


def read_matrix(flat_ref, at, height, amount, out_ref):
    for i in range(amount):
        chunk = flat_ref[pl.ds(at + i, height, stride=amount), :]
        out_ref[:, i * LANES : (i + 1) * LANES] = chunk.astype(bf16)


def normalise(values):
    average = jnp.mean(values, axis=-1, keepdims=True)
    centred = values - average
    variance = jnp.mean(centred * centred, axis=-1, keepdims=True)
    inverse = lax.rsqrt(variance + epsilon)
    return (centred * inverse, inverse)


def norm_back(grad, unit, inverse, gain):
    scaled = grad * gain
    first = jnp.mean(scaled, axis=-1, keepdims=True)
    second = jnp.mean(scaled * unit, axis=-1, keepdims=True)
    return inverse * (scaled - first - unit * second)


def slot_mask(meta_ref, window, by_column):
    shape = (window, SPAN) if by_column else (SPAN, window)
    spot = lax.broadcasted_iota(jnp.int32, shape, 0 if by_column else 1)
    row = lax.broadcasted_iota(jnp.int32, shape, 1 if by_column else 0)
    start = jnp.where(row < SLOT, meta_ref[0], meta_ref[2] - SLOT)
    limit = jnp.where(row < SLOT, meta_ref[1], meta_ref[3] + SLOT)
    return jnp.where((spot == row + start) & (row < limit), 1.0, 0.0).astype(bf16)


def head_lanes(half):
    lane = lax.broadcasted_iota(jnp.int32, (1, LANES), 1)
    return (lane < HEAD_DIM) if half == 0 else (lane >= HEAD_DIM)


def attend_kernel(
    meta_ref, before_ref, own_ref, after_ref, mask_ref,
    mine_ref, other_ref,
    middle_ref, cotangent_ref, inputs_ref, normed_ref, qkv_ref, probability_ref,
    context_ref, classes_ref, w_qkv_ref, w_out_ref, gain_ref,
    flat_ref, window_ref,
):
    window = window_ref.shape[0]
    lay_out_blocks(meta_ref, mine_ref, other_ref, flat_ref)
    read_matrix(flat_ref, W_QKV_AT, D, QKV_ROWS, w_qkv_ref)
    read_matrix(flat_ref, W_OUT_AT, D, D_ROWS, w_out_ref)
    gain = read_vector(flat_ref, GAIN_AT, D_ROWS)
    shift = read_vector(flat_ref, SHIFT_AT, D_ROWS)
    gain_ref[...] = gain
    bias_query = read_vector(flat_ref, BIAS_QUERY_AT, D_ROWS)
    bias_value = read_vector(flat_ref, BIAS_VALUE_AT, D_ROWS)
    bias_out = read_vector(flat_ref, BIAS_OUT_AT, D_ROWS)
    table = (mask_ref[...] * flat_ref[TABLE_AT : TABLE_AT + 1]).astype(bf16)

    halo = before_ref.shape[0]
    own = own_ref.shape[0]
    window_ref[0:halo] = before_ref[...]
    window_ref[halo : halo + own] = own_ref[...]
    window_ref[halo + own : window] = after_ref[...]
    picked = dot(slot_mask(meta_ref, window, False), window_ref[...])
    inputs = picked[:, :D]
    inputs_ref[...] = inputs.astype(bf16)
    cotangent_ref[...] = picked[:, D : 2 * D].astype(bf16)
    classes_ref[...] = picked[:, 2 * D :].astype(bf16)

    unit, _ = normalise(inputs)
    normed_ref[...] = (unit * gain + shift).astype(bf16)
    normed = normed_ref[...]
    qkv_ref[:, :D] = (dot(normed, w_qkv_ref[:, :D]) + bias_query).astype(bf16)
    qkv_ref[:, D : 2 * D] = dot(normed, w_qkv_ref[:, D : 2 * D]).astype(bf16)
    qkv_ref[:, 2 * D :] = (dot(normed, w_qkv_ref[:, 2 * D :]) + bias_value).astype(bf16)

    for slot in range(2):
        rows = slice(slot * SLOT, (slot + 1) * SLOT)
        key = lax.broadcasted_iota(jnp.int32, (1, SLOT), 1)
        key_bias = dot_cols(table, classes_ref[rows])
        key_bias = jnp.where(key < meta_ref[2 * slot + 1], key_bias, masked_score)
        for pair in range(HEADS // 2):
            lanes = slice(pair * LANES, (pair + 1) * LANES)
            queries = qkv_ref[rows, lanes]
            keys = qkv_ref[rows, D + pair * LANES : D + (pair + 1) * LANES]
            values = qkv_ref[rows, 2 * D + pair * LANES : 2 * D + (pair + 1) * LANES]
            mixed = []
            for half in range(2):
                head = 2 * pair + half
                chosen = jnp.where(head_lanes(half), queries, jnp.zeros_like(queries))
                scores = dot_cols(chosen, keys) * score_scale + key_bias[head : head + 1]
                peak = jnp.max(scores, axis=-1, keepdims=True)
                weights = jnp.exp(scores - peak)
                total = jnp.sum(weights, axis=-1, keepdims=True)
                probability = (weights * (1.0 / total)).astype(bf16)
                probability_ref[slot * HEADS + head] = probability
                mixed.append(dot(probability, values))
            context_ref[rows, lanes] = jnp.where(head_lanes(0), mixed[0], mixed[1]).astype(bf16)
    middle_ref[...] = inputs + dot(context_ref[...], w_out_ref[...]) + bias_out


def feed_kernel(
    meta_ref, middle_ref, cotangent_ref,
    mine_ref, other_ref,
    output_ref, grad_middle_ref, keep_ref, send_ref,
    flat_ref, w_up_ref, w_down_ref, normed_ref,
):
    window = output_ref.shape[0]
    lay_out_blocks(meta_ref, mine_ref, other_ref, flat_ref)
    read_matrix(flat_ref, W_UP_AT, D, FF_ROWS, w_up_ref)
    read_matrix(flat_ref, W_DOWN_AT, FF, D_ROWS, w_down_ref)
    gain = read_vector(flat_ref, GAIN_AT, D_ROWS)
    shift = read_vector(flat_ref, SHIFT_AT, D_ROWS)
    bias_up = read_vector(flat_ref, BIAS_UP_AT, FF_ROWS)
    bias_down = read_vector(flat_ref, BIAS_DOWN_AT, D_ROWS)

    middle = middle_ref[...]
    cotangent = cotangent_ref[...]
    unit, inverse = normalise(middle)
    normed_ref[...] = (unit * gain + shift).astype(bf16)
    normed = normed_ref[...]
    output = middle + bias_down
    grad = jnp.zeros((SPAN, D), f32)
    slope = math.sqrt(2.0 / math.pi)
    for step in range(FF // D):
        cols = slice(step * D, (step + 1) * D)
        w_up = w_up_ref[:, cols]
        w_down = w_down_ref[cols]
        hidden = dot(normed, w_up) + bias_up[:, cols]
        square = hidden * hidden
        bend = jnp.tanh(slope * hidden * (1.0 + 0.044715 * square))
        half = 0.5 * (1.0 + bend)
        active = (hidden * half).astype(bf16)
        steep = half + 0.5 * hidden * (1.0 - bend * bend) * (
            slope * (1.0 + (3 * 0.044715) * square)
        )
        grad_hidden_wide = dot_cols(cotangent, w_down) * steep
        grad_hidden = grad_hidden_wide.astype(bf16)
        output = output + dot(active, w_down)
        grad = grad + dot_cols(grad_hidden, w_up)
        grad_down = dot_rows(active, cotangent)
        grad_up = dot_rows(normed, grad_hidden)
        grad_bias = jnp.sum(grad_hidden.astype(f32), axis=0, keepdims=True)
        write_vector(flat_ref, BIAS_UP_AT + step * D_ROWS, D_ROWS, grad_bias)
        for i in range(D_ROWS):
            lanes = slice(i * LANES, (i + 1) * LANES)
            flat_ref[pl.ds(W_UP_AT + step * D_ROWS + i, D, stride=FF_ROWS), :] = grad_up[:, lanes]
            flat_ref[pl.ds(W_DOWN_AT + step * D * D_ROWS + i, D, stride=D_ROWS), :] = grad_down[
                :, lanes
            ]
    output_ref[...] = dot(slot_mask(meta_ref, window, True), output.astype(bf16)).astype(bf16)
    grad_output = cotangent.astype(f32)
    write_vector(flat_ref, GAIN_AT, D_ROWS, jnp.sum(grad * unit, axis=0, keepdims=True))
    write_vector(flat_ref, SHIFT_AT, D_ROWS, jnp.sum(grad, axis=0, keepdims=True))
    write_vector(flat_ref, BIAS_DOWN_AT, D_ROWS, jnp.sum(grad_output, axis=0, keepdims=True))
    flat_ref[FEED_END:] = jnp.zeros((flat_ref.shape[0] - FEED_END, LANES), f32)
    grad_middle_ref[...] = grad_output + norm_back(grad, unit, inverse, gain)
    cut_blocks(meta_ref, flat_ref, keep_ref, send_ref)


def slot_back(
    slot, qkv_ref, probability_ref, classes_ref, grad_context_ref, grad_qkv_ref
):
    rows = slice(slot * SLOT, (slot + 1) * SLOT)
    key_sums = []
    for pair in range(HEADS // 2):
        lanes = slice(pair * LANES, (pair + 1) * LANES)
        key_lanes = slice(D + pair * LANES, D + (pair + 1) * LANES)
        value_lanes = slice(2 * D + pair * LANES, 2 * D + (pair + 1) * LANES)
        queries = qkv_ref[rows, lanes]
        keys = qkv_ref[rows, key_lanes]
        values = qkv_ref[rows, value_lanes]
        grad_context = grad_context_ref[rows, lanes]
        parts = []
        for half in range(2):
            head = 2 * pair + half
            chosen = jnp.where(head_lanes(half), grad_context, jnp.zeros_like(grad_context))
            grad_probs = dot_cols(chosen, values)
            narrow = probability_ref[slot * HEADS + head]
            probability = narrow.astype(f32)
            weighted = probability * grad_probs
            grad_scores = weighted - probability * jnp.sum(weighted, axis=-1, keepdims=True)
            key_sums.append(jnp.sum(grad_scores, axis=0, keepdims=True))
            grad_raw = (grad_scores * score_scale).astype(bf16)
            parts.append(
                (dot(grad_raw, keys), dot_rows(grad_raw, queries), dot_rows(narrow, grad_context))
            )
        low = head_lanes(0)
        for where, first, second in zip((lanes, key_lanes, value_lanes), *parts):
            grad_qkv_ref[:, where] = jnp.where(low, first, second).astype(bf16)
    sums = jnp.concatenate(key_sums + [jnp.zeros((8 - HEADS, SLOT), f32)], axis=0)
    sums_high = sums.astype(bf16)
    sums_low = (sums - sums_high.astype(f32)).astype(bf16)
    classes = classes_ref[rows]
    return dot(sums_high, classes) + dot(sums_low, classes)


def attend_back_kernel(
    meta_ref, grad_middle_ref, qkv_ref, probability_ref, context_ref, classes_ref, w_out_ref,
    grad_qkv_ref, grad_w_out_ref, grad_bias_out_ref, grad_table_ref, grad_context_ref,
):
    grad_branch = grad_middle_ref[...].astype(bf16)
    grad_bias_out_ref[...] = jnp.sum(grad_branch.astype(f32), axis=0, keepdims=True)
    grad_w_out_ref[...] = dot_rows(context_ref[...], grad_branch)
    grad_context_ref[...] = dot_cols(grad_branch, w_out_ref[...]).astype(bf16)
    grad_table_ref[...] = slot_back(
        0, qkv_ref, probability_ref, classes_ref, grad_context_ref, grad_qkv_ref
    )


def inputs_back_kernel(
    meta_ref, grad_middle_ref, mask_ref, inputs_ref, normed_ref, qkv_ref, probability_ref,
    classes_ref, w_qkv_ref, gain_ref,
    grad_first_ref, grad_w_out_ref, grad_bias_out_ref, grad_table_ref, grad_context_ref,
    grad_inputs_ref, keep_ref, send_ref,
    flat_ref, grad_second_ref, grad_qkv_ref,
):
    window = grad_inputs_ref.shape[0]
    grad_table = grad_table_ref[...] + slot_back(
        1, qkv_ref, probability_ref, classes_ref, grad_context_ref, grad_second_ref
    )
    grad_qkv_ref[:SLOT] = grad_first_ref[...]
    grad_qkv_ref[SLOT:] = grad_second_ref[...]
    flat_ref[TABLE_AT:] = jnp.zeros((flat_ref.shape[0] - TABLE_AT, LANES), f32)
    flat_ref[TABLE_AT : TABLE_AT + 1] = jnp.sum(grad_table * mask_ref[...], axis=0, keepdims=True)
    write_vector(flat_ref, BIAS_OUT_AT, D_ROWS, grad_bias_out_ref[...])
    for i in range(D_ROWS):
        flat_ref[pl.ds(W_OUT_AT + i, D, stride=D_ROWS), :] = grad_w_out_ref[
            :, i * LANES : (i + 1) * LANES
        ]
    grad_qkv = grad_qkv_ref[...]
    column_sums = jnp.sum(grad_qkv.astype(f32), axis=0, keepdims=True)
    write_vector(flat_ref, BIAS_QUERY_AT, D_ROWS, column_sums[:, :D])
    write_vector(flat_ref, BIAS_VALUE_AT, D_ROWS, column_sums[:, 2 * D :])
    normed = normed_ref[...]
    for part in range(3):
        grad_w = dot_rows(normed, grad_qkv_ref[:, part * D : (part + 1) * D])
        for i in range(D_ROWS):
            flat_ref[pl.ds(W_QKV_AT + part * D_ROWS + i, D, stride=QKV_ROWS), :] = grad_w[
                :, i * LANES : (i + 1) * LANES
            ]
    grad_normed = dot_cols(grad_qkv, w_qkv_ref[...])
    gain = gain_ref[...]
    unit, inverse = normalise(inputs_ref[...].astype(f32))
    write_vector(flat_ref, GAIN_AT, D_ROWS, jnp.sum(grad_normed * unit, axis=0, keepdims=True))
    write_vector(flat_ref, SHIFT_AT, D_ROWS, jnp.sum(grad_normed, axis=0, keepdims=True))
    grad_inputs = grad_middle_ref[...] + norm_back(grad_normed, unit, inverse, gain)
    high = grad_inputs.astype(bf16)
    low_part = (grad_inputs - high.astype(f32)).astype(bf16)
    back = slot_mask(meta_ref, window, True)
    grad_inputs_ref[...] = dot(back, high) + dot(back, low_part)
    cut_blocks(meta_ref, flat_ref, keep_ref, send_ref)


def call_kernel(kernel, out_shapes, scratch, flops, operands):
    vmem = pl.BlockSpec(memory_space=pltpu.VMEM)
    smem = pl.BlockSpec(memory_space=pltpu.SMEM)
    specs = [smem if operand.dtype == jnp.int32 else vmem for operand in operands]
    return pl.pallas_call(
        kernel,
        out_shape=out_shapes,
        in_specs=specs,
        out_specs=[vmem] * len(out_shapes),
        scratch_shapes=scratch,
        compiler_params=pltpu.CompilerParams(vmem_limit_bytes=32 * 1024 * 1024),
        cost_estimate=pl.CostEstimate(flops=flops, bytes_accessed=1, transcendentals=0),
    )(*operands)


def plan_slots(image_id, devices):
    token_rows = image_id.shape[0]
    device = lax.axis_index("fsdp")
    ends = jnp.sum((image_id == image_id[0]).astype(jnp.int32))
    first, last = device == 0, device == devices - 1
    holds = first | (ends >= IMG // 2 + 1)
    start = jnp.where(first, 0, jnp.where(holds, ends - IMG, ends))
    stop = jnp.where(last, token_rows, token_rows + IMG)
    stop_one = jnp.where(holds, ends, jnp.minimum(ends + IMG, stop))
    next_centre = stop_one + IMG // 2
    has_next = (stop_one < stop) & (last | (next_centre < token_rows))
    stop_two = jnp.where(has_next, jnp.minimum(stop_one + IMG, stop), stop_one)
    zero = jnp.zeros((), jnp.int32)
    return jnp.stack(
        [
            start + HALO, stop_one - start, stop_one + HALO, stop_two - stop_one,
            device % CORES, device // (CORES * SQUARE), (device // CORES) % SQUARE, zero,
        ]
    ).astype(jnp.int32)


def struct(shape, kind):
    return jax.ShapeDtypeStruct(shape, kind)


def pack(parts):
    packed = struct((len(parts),) + parts[0].shape, bf16)
    return call_kernel(pack_kernel, [packed], [], 1, parts)[0]


def gather_columns(rows, devices):
    depth = devices // (CORES * SQUARE)
    return pack([rows] + pass_layers([rows] * depth, devices))


def gather_planes(column, devices):
    return pack([column] + pass_chips([column] * SQUARE, devices))


def add_cores(keep, send, devices):
    parts = [struct(keep.shape[1:], bf16)] * SQUARE
    return call_kernel(add_cores_kernel, parts, [], 1, [keep, pass_cores(send, devices)])


def add_chips(parts, passed):
    depth, padded, lanes = parts[0].shape
    sums = [struct((padded, lanes), bf16)] * depth
    return call_kernel(add_chips_kernel, sums, [], 1, [parts[0]] + passed)


def shards(inputs, attn_blocks, mlp_blocks, image_id, bias_id, out_grad):
    token_rows = inputs.shape[0]
    devices = lax.axis_size("fsdp")
    depth = devices // (CORES * SQUARE)
    window = token_rows + 2 * HALO
    attn_flat = devices * attn_blocks.shape[1] // LANES
    mlp_flat = devices * mlp_blocks.shape[1] // LANES
    barrier = lax.optimization_barrier

    lane = jnp.arange(LANES, dtype=jnp.int32)
    classes = ((lane // HEADS)[None, :] == bias_id[:, None]) & (lane < NB * HEADS)[None, :]
    tokens = jnp.concatenate([inputs, out_grad, classes.astype(bf16)], axis=1)
    up = [(i, i + 1) for i in range(devices - 1)]
    down = [(i + 1, i) for i in range(devices - 1)]
    meta = plan_slots(image_id, devices)
    head = jnp.arange(8, dtype=jnp.int32)
    head_mask = ((lane % HEADS)[None, :] == head[:, None]) & (lane < NB * HEADS)[None, :]
    head_mask = head_mask.astype(f32)

    attn_rows = as_rows(attn_blocks)
    mlp_rows = as_rows(mlp_blocks)
    attn_column = gather_columns(attn_rows, devices)
    mlp_parts = pass_layers([mlp_rows] * depth, devices)
    attn_column, tokens = barrier((attn_column, tokens))
    before = lax.ppermute(tokens[token_rows - HALO :], "fsdp", up)
    after = lax.ppermute(tokens[:HALO], "fsdp", down)
    mlp_column = pack([mlp_rows] + mlp_parts)
    attn_mine = gather_planes(attn_column, devices)
    mlp_column, attn_mine, before, after, meta, head_mask = barrier(
        (mlp_column, attn_mine, before, after, meta, head_mask)
    )
    mlp_passed = pass_chips([mlp_column] * SQUARE, devices)
    attn_other = pass_cores(attn_mine, devices)

    (
        middle, cotangent, inputs_span, normed, qkv, probability, context, classes_span,
        w_qkv, w_out, gain,
    ) = call_kernel(
        attend_kernel,
        [
            struct((SPAN, D), f32),
            struct((SPAN, D), bf16),
            struct((SPAN, D), bf16),
            struct((SPAN, D), bf16),
            struct((SPAN, 3 * D), bf16),
            struct((2 * HEADS, SLOT, SLOT), bf16),
            struct((SPAN, D), bf16),
            struct((SPAN, LANES), bf16),
            struct((D, 3 * D), bf16),
            struct((D, D), bf16),
            struct((1, D), f32),
        ],
        [pltpu.VMEM((attn_flat + 16, LANES), f32), pltpu.VMEM((window, WIDE), bf16)],
        1,
        [meta, before, tokens, after, head_mask, attn_mine, attn_other],
    )
    mlp_passed, middle = barrier((mlp_passed, middle))
    mlp_mine = pack([mlp_column] + mlp_passed)
    mlp_other = pass_cores(mlp_mine, devices)
    feed_blocks = struct((SQUARE,) + mlp_column.shape, bf16)
    output, grad_middle, feed_keep, feed_send = call_kernel(
        feed_kernel,
        [struct((window, D), bf16), struct((SPAN, D), f32), feed_blocks, feed_blocks],
        [
            pltpu.VMEM((mlp_flat + 16, LANES), f32),
            pltpu.VMEM((D, FF), bf16),
            pltpu.VMEM((FF, D), bf16),
            pltpu.VMEM((SPAN, D), bf16),
        ],
        1,
        [meta, middle, cotangent, mlp_mine, mlp_other],
    )
    feed_parts = add_cores(feed_keep, feed_send, devices)
    grad_first, grad_w_out, grad_bias_out, grad_table, grad_context = call_kernel(
        attend_back_kernel,
        [
            struct((SLOT, 3 * D), bf16),
            struct((D, D), f32),
            struct((1, D), f32),
            struct((8, LANES), f32),
            struct((SPAN, D), bf16),
        ],
        [],
        1,
        [meta, grad_middle, qkv, probability, context, classes_span, w_out],
    )
    feed_parts, grad_first = barrier((feed_parts, grad_first))
    feed_passed = pass_chips(feed_parts, devices)
    attn_blocks_out = struct((SQUARE,) + attn_column.shape, bf16)
    grad_inputs, attn_keep, attn_send = call_kernel(
        inputs_back_kernel,
        [struct((window, D), f32), attn_blocks_out, attn_blocks_out],
        [
            pltpu.VMEM((attn_flat + 16, LANES), f32),
            pltpu.VMEM((SLOT, 3 * D), bf16),
            pltpu.VMEM((SPAN, 3 * D), bf16),
        ],
        1,
        [
            meta, grad_middle, head_mask, inputs_span, normed, qkv, probability, classes_span,
            w_qkv, gain, grad_first, grad_w_out, grad_bias_out, grad_table, grad_context,
        ],
    )
    edges = jnp.concatenate([output, grad_inputs.astype(bf16)], axis=1)
    from_next = lax.ppermute(edges[:HALO], "fsdp", down)
    from_last = lax.ppermute(edges[window - HALO :], "fsdp", up)
    attn_send, feed_passed, from_next, from_last = barrier(
        (attn_send, feed_passed, from_next, from_last)
    )
    attn_parts = list(add_cores(attn_keep, attn_send, devices))
    feed_sums = add_chips(feed_parts, feed_passed)
    feed_layers = [feed_sums[0]] + pass_layers(feed_sums, devices)
    attn_parts[-1], feed_layers[1] = barrier((attn_parts[-1], feed_layers[1]))
    attn_passed = pass_chips(attn_parts, devices)
    attn_sums = add_chips(attn_parts, attn_passed)
    attn_layers = [attn_sums[0]] + pass_layers(attn_sums, devices)
    feed_sum = sum(part.astype(f32) for part in feed_layers)
    attn_sum = sum(part.astype(f32) for part in attn_layers)
    gap = jnp.zeros((token_rows - HALO, 2 * D), bf16)
    extra = jnp.concatenate([from_last, gap]) + jnp.concatenate([gap, from_next])
    own = slice(HALO, HALO + token_rows)
    output = output[own] + extra[:, :D]
    grad_inputs = grad_inputs[own] + extra[:, D:].astype(f32)
    return (output, grad_inputs, as_block(attn_sum, attn_blocks), as_block(feed_sum, mlp_blocks))


def solution(mesh):
    return jax.shard_map(
        shards,
        mesh=mesh,
        in_specs=(
            P("fsdp", None),
            P("fsdp", None),
            P("fsdp", None),
            P("fsdp"),
            P("fsdp"),
            P("fsdp", None),
        ),
        out_specs=(P("fsdp", None), P("fsdp", None), P("fsdp", None), P("fsdp", None)),
        check_vma=False,
    )
```

```python
import functools
import math

import jax
import jax.numpy as jnp
from jax import lax
from jax.experimental import pallas as pl
from jax.experimental.pallas import tpu as pltpu
from jax.sharding import PartitionSpec as P

D = 384
FF = 1536
HEADS = 6
HEAD_DIM = 64
IMG = 197
NB = 16

LANES = 128
CORES = 2
SQUARE = 4
SLOT = 208
SPAN = 2 * SLOT
HALO = 112
WIDE = 2 * D + LANES
D_ROWS = D // LANES
FF_ROWS = FF // LANES
QKV_ROWS = 3 * D // LANES

GAIN_AT = 0
SHIFT_AT = D_ROWS
W_QKV_AT = 2 * D_ROWS
BIAS_QUERY_AT = W_QKV_AT + D * QKV_ROWS
BIAS_VALUE_AT = BIAS_QUERY_AT + D_ROWS
W_OUT_AT = BIAS_VALUE_AT + D_ROWS
BIAS_OUT_AT = W_OUT_AT + D * D_ROWS
TABLE_AT = BIAS_OUT_AT + D_ROWS
W_UP_AT = 2 * D_ROWS
BIAS_UP_AT = W_UP_AT + D * FF_ROWS
W_DOWN_AT = BIAS_UP_AT + FF_ROWS
BIAS_DOWN_AT = W_DOWN_AT + FF * D_ROWS
FEED_END = BIAS_DOWN_AT + D_ROWS

epsilon = 1e-06
score_scale = HEAD_DIM ** (-0.5)
masked_score = -1e30
f32 = jnp.float32
bf16 = jnp.bfloat16


def dot(left, right):
    return lax.dot_general(left, right, (((1,), (0,)), ((), ())), preferred_element_type=f32)


def dot_rows(left, right):
    return lax.dot_general(left, right, (((0,), (0,)), ((), ())), preferred_element_type=f32)


def dot_cols(left, right):
    return lax.dot_general(left, right, (((1,), (1,)), ((), ())), preferred_element_type=f32)


def pass_on(value, step, devices):
    return lax.ppermute(value, "fsdp", [(i, i ^ step) for i in range(devices)])


def pass_cores(value, devices):
    return pass_on(value, 1, devices)


def pass_chips(parts, devices):
    return [pass_on(part, q * CORES, devices) for q, part in enumerate(parts) if q]


def pass_layers(parts, devices):
    return [pass_on(part, k * CORES * SQUARE, devices) for k, part in enumerate(parts) if k]


def rounded(amount, step):
    return -(-amount // step) * step


def as_rows(block):
    rows = block.shape[1] // LANES
    return jnp.pad(block.reshape(rows, LANES), ((0, rounded(rows, 8) - rows), (0, 0)))


def as_block(part, like):
    width = like.shape[1]
    return part.astype(f32)[: width // LANES].reshape(1, width)


def block_row(meta_ref, step, spot, layer, rows):
    where = (meta_ref[5] ^ layer) * SQUARE + (meta_ref[6] ^ spot)
    return (where * CORES + (meta_ref[4] ^ step)) * rows


def lay_out_blocks(meta_ref, mine_ref, other_ref, flat_ref):
    spots, depth, padded, lanes = mine_ref.shape
    rows = flat_ref.shape[0] // (CORES * spots * depth)
    for step, block_ref in enumerate((mine_ref, other_ref)):
        for spot in range(spots):
            for layer in range(depth):
                base = block_row(meta_ref, step, spot, layer, rows)
                flat_ref[pl.ds(base, rows), :] = block_ref[spot, layer].astype(f32)[:rows]


def cut_blocks(meta_ref, flat_ref, keep_ref, send_ref):
    spots, depth, padded, lanes = keep_ref.shape
    rows = flat_ref.shape[0] // (CORES * spots * depth)
    for step, out_ref in enumerate((keep_ref, send_ref)):
        for spot in range(spots):
            for layer in range(depth):
                base = block_row(meta_ref, step, spot, layer, rows)
                out_ref[spot, layer] = flat_ref[pl.ds(base, padded), :].astype(bf16)


def pack_kernel(*refs):
    for layer, part_ref in enumerate(refs[:-1]):
        refs[-1][layer] = part_ref[...]


def add_cores_kernel(keep_ref, other_ref, *out_refs):
    for spot, out_ref in enumerate(out_refs):
        total = keep_ref[spot].astype(f32) + other_ref[spot].astype(f32)
        out_ref[...] = total.astype(bf16)


def add_chips_kernel(*refs):
    parts, (keep_ref, send_ref) = refs[:SQUARE], refs[SQUARE:]
    half = keep_ref.shape[0]
    for layer in range(2 * half):
        total = parts[0][layer].astype(f32)
        for part_ref in parts[1:]:
            total = total + part_ref[layer].astype(f32)
        if layer < half:
            keep_ref[layer] = total.astype(bf16)
        else:
            send_ref[layer - half] = total.astype(bf16)


def add_layers_kernel(keep_ref, other_ref, near_ref, send_ref):
    half = near_ref.shape[0]
    near_ref[...] = (keep_ref[:half].astype(f32) + other_ref[:half].astype(f32)).astype(bf16)
    send_ref[...] = (keep_ref[half:].astype(f32) + other_ref[half:].astype(f32)).astype(bf16)


def sixth(index):
    return (index * 43) >> 8


def head_mask():
    lane = lax.broadcasted_iota(jnp.int32, (8, LANES), 1)
    head = lax.broadcasted_iota(jnp.int32, (8, LANES), 0)
    inside = (lane - HEADS * sixth(lane) == head) & (lane < NB * HEADS)
    return jnp.where(inside, 1.0, 0.0)


def prepare_kernel(
    last_device, device_ref, image_ref, bias_ref, inputs_ref, out_grad_ref,
    tokens_ref, first_ref, last_ref, meta_ref,
):
    token_rows = inputs_ref.shape[0]
    tokens_ref[:, :D] = inputs_ref[...]
    tokens_ref[:, D : 2 * D] = out_grad_ref[...]
    entry = sixth(lax.broadcasted_iota(jnp.int32, (LANES, LANES), 0))
    inside = entry < NB
    for step in range(token_rows // LANES):
        same = inside & (entry == bias_ref[step : step + 1])
        classes = jnp.transpose(jnp.where(same, 1.0, 0.0))
        tokens_ref[step * LANES : (step + 1) * LANES, 2 * D :] = classes.astype(bf16)
    first_ref[...] = tokens_ref[:HALO]
    last_ref[...] = tokens_ref[token_rows - HALO :]
    images = image_ref[...]
    ends = jnp.sum(jnp.where(images == images[0:1, 0:1], 1, 0))
    device = device_ref[0]
    first, last = device == 0, device == last_device
    holds = first | (ends >= IMG // 2 + 1)
    start = jnp.where(first, 0, jnp.where(holds, ends - IMG, ends))
    stop = jnp.where(last, token_rows, token_rows + IMG)
    stop_one = jnp.where(holds, ends, jnp.minimum(ends + IMG, stop))
    has_next = (stop_one < stop) & (last | (stop_one + IMG // 2 < token_rows))
    stop_two = jnp.where(has_next, jnp.minimum(stop_one + IMG, stop), stop_one)
    meta_ref[0] = start + HALO
    meta_ref[1] = stop_one - start
    meta_ref[2] = stop_one + HALO
    meta_ref[3] = stop_two - stop_one
    meta_ref[4] = device & (CORES - 1)
    meta_ref[5] = device >> 3
    meta_ref[6] = (device >> 1) & (SQUARE - 1)
    meta_ref[7] = 0


def read_vector(flat_ref, at, amount):
    return jnp.concatenate([flat_ref[at + i : at + i + 1] for i in range(amount)], axis=1)


def write_vector(flat_ref, at, amount, value):
    for i in range(amount):
        flat_ref[at + i : at + i + 1] = value[:, i * LANES : (i + 1) * LANES]


def read_matrix(flat_ref, at, height, amount, out_ref):
    for i in range(amount):
        chunk = flat_ref[pl.ds(at + i, height, stride=amount), :]
        out_ref[:, i * LANES : (i + 1) * LANES] = chunk.astype(bf16)


def normalise(values):
    average = jnp.mean(values, axis=-1, keepdims=True)
    centred = values - average
    variance = jnp.mean(centred * centred, axis=-1, keepdims=True)
    inverse = lax.rsqrt(variance + epsilon)
    return (centred * inverse, inverse)


def norm_back(grad, unit, inverse, gain):
    scaled = grad * gain
    first = jnp.mean(scaled, axis=-1, keepdims=True)
    second = jnp.mean(scaled * unit, axis=-1, keepdims=True)
    return inverse * (scaled - first - unit * second)


def slot_mask(meta_ref, window, by_column):
    shape = (window, SPAN) if by_column else (SPAN, window)
    spot = lax.broadcasted_iota(jnp.int32, shape, 0 if by_column else 1)
    row = lax.broadcasted_iota(jnp.int32, shape, 1 if by_column else 0)
    start = jnp.where(row < SLOT, meta_ref[0], meta_ref[2] - SLOT)
    limit = jnp.where(row < SLOT, meta_ref[1], meta_ref[3] + SLOT)
    return jnp.where((spot == row + start) & (row < limit), 1.0, 0.0).astype(bf16)


def head_lanes(half):
    lane = lax.broadcasted_iota(jnp.int32, (1, LANES), 1)
    return (lane < HEAD_DIM) if half == 0 else (lane >= HEAD_DIM)


def attend_kernel(
    meta_ref, before_ref, own_ref, after_ref,
    mine_ref, other_ref,
    middle_ref, cotangent_ref, inputs_ref, normed_ref, qkv_ref, probability_ref,
    context_ref, classes_ref, w_qkv_ref, w_out_ref, gain_ref,
    flat_ref, window_ref,
):
    window = window_ref.shape[0]
    lay_out_blocks(meta_ref, mine_ref, other_ref, flat_ref)
    read_matrix(flat_ref, W_QKV_AT, D, QKV_ROWS, w_qkv_ref)
    read_matrix(flat_ref, W_OUT_AT, D, D_ROWS, w_out_ref)
    gain = read_vector(flat_ref, GAIN_AT, D_ROWS)
    shift = read_vector(flat_ref, SHIFT_AT, D_ROWS)
    gain_ref[...] = gain
    bias_query = read_vector(flat_ref, BIAS_QUERY_AT, D_ROWS)
    bias_value = read_vector(flat_ref, BIAS_VALUE_AT, D_ROWS)
    bias_out = read_vector(flat_ref, BIAS_OUT_AT, D_ROWS)
    table = (head_mask() * flat_ref[TABLE_AT : TABLE_AT + 1]).astype(bf16)

    halo = before_ref.shape[0]
    own = own_ref.shape[0]
    window_ref[0:halo] = before_ref[...]
    window_ref[halo : halo + own] = own_ref[...]
    window_ref[halo + own : window] = after_ref[...]
    picked = dot(slot_mask(meta_ref, window, False), window_ref[...])
    inputs = picked[:, :D]
    inputs_ref[...] = inputs.astype(bf16)
    cotangent_ref[...] = picked[:, D : 2 * D].astype(bf16)
    classes_ref[...] = picked[:, 2 * D :].astype(bf16)

    unit, _ = normalise(inputs)
    normed_ref[...] = (unit * gain + shift).astype(bf16)
    normed = normed_ref[...]
    qkv_ref[:, :D] = (dot(normed, w_qkv_ref[:, :D]) + bias_query).astype(bf16)
    qkv_ref[:, D : 2 * D] = dot(normed, w_qkv_ref[:, D : 2 * D]).astype(bf16)
    qkv_ref[:, 2 * D :] = (dot(normed, w_qkv_ref[:, 2 * D :]) + bias_value).astype(bf16)

    for slot in range(2):
        rows = slice(slot * SLOT, (slot + 1) * SLOT)
        key = lax.broadcasted_iota(jnp.int32, (1, SLOT), 1)
        key_bias = dot_cols(table, classes_ref[rows])
        key_bias = jnp.where(key < meta_ref[2 * slot + 1], key_bias, masked_score)
        for pair in range(HEADS // 2):
            lanes = slice(pair * LANES, (pair + 1) * LANES)
            queries = qkv_ref[rows, lanes]
            keys = qkv_ref[rows, D + pair * LANES : D + (pair + 1) * LANES]
            values = qkv_ref[rows, 2 * D + pair * LANES : 2 * D + (pair + 1) * LANES]
            mixed = []
            for half in range(2):
                head = 2 * pair + half
                chosen = jnp.where(head_lanes(half), queries, jnp.zeros_like(queries))
                scores = dot_cols(chosen, keys) * score_scale + key_bias[head : head + 1]
                peak = jnp.max(scores, axis=-1, keepdims=True)
                weights = jnp.exp(scores - peak)
                total = jnp.sum(weights, axis=-1, keepdims=True)
                probability = (weights * (1.0 / total)).astype(bf16)
                probability_ref[slot * HEADS + head] = probability
                mixed.append(dot(probability, values))
            context_ref[rows, lanes] = jnp.where(head_lanes(0), mixed[0], mixed[1]).astype(bf16)
    middle_ref[...] = inputs + dot(context_ref[...], w_out_ref[...]) + bias_out


def feed_kernel(
    meta_ref, middle_ref, cotangent_ref,
    mine_ref, other_ref,
    output_ref, grad_middle_ref, keep_ref, send_ref,
    flat_ref, w_up_ref, w_down_ref, normed_ref,
):
    window = output_ref.shape[0]
    lay_out_blocks(meta_ref, mine_ref, other_ref, flat_ref)
    read_matrix(flat_ref, W_UP_AT, D, FF_ROWS, w_up_ref)
    read_matrix(flat_ref, W_DOWN_AT, FF, D_ROWS, w_down_ref)
    gain = read_vector(flat_ref, GAIN_AT, D_ROWS)
    shift = read_vector(flat_ref, SHIFT_AT, D_ROWS)
    bias_up = read_vector(flat_ref, BIAS_UP_AT, FF_ROWS)
    bias_down = read_vector(flat_ref, BIAS_DOWN_AT, D_ROWS)

    middle = middle_ref[...]
    cotangent = cotangent_ref[...]
    unit, inverse = normalise(middle)
    normed_ref[...] = (unit * gain + shift).astype(bf16)
    normed = normed_ref[...]
    output = middle + bias_down
    grad = jnp.zeros((SPAN, D), f32)
    slope = math.sqrt(2.0 / math.pi)
    for step in range(FF // D):
        cols = slice(step * D, (step + 1) * D)
        w_up = w_up_ref[:, cols]
        w_down = w_down_ref[cols]
        hidden = dot(normed, w_up) + bias_up[:, cols]
        square = hidden * hidden
        bend = jnp.tanh(slope * hidden * (1.0 + 0.044715 * square))
        half = 0.5 * (1.0 + bend)
        active = (hidden * half).astype(bf16)
        steep = half + 0.5 * hidden * (1.0 - bend * bend) * (
            slope * (1.0 + (3 * 0.044715) * square)
        )
        grad_hidden_wide = dot_cols(cotangent, w_down) * steep
        grad_hidden = grad_hidden_wide.astype(bf16)
        output = output + dot(active, w_down)
        grad = grad + dot_cols(grad_hidden, w_up)
        grad_down = dot_rows(active, cotangent)
        grad_up = dot_rows(normed, grad_hidden)
        grad_bias = jnp.sum(grad_hidden.astype(f32), axis=0, keepdims=True)
        write_vector(flat_ref, BIAS_UP_AT + step * D_ROWS, D_ROWS, grad_bias)
        for i in range(D_ROWS):
            lanes = slice(i * LANES, (i + 1) * LANES)
            flat_ref[pl.ds(W_UP_AT + step * D_ROWS + i, D, stride=FF_ROWS), :] = grad_up[:, lanes]
            flat_ref[pl.ds(W_DOWN_AT + step * D * D_ROWS + i, D, stride=D_ROWS), :] = grad_down[
                :, lanes
            ]
    output_ref[...] = dot(slot_mask(meta_ref, window, True), output.astype(bf16)).astype(bf16)
    grad_output = cotangent.astype(f32)
    write_vector(flat_ref, GAIN_AT, D_ROWS, jnp.sum(grad * unit, axis=0, keepdims=True))
    write_vector(flat_ref, SHIFT_AT, D_ROWS, jnp.sum(grad, axis=0, keepdims=True))
    write_vector(flat_ref, BIAS_DOWN_AT, D_ROWS, jnp.sum(grad_output, axis=0, keepdims=True))
    flat_ref[FEED_END:] = jnp.zeros((flat_ref.shape[0] - FEED_END, LANES), f32)
    grad_middle_ref[...] = grad_output + norm_back(grad, unit, inverse, gain)
    cut_blocks(meta_ref, flat_ref, keep_ref, send_ref)


def slot_back(
    slot, qkv_ref, probability_ref, classes_ref, grad_context_ref, grad_qkv_ref
):
    rows = slice(slot * SLOT, (slot + 1) * SLOT)
    key_sums = []
    for pair in range(HEADS // 2):
        lanes = slice(pair * LANES, (pair + 1) * LANES)
        key_lanes = slice(D + pair * LANES, D + (pair + 1) * LANES)
        value_lanes = slice(2 * D + pair * LANES, 2 * D + (pair + 1) * LANES)
        queries = qkv_ref[rows, lanes]
        keys = qkv_ref[rows, key_lanes]
        values = qkv_ref[rows, value_lanes]
        grad_context = grad_context_ref[rows, lanes]
        parts = []
        for half in range(2):
            head = 2 * pair + half
            chosen = jnp.where(head_lanes(half), grad_context, jnp.zeros_like(grad_context))
            grad_probs = dot_cols(chosen, values)
            narrow = probability_ref[slot * HEADS + head]
            probability = narrow.astype(f32)
            weighted = probability * grad_probs
            grad_scores = weighted - probability * jnp.sum(weighted, axis=-1, keepdims=True)
            key_sums.append(jnp.sum(grad_scores, axis=0, keepdims=True))
            grad_raw = (grad_scores * score_scale).astype(bf16)
            parts.append(
                (dot(grad_raw, keys), dot_rows(grad_raw, queries), dot_rows(narrow, grad_context))
            )
        low = head_lanes(0)
        for where, first, second in zip((lanes, key_lanes, value_lanes), *parts):
            grad_qkv_ref[:, where] = jnp.where(low, first, second).astype(bf16)
    sums = jnp.concatenate(key_sums + [jnp.zeros((8 - HEADS, SLOT), f32)], axis=0)
    sums_high = sums.astype(bf16)
    sums_low = (sums - sums_high.astype(f32)).astype(bf16)
    classes = classes_ref[rows]
    return dot(sums_high, classes) + dot(sums_low, classes)


def attend_back_kernel(
    meta_ref, grad_middle_ref, qkv_ref, probability_ref, context_ref, classes_ref, w_out_ref,
    grad_qkv_ref, grad_w_out_ref, grad_bias_out_ref, grad_table_ref, grad_context_ref,
):
    grad_branch = grad_middle_ref[...].astype(bf16)
    grad_bias_out_ref[...] = jnp.sum(grad_branch.astype(f32), axis=0, keepdims=True)
    grad_w_out_ref[...] = dot_rows(context_ref[...], grad_branch)
    grad_context_ref[...] = dot_cols(grad_branch, w_out_ref[...]).astype(bf16)
    grad_table_ref[...] = slot_back(
        0, qkv_ref, probability_ref, classes_ref, grad_context_ref, grad_qkv_ref
    )


def inputs_back_kernel(
    meta_ref, grad_middle_ref, inputs_ref, normed_ref, qkv_ref, probability_ref,
    classes_ref, w_qkv_ref, gain_ref,
    grad_first_ref, grad_w_out_ref, grad_bias_out_ref, grad_table_ref, grad_context_ref,
    grad_inputs_ref, keep_ref, send_ref,
    flat_ref, grad_second_ref, grad_qkv_ref,
):
    window = grad_inputs_ref.shape[0]
    grad_table = grad_table_ref[...] + slot_back(
        1, qkv_ref, probability_ref, classes_ref, grad_context_ref, grad_second_ref
    )
    grad_qkv_ref[:SLOT] = grad_first_ref[...]
    grad_qkv_ref[SLOT:] = grad_second_ref[...]
    flat_ref[TABLE_AT:] = jnp.zeros((flat_ref.shape[0] - TABLE_AT, LANES), f32)
    flat_ref[TABLE_AT : TABLE_AT + 1] = jnp.sum(grad_table * head_mask(), axis=0, keepdims=True)
    write_vector(flat_ref, BIAS_OUT_AT, D_ROWS, grad_bias_out_ref[...])
    for i in range(D_ROWS):
        flat_ref[pl.ds(W_OUT_AT + i, D, stride=D_ROWS), :] = grad_w_out_ref[
            :, i * LANES : (i + 1) * LANES
        ]
    grad_qkv = grad_qkv_ref[...]
    column_sums = jnp.sum(grad_qkv.astype(f32), axis=0, keepdims=True)
    write_vector(flat_ref, BIAS_QUERY_AT, D_ROWS, column_sums[:, :D])
    write_vector(flat_ref, BIAS_VALUE_AT, D_ROWS, column_sums[:, 2 * D :])
    normed = normed_ref[...]
    for part in range(3):
        grad_w = dot_rows(normed, grad_qkv_ref[:, part * D : (part + 1) * D])
        for i in range(D_ROWS):
            flat_ref[pl.ds(W_QKV_AT + part * D_ROWS + i, D, stride=QKV_ROWS), :] = grad_w[
                :, i * LANES : (i + 1) * LANES
            ]
    grad_normed = dot_cols(grad_qkv, w_qkv_ref[...])
    gain = gain_ref[...]
    unit, inverse = normalise(inputs_ref[...].astype(f32))
    write_vector(flat_ref, GAIN_AT, D_ROWS, jnp.sum(grad_normed * unit, axis=0, keepdims=True))
    write_vector(flat_ref, SHIFT_AT, D_ROWS, jnp.sum(grad_normed, axis=0, keepdims=True))
    grad_inputs = grad_middle_ref[...] + norm_back(grad_normed, unit, inverse, gain)
    high = grad_inputs.astype(bf16)
    low_part = (grad_inputs - high.astype(f32)).astype(bf16)
    back = slot_mask(meta_ref, window, True)
    grad_inputs_ref[...] = dot(back, high) + dot(back, low_part)
    cut_blocks(meta_ref, flat_ref, keep_ref, send_ref)


def call_kernel(kernel, out_shapes, scratch, flops, operands):
    vmem = pl.BlockSpec(memory_space=pltpu.VMEM)
    smem = pl.BlockSpec(memory_space=pltpu.SMEM)
    specs = [smem if operand.dtype == jnp.int32 and operand.ndim == 1 else vmem for operand in operands]
    return pl.pallas_call(
        kernel,
        out_shape=out_shapes,
        in_specs=specs,
        out_specs=[smem if shape.dtype == jnp.int32 else vmem for shape in out_shapes],
        scratch_shapes=scratch,
        compiler_params=pltpu.CompilerParams(vmem_limit_bytes=32 * 1024 * 1024),
        cost_estimate=pl.CostEstimate(flops=flops, bytes_accessed=1, transcendentals=0),
    )(*operands)


def struct(shape, kind):
    return jax.ShapeDtypeStruct(shape, kind)


def pack(parts):
    packed = struct((len(parts),) + parts[0].shape, bf16)
    return call_kernel(pack_kernel, [packed], [], 1, parts)[0]


def gather_columns(rows, devices):
    depth = devices // (CORES * SQUARE)
    return pack([rows] + pass_layers([rows] * depth, devices))


def gather_planes(column, devices):
    return pack([column] + pass_chips([column] * SQUARE, devices))


def add_cores(keep, send, devices):
    parts = [struct(keep.shape[1:], bf16)] * SQUARE
    return call_kernel(add_cores_kernel, parts, [], 1, [keep, pass_cores(send, devices)])


def add_chips(parts, passed):
    depth, padded, lanes = parts[0].shape
    halves = [struct((depth // 2, padded, lanes), bf16)] * 2
    return call_kernel(add_chips_kernel, halves, [], 1, [parts[0]] + passed)


def add_layers(keep, send, devices):
    half, padded, lanes = keep.shape
    while half > 1:
        other = pass_on(send, half * CORES * SQUARE, devices)
        half //= 2
        halves = [struct((half, padded, lanes), bf16)] * 2
        keep, send = call_kernel(add_layers_kernel, halves, [], 1, [keep, other])
    other = pass_on(send, CORES * SQUARE, devices)
    return keep[0].astype(f32) + other[0].astype(f32)


def shards(inputs, attn_blocks, mlp_blocks, image_id, bias_id, out_grad):
    token_rows = inputs.shape[0]
    devices = lax.axis_size("fsdp")
    depth = devices // (CORES * SQUARE)
    window = token_rows + 2 * HALO
    attn_flat = devices * attn_blocks.shape[1] // LANES
    mlp_flat = devices * mlp_blocks.shape[1] // LANES
    barrier = lax.optimization_barrier

    up = [(i, i + 1) for i in range(devices - 1)]
    down = [(i + 1, i) for i in range(devices - 1)]
    tokens, first_rows, last_rows, meta = call_kernel(
        functools.partial(prepare_kernel, devices - 1),
        [
            struct((token_rows, WIDE), bf16),
            struct((HALO, WIDE), bf16),
            struct((HALO, WIDE), bf16),
            struct((8,), jnp.int32),
        ],
        [],
        1,
        [
            lax.axis_index("fsdp").astype(jnp.int32).reshape(1),
            image_id.reshape(-1, LANES),
            bias_id.reshape(-1, LANES),
            inputs,
            out_grad,
        ],
    )
    attn_rows = as_rows(attn_blocks)
    mlp_rows = as_rows(mlp_blocks)
    attn_column = gather_columns(attn_rows, devices)
    mlp_parts = pass_layers([mlp_rows] * depth, devices)
    attn_column, first_rows, last_rows = barrier((attn_column, first_rows, last_rows))
    before = lax.ppermute(last_rows, "fsdp", up)
    after = lax.ppermute(first_rows, "fsdp", down)
    mlp_column = pack([mlp_rows] + mlp_parts)
    attn_mine = gather_planes(attn_column, devices)
    mlp_column, attn_mine = barrier((mlp_column, attn_mine))
    mlp_passed = pass_chips([mlp_column] * SQUARE, devices)
    attn_other = pass_cores(attn_mine, devices)

    (
        middle, cotangent, inputs_span, normed, qkv, probability, context, classes_span,
        w_qkv, w_out, gain,
    ) = call_kernel(
        attend_kernel,
        [
            struct((SPAN, D), f32),
            struct((SPAN, D), bf16),
            struct((SPAN, D), bf16),
            struct((SPAN, D), bf16),
            struct((SPAN, 3 * D), bf16),
            struct((2 * HEADS, SLOT, SLOT), bf16),
            struct((SPAN, D), bf16),
            struct((SPAN, LANES), bf16),
            struct((D, 3 * D), bf16),
            struct((D, D), bf16),
            struct((1, D), f32),
        ],
        [pltpu.VMEM((attn_flat + 16, LANES), f32), pltpu.VMEM((window, WIDE), bf16)],
        1,
        [meta, before, tokens, after, attn_mine, attn_other],
    )
    mlp_passed, middle = barrier((mlp_passed, middle))
    mlp_mine = pack([mlp_column] + mlp_passed)
    mlp_other = pass_cores(mlp_mine, devices)
    feed_blocks = struct((SQUARE,) + mlp_column.shape, bf16)
    output, grad_middle, feed_keep, feed_send = call_kernel(
        feed_kernel,
        [struct((window, D), bf16), struct((SPAN, D), f32), feed_blocks, feed_blocks],
        [
            pltpu.VMEM((mlp_flat + 16, LANES), f32),
            pltpu.VMEM((D, FF), bf16),
            pltpu.VMEM((FF, D), bf16),
            pltpu.VMEM((SPAN, D), bf16),
        ],
        1,
        [meta, middle, cotangent, mlp_mine, mlp_other],
    )
    feed_parts = add_cores(feed_keep, feed_send, devices)
    grad_first, grad_w_out, grad_bias_out, grad_table, grad_context = call_kernel(
        attend_back_kernel,
        [
            struct((SLOT, 3 * D), bf16),
            struct((D, D), f32),
            struct((1, D), f32),
            struct((8, LANES), f32),
            struct((SPAN, D), bf16),
        ],
        [],
        1,
        [meta, grad_middle, qkv, probability, context, classes_span, w_out],
    )
    feed_parts, grad_first = barrier((feed_parts, grad_first))
    feed_passed = pass_chips(feed_parts, devices)
    attn_blocks_out = struct((SQUARE,) + attn_column.shape, bf16)
    grad_inputs, attn_keep, attn_send = call_kernel(
        inputs_back_kernel,
        [struct((window, D), f32), attn_blocks_out, attn_blocks_out],
        [
            pltpu.VMEM((attn_flat + 16, LANES), f32),
            pltpu.VMEM((SLOT, 3 * D), bf16),
            pltpu.VMEM((SPAN, 3 * D), bf16),
        ],
        1,
        [
            meta, grad_middle, inputs_span, normed, qkv, probability, classes_span,
            w_qkv, gain, grad_first, grad_w_out, grad_bias_out, grad_table, grad_context,
        ],
    )
    edges = jnp.concatenate([output, grad_inputs.astype(bf16)], axis=1)
    from_next = lax.ppermute(edges[:HALO], "fsdp", down)
    from_last = lax.ppermute(edges[window - HALO :], "fsdp", up)
    attn_send, feed_passed, from_next, from_last = barrier(
        (attn_send, feed_passed, from_next, from_last)
    )
    attn_parts = list(add_cores(attn_keep, attn_send, devices))
    feed_sum = add_layers(*add_chips(feed_parts, feed_passed), devices)
    attn_passed = pass_chips(attn_parts, devices)
    attn_sum = add_layers(*add_chips(attn_parts, attn_passed), devices)
    gap = jnp.zeros((token_rows - HALO, 2 * D), bf16)
    extra = jnp.concatenate([from_last, gap]) + jnp.concatenate([gap, from_next])
    own = slice(HALO, HALO + token_rows)
    output = output[own] + extra[:, :D]
    grad_inputs = grad_inputs[own] + extra[:, D:].astype(f32)
    return (output, grad_inputs, as_block(attn_sum, attn_blocks), as_block(feed_sum, mlp_blocks))


def solution(mesh):
    return jax.shard_map(
        shards,
        mesh=mesh,
        in_specs=(
            P("fsdp", None),
            P("fsdp", None),
            P("fsdp", None),
            P("fsdp"),
            P("fsdp"),
            P("fsdp", None),
        ),
        out_specs=(P("fsdp", None), P("fsdp", None), P("fsdp", None), P("fsdp", None)),
        check_vma=False,
    )
```

```python
import functools
import math

import jax
import jax.numpy as jnp
from jax import lax
from jax.experimental import pallas as pl
from jax.experimental.pallas import tpu as pltpu
from jax.sharding import PartitionSpec as P

D = 384
FF = 1536
HEADS = 6
HEAD_DIM = 64
IMG = 197
NB = 16

LANES = 128
CORES = 2
SQUARE = 4
SLOT = 208
SPAN = 2 * SLOT
HALO = 112
WIDE = 2 * D + LANES
D_ROWS = D // LANES
FF_ROWS = FF // LANES
QKV_ROWS = 3 * D // LANES

GAIN_AT = 0
SHIFT_AT = D_ROWS
W_QKV_AT = 2 * D_ROWS
BIAS_QUERY_AT = W_QKV_AT + D * QKV_ROWS
BIAS_VALUE_AT = BIAS_QUERY_AT + D_ROWS
W_OUT_AT = BIAS_VALUE_AT + D_ROWS
BIAS_OUT_AT = W_OUT_AT + D * D_ROWS
TABLE_AT = BIAS_OUT_AT + D_ROWS
W_UP_AT = 2 * D_ROWS
BIAS_UP_AT = W_UP_AT + D * FF_ROWS
W_DOWN_AT = BIAS_UP_AT + FF_ROWS
BIAS_DOWN_AT = W_DOWN_AT + FF * D_ROWS
FEED_END = BIAS_DOWN_AT + D_ROWS

epsilon = 1e-06
score_scale = HEAD_DIM ** (-0.5)
masked_score = -1e30
f32 = jnp.float32
bf16 = jnp.bfloat16


def dot(left, right):
    return lax.dot_general(left, right, (((1,), (0,)), ((), ())), preferred_element_type=f32)


def dot_rows(left, right):
    return lax.dot_general(left, right, (((0,), (0,)), ((), ())), preferred_element_type=f32)


def dot_cols(left, right):
    return lax.dot_general(left, right, (((1,), (1,)), ((), ())), preferred_element_type=f32)


def pass_on(value, step, devices):
    return lax.ppermute(value, "fsdp", [(i, i ^ step) for i in range(devices)])


def pass_cores(value, devices):
    return pass_on(value, 1, devices)


def pass_chips(parts, devices):
    return [pass_on(part, q * CORES, devices) for q, part in enumerate(parts) if q]


def pass_layers(parts, devices):
    return [pass_on(part, k * CORES * SQUARE, devices) for k, part in enumerate(parts) if k]


def rounded(amount, step):
    return -(-amount // step) * step


def as_rows(block):
    rows = block.shape[1] // LANES
    return jnp.pad(block.reshape(rows, LANES), ((0, rounded(rows, 8) - rows), (0, 0)))


def as_block(part, like):
    width = like.shape[1]
    return part.astype(f32)[: width // LANES].reshape(1, width)


def block_row(meta_ref, step, spot, layer, rows):
    where = (meta_ref[5] ^ layer) * SQUARE + (meta_ref[6] ^ spot)
    return (where * CORES + (meta_ref[4] ^ step)) * rows


def lay_out_blocks(meta_ref, mine_ref, other_ref, flat_ref):
    spots, depth, padded, lanes = mine_ref.shape
    rows = flat_ref.shape[0] // (CORES * spots * depth)
    for step, block_ref in enumerate((mine_ref, other_ref)):
        for spot in range(spots):
            for layer in range(depth):
                base = block_row(meta_ref, step, spot, layer, rows)
                flat_ref[pl.ds(base, rows), :] = block_ref[spot, layer].astype(f32)[:rows]


def cut_blocks(meta_ref, flat_ref, keep_ref, send_ref):
    spots, depth, padded, lanes = keep_ref.shape
    rows = flat_ref.shape[0] // (CORES * spots * depth)
    for step, out_ref in enumerate((keep_ref, send_ref)):
        for spot in range(spots):
            for layer in range(depth):
                base = block_row(meta_ref, step, spot, layer, rows)
                out_ref[spot, layer] = flat_ref[pl.ds(base, padded), :].astype(bf16)


def pack_kernel(*refs):
    for layer, part_ref in enumerate(refs[:-1]):
        refs[-1][layer] = part_ref[...]


def join_kernel(near_ref, far_ref, joined_ref):
    half = near_ref.shape[0]
    joined_ref[:half] = near_ref[...]
    joined_ref[half:] = far_ref[...]


def add_cores_kernel(keep_ref, other_ref, *out_refs):
    for spot, out_ref in enumerate(out_refs):
        total = keep_ref[spot].astype(f32) + other_ref[spot].astype(f32)
        out_ref[...] = total.astype(bf16)


def add_chips_kernel(*refs):
    parts, (keep_ref, send_ref) = refs[:SQUARE], refs[SQUARE:]
    half = keep_ref.shape[0]
    for layer in range(2 * half):
        total = parts[0][layer].astype(f32)
        for part_ref in parts[1:]:
            total = total + part_ref[layer].astype(f32)
        if layer < half:
            keep_ref[layer] = total.astype(bf16)
        else:
            send_ref[layer - half] = total.astype(bf16)


def add_layers_kernel(keep_ref, other_ref, near_ref, send_ref):
    half = near_ref.shape[0]
    near_ref[...] = (keep_ref[:half].astype(f32) + other_ref[:half].astype(f32)).astype(bf16)
    send_ref[...] = (keep_ref[half:].astype(f32) + other_ref[half:].astype(f32)).astype(bf16)


def sixth(index):
    return (index * 43) >> 8


def head_mask():
    lane = lax.broadcasted_iota(jnp.int32, (8, LANES), 1)
    head = lax.broadcasted_iota(jnp.int32, (8, LANES), 0)
    inside = (lane - HEADS * sixth(lane) == head) & (lane < NB * HEADS)
    return jnp.where(inside, 1.0, 0.0)


def edge_rows(core, near_core, last):
    return pl.ds(pl.multiple_of(jnp.where(core == near_core, last, 0), 16), HALO)


def prepare_kernel(
    last_device, device_ref, image_hbm, bias_hbm, inputs_hbm, out_grad_hbm,
    tokens_ref, inner_ref, outer_ref, meta_ref,
    image_ref, bias_ref, semaphores,
):
    token_rows = tokens_ref.shape[0]
    moves = [
        pltpu.make_async_copy(source, target, semaphores.at[step])
        for step, (source, target) in enumerate(
            [
                (bias_hbm, bias_ref),
                (image_hbm, image_ref),
                (inputs_hbm, tokens_ref.at[:, 0:D]),
                (out_grad_hbm, tokens_ref.at[:, D : 2 * D]),
            ]
        )
    ]
    for move in moves:
        move.start()
    entry = sixth(lax.broadcasted_iota(jnp.int32, (LANES, LANES), 0))
    inside = entry < NB
    moves[0].wait()
    for step in range(token_rows // LANES):
        same = inside & (entry == bias_ref[step : step + 1])
        classes = jnp.transpose(jnp.where(same, 1.0, 0.0))
        tokens_ref[step * LANES : (step + 1) * LANES, 2 * D :] = classes.astype(bf16)
    moves[1].wait()
    images = image_ref[...]
    ends = jnp.sum(jnp.where(images == images[0:1, 0:1], 1, 0))
    device = device_ref[0]
    first, last = device == 0, device == last_device
    holds = first | (ends >= IMG // 2 + 1)
    start = jnp.where(first, 0, jnp.where(holds, ends - IMG, ends))
    stop = jnp.where(last, token_rows, token_rows + IMG)
    stop_one = jnp.where(holds, ends, jnp.minimum(ends + IMG, stop))
    has_next = (stop_one < stop) & (last | (stop_one + IMG // 2 < token_rows))
    stop_two = jnp.where(has_next, jnp.minimum(stop_one + IMG, stop), stop_one)
    meta_ref[0] = start + HALO
    meta_ref[1] = stop_one - start
    meta_ref[2] = stop_one + HALO
    meta_ref[3] = stop_two - stop_one
    meta_ref[4] = device & (CORES - 1)
    meta_ref[5] = device >> 3
    meta_ref[6] = (device >> 1) & (SQUARE - 1)
    meta_ref[7] = 0
    moves[2].wait()
    moves[3].wait()
    core = device & (CORES - 1)
    inner_ref[...] = tokens_ref[edge_rows(core, 0, token_rows - HALO)]
    outer_ref[...] = tokens_ref[edge_rows(core, 1, token_rows - HALO)]


def read_vector(flat_ref, at, amount):
    return jnp.concatenate([flat_ref[at + i : at + i + 1] for i in range(amount)], axis=1)


def write_vector(flat_ref, at, amount, value):
    for i in range(amount):
        flat_ref[at + i : at + i + 1] = value[:, i * LANES : (i + 1) * LANES]


def read_matrix(flat_ref, at, height, amount, out_ref):
    for i in range(amount):
        chunk = flat_ref[pl.ds(at + i, height, stride=amount), :]
        out_ref[:, i * LANES : (i + 1) * LANES] = chunk.astype(bf16)


def normalise(values):
    average = jnp.mean(values, axis=-1, keepdims=True)
    centred = values - average
    variance = jnp.mean(centred * centred, axis=-1, keepdims=True)
    inverse = lax.rsqrt(variance + epsilon)
    return (centred * inverse, inverse)


def norm_back(grad, unit, inverse, gain):
    scaled = grad * gain
    first = jnp.mean(scaled, axis=-1, keepdims=True)
    second = jnp.mean(scaled * unit, axis=-1, keepdims=True)
    return inverse * (scaled - first - unit * second)


def slot_mask(meta_ref, window, by_column):
    shape = (window, SPAN) if by_column else (SPAN, window)
    spot = lax.broadcasted_iota(jnp.int32, shape, 0 if by_column else 1)
    row = lax.broadcasted_iota(jnp.int32, shape, 1 if by_column else 0)
    start = jnp.where(row < SLOT, meta_ref[0], meta_ref[2] - SLOT)
    limit = jnp.where(row < SLOT, meta_ref[1], meta_ref[3] + SLOT)
    return jnp.where((spot == row + start) & (row < limit), 1.0, 0.0).astype(bf16)


def head_lanes(half):
    lane = lax.broadcasted_iota(jnp.int32, (1, LANES), 1)
    return (lane < HEAD_DIM) if half == 0 else (lane >= HEAD_DIM)


def attend_kernel(
    meta_ref, inner_ref, own_ref, outer_ref,
    mine_ref, other_ref,
    middle_ref, cotangent_ref, inputs_ref, normed_ref, qkv_ref, probability_ref,
    context_ref, classes_ref, w_qkv_ref, w_out_ref, gain_ref,
    flat_ref, window_ref,
):
    window = window_ref.shape[0]
    lay_out_blocks(meta_ref, mine_ref, other_ref, flat_ref)
    read_matrix(flat_ref, W_QKV_AT, D, QKV_ROWS, w_qkv_ref)
    read_matrix(flat_ref, W_OUT_AT, D, D_ROWS, w_out_ref)
    gain = read_vector(flat_ref, GAIN_AT, D_ROWS)
    shift = read_vector(flat_ref, SHIFT_AT, D_ROWS)
    gain_ref[...] = gain
    bias_query = read_vector(flat_ref, BIAS_QUERY_AT, D_ROWS)
    bias_value = read_vector(flat_ref, BIAS_VALUE_AT, D_ROWS)
    bias_out = read_vector(flat_ref, BIAS_OUT_AT, D_ROWS)
    table = (head_mask() * flat_ref[TABLE_AT : TABLE_AT + 1]).astype(bf16)

    own = own_ref.shape[0]
    window_ref[edge_rows(meta_ref[4], 0, HALO + own)] = inner_ref[...]
    window_ref[HALO : HALO + own] = own_ref[...]
    window_ref[edge_rows(meta_ref[4], 1, HALO + own)] = outer_ref[...]
    picked = dot(slot_mask(meta_ref, window, False), window_ref[...])
    inputs = picked[:, :D]
    inputs_ref[...] = inputs.astype(bf16)
    cotangent_ref[...] = picked[:, D : 2 * D].astype(bf16)
    classes_ref[...] = picked[:, 2 * D :].astype(bf16)

    unit, _ = normalise(inputs)
    normed_ref[...] = (unit * gain + shift).astype(bf16)
    normed = normed_ref[...]
    qkv_ref[:, :D] = (dot(normed, w_qkv_ref[:, :D]) + bias_query).astype(bf16)
    qkv_ref[:, D : 2 * D] = dot(normed, w_qkv_ref[:, D : 2 * D]).astype(bf16)
    qkv_ref[:, 2 * D :] = (dot(normed, w_qkv_ref[:, 2 * D :]) + bias_value).astype(bf16)

    for slot in range(2):
        rows = slice(slot * SLOT, (slot + 1) * SLOT)
        key = lax.broadcasted_iota(jnp.int32, (1, SLOT), 1)
        key_bias = dot_cols(table, classes_ref[rows])
        key_bias = jnp.where(key < meta_ref[2 * slot + 1], key_bias, masked_score)
        for pair in range(HEADS // 2):
            lanes = slice(pair * LANES, (pair + 1) * LANES)
            queries = qkv_ref[rows, lanes]
            keys = qkv_ref[rows, D + pair * LANES : D + (pair + 1) * LANES]
            values = qkv_ref[rows, 2 * D + pair * LANES : 2 * D + (pair + 1) * LANES]
            mixed = []
            for half in range(2):
                head = 2 * pair + half
                chosen = jnp.where(head_lanes(half), queries, jnp.zeros_like(queries))
                scores = dot_cols(chosen, keys) * score_scale + key_bias[head : head + 1]
                peak = jnp.max(scores, axis=-1, keepdims=True)
                weights = jnp.exp(scores - peak)
                total = jnp.sum(weights, axis=-1, keepdims=True)
                probability = (weights * (1.0 / total)).astype(bf16)
                probability_ref[slot * HEADS + head] = probability
                mixed.append(dot(probability, values))
            context_ref[rows, lanes] = jnp.where(head_lanes(0), mixed[0], mixed[1]).astype(bf16)
    middle_ref[...] = inputs + dot(context_ref[...], w_out_ref[...]) + bias_out


def feed_kernel(
    meta_ref, middle_ref, cotangent_ref,
    mine_ref, other_ref,
    output_ref, grad_middle_ref, keep_ref, send_ref,
    flat_ref, w_up_ref, w_down_ref, normed_ref,
):
    window = output_ref.shape[0]
    lay_out_blocks(meta_ref, mine_ref, other_ref, flat_ref)
    read_matrix(flat_ref, W_UP_AT, D, FF_ROWS, w_up_ref)
    read_matrix(flat_ref, W_DOWN_AT, FF, D_ROWS, w_down_ref)
    gain = read_vector(flat_ref, GAIN_AT, D_ROWS)
    shift = read_vector(flat_ref, SHIFT_AT, D_ROWS)
    bias_up = read_vector(flat_ref, BIAS_UP_AT, FF_ROWS)
    bias_down = read_vector(flat_ref, BIAS_DOWN_AT, D_ROWS)

    middle = middle_ref[...]
    cotangent = cotangent_ref[...]
    unit, inverse = normalise(middle)
    normed_ref[...] = (unit * gain + shift).astype(bf16)
    normed = normed_ref[...]
    output = middle + bias_down
    grad = jnp.zeros((SPAN, D), f32)
    slope = math.sqrt(2.0 / math.pi)
    for step in range(FF // D):
        cols = slice(step * D, (step + 1) * D)
        w_up = w_up_ref[:, cols]
        w_down = w_down_ref[cols]
        hidden = dot(normed, w_up) + bias_up[:, cols]
        square = hidden * hidden
        bend = jnp.tanh(slope * hidden * (1.0 + 0.044715 * square))
        half = 0.5 * (1.0 + bend)
        active = (hidden * half).astype(bf16)
        steep = half + 0.5 * hidden * (1.0 - bend * bend) * (
            slope * (1.0 + (3 * 0.044715) * square)
        )
        grad_hidden_wide = dot_cols(cotangent, w_down) * steep
        grad_hidden = grad_hidden_wide.astype(bf16)
        output = output + dot(active, w_down)
        grad = grad + dot_cols(grad_hidden, w_up)
        grad_down = dot_rows(active, cotangent)
        grad_up = dot_rows(normed, grad_hidden)
        grad_bias = jnp.sum(grad_hidden.astype(f32), axis=0, keepdims=True)
        write_vector(flat_ref, BIAS_UP_AT + step * D_ROWS, D_ROWS, grad_bias)
        for i in range(D_ROWS):
            lanes = slice(i * LANES, (i + 1) * LANES)
            flat_ref[pl.ds(W_UP_AT + step * D_ROWS + i, D, stride=FF_ROWS), :] = grad_up[:, lanes]
            flat_ref[pl.ds(W_DOWN_AT + step * D * D_ROWS + i, D, stride=D_ROWS), :] = grad_down[
                :, lanes
            ]
    output_ref[...] = dot(slot_mask(meta_ref, window, True), output.astype(bf16)).astype(bf16)
    grad_output = cotangent.astype(f32)
    write_vector(flat_ref, GAIN_AT, D_ROWS, jnp.sum(grad * unit, axis=0, keepdims=True))
    write_vector(flat_ref, SHIFT_AT, D_ROWS, jnp.sum(grad, axis=0, keepdims=True))
    write_vector(flat_ref, BIAS_DOWN_AT, D_ROWS, jnp.sum(grad_output, axis=0, keepdims=True))
    flat_ref[FEED_END:] = jnp.zeros((flat_ref.shape[0] - FEED_END, LANES), f32)
    grad_middle_ref[...] = grad_output + norm_back(grad, unit, inverse, gain)
    cut_blocks(meta_ref, flat_ref, keep_ref, send_ref)


def slot_back(
    slot, qkv_ref, probability_ref, classes_ref, grad_context_ref, grad_qkv_ref
):
    rows = slice(slot * SLOT, (slot + 1) * SLOT)
    key_sums = []
    for pair in range(HEADS // 2):
        lanes = slice(pair * LANES, (pair + 1) * LANES)
        key_lanes = slice(D + pair * LANES, D + (pair + 1) * LANES)
        value_lanes = slice(2 * D + pair * LANES, 2 * D + (pair + 1) * LANES)
        queries = qkv_ref[rows, lanes]
        keys = qkv_ref[rows, key_lanes]
        values = qkv_ref[rows, value_lanes]
        grad_context = grad_context_ref[rows, lanes]
        parts = []
        for half in range(2):
            head = 2 * pair + half
            chosen = jnp.where(head_lanes(half), grad_context, jnp.zeros_like(grad_context))
            grad_probs = dot_cols(chosen, values)
            narrow = probability_ref[slot * HEADS + head]
            probability = narrow.astype(f32)
            weighted = probability * grad_probs
            grad_scores = weighted - probability * jnp.sum(weighted, axis=-1, keepdims=True)
            key_sums.append(jnp.sum(grad_scores, axis=0, keepdims=True))
            grad_raw = (grad_scores * score_scale).astype(bf16)
            parts.append(
                (dot(grad_raw, keys), dot_rows(grad_raw, queries), dot_rows(narrow, grad_context))
            )
        low = head_lanes(0)
        for where, first, second in zip((lanes, key_lanes, value_lanes), *parts):
            grad_qkv_ref[:, where] = jnp.where(low, first, second).astype(bf16)
    sums = jnp.concatenate(key_sums + [jnp.zeros((8 - HEADS, SLOT), f32)], axis=0)
    sums_high = sums.astype(bf16)
    sums_low = (sums - sums_high.astype(f32)).astype(bf16)
    classes = classes_ref[rows]
    return dot(sums_high, classes) + dot(sums_low, classes)


def attend_back_kernel(
    meta_ref, grad_middle_ref, qkv_ref, probability_ref, context_ref, classes_ref, w_out_ref,
    grad_qkv_ref, grad_w_out_ref, grad_bias_out_ref, grad_table_ref, grad_context_ref,
):
    grad_branch = grad_middle_ref[...].astype(bf16)
    grad_bias_out_ref[...] = jnp.sum(grad_branch.astype(f32), axis=0, keepdims=True)
    grad_w_out_ref[...] = dot_rows(context_ref[...], grad_branch)
    grad_context_ref[...] = dot_cols(grad_branch, w_out_ref[...]).astype(bf16)
    grad_table_ref[...] = slot_back(
        0, qkv_ref, probability_ref, classes_ref, grad_context_ref, grad_qkv_ref
    )


def inputs_back_kernel(
    meta_ref, grad_middle_ref, output_ref, inputs_ref, normed_ref, qkv_ref, probability_ref,
    classes_ref, w_qkv_ref, gain_ref,
    grad_first_ref, grad_w_out_ref, grad_bias_out_ref, grad_table_ref, grad_context_ref,
    own_output_ref, own_grad_ref, inner_ref, outer_ref, keep_ref, send_ref,
    flat_ref, grad_second_ref, grad_qkv_ref, grad_inputs_ref,
):
    window = grad_inputs_ref.shape[0]
    grad_table = grad_table_ref[...] + slot_back(
        1, qkv_ref, probability_ref, classes_ref, grad_context_ref, grad_second_ref
    )
    grad_qkv_ref[:SLOT] = grad_first_ref[...]
    grad_qkv_ref[SLOT:] = grad_second_ref[...]
    flat_ref[TABLE_AT:] = jnp.zeros((flat_ref.shape[0] - TABLE_AT, LANES), f32)
    flat_ref[TABLE_AT : TABLE_AT + 1] = jnp.sum(grad_table * head_mask(), axis=0, keepdims=True)
    write_vector(flat_ref, BIAS_OUT_AT, D_ROWS, grad_bias_out_ref[...])
    for i in range(D_ROWS):
        flat_ref[pl.ds(W_OUT_AT + i, D, stride=D_ROWS), :] = grad_w_out_ref[
            :, i * LANES : (i + 1) * LANES
        ]
    grad_qkv = grad_qkv_ref[...]
    column_sums = jnp.sum(grad_qkv.astype(f32), axis=0, keepdims=True)
    write_vector(flat_ref, BIAS_QUERY_AT, D_ROWS, column_sums[:, :D])
    write_vector(flat_ref, BIAS_VALUE_AT, D_ROWS, column_sums[:, 2 * D :])
    normed = normed_ref[...]
    for part in range(3):
        grad_w = dot_rows(normed, grad_qkv_ref[:, part * D : (part + 1) * D])
        for i in range(D_ROWS):
            flat_ref[pl.ds(W_QKV_AT + part * D_ROWS + i, D, stride=QKV_ROWS), :] = grad_w[
                :, i * LANES : (i + 1) * LANES
            ]
    grad_normed = dot_cols(grad_qkv, w_qkv_ref[...])
    gain = gain_ref[...]
    unit, inverse = normalise(inputs_ref[...].astype(f32))
    write_vector(flat_ref, GAIN_AT, D_ROWS, jnp.sum(grad_normed * unit, axis=0, keepdims=True))
    write_vector(flat_ref, SHIFT_AT, D_ROWS, jnp.sum(grad_normed, axis=0, keepdims=True))
    grad_inputs = grad_middle_ref[...] + norm_back(grad_normed, unit, inverse, gain)
    high = grad_inputs.astype(bf16)
    low_part = (grad_inputs - high.astype(f32)).astype(bf16)
    back = slot_mask(meta_ref, window, True)
    grad_inputs_ref[...] = dot(back, high) + dot(back, low_part)
    own = slice(HALO, window - HALO)
    own_output_ref[...] = output_ref[own]
    own_grad_ref[...] = grad_inputs_ref[own]
    for near_core, edge_ref in enumerate((inner_ref, outer_ref)):
        edge = edge_rows(meta_ref[4], near_core, window - HALO)
        edge_ref[:, :D] = output_ref[edge]
        edge_ref[:, D:] = grad_inputs_ref[edge].astype(bf16)
    cut_blocks(meta_ref, flat_ref, keep_ref, send_ref)


def combine_kernel(
    meta_ref, own_output_ref, own_grad_ref, inner_ref, outer_ref, output_ref, grad_inputs_ref
):
    last = output_ref.shape[0] - HALO
    output_ref[HALO:last] = own_output_ref[HALO:last]
    grad_inputs_ref[HALO:last] = own_grad_ref[HALO:last]
    for near_core, edge_ref in enumerate((inner_ref, outer_ref)):
        edge = edge_rows(meta_ref[4], near_core, last)
        output_ref[edge] = (
            own_output_ref[edge].astype(f32) + edge_ref[:, :D].astype(f32)
        ).astype(bf16)
        grad_inputs_ref[edge] = own_grad_ref[edge] + edge_ref[:, D:].astype(f32)


def call_kernel(kernel, out_shapes, scratch, flops, operands, far=(), room=32 * 1024 * 1024):
    vmem = pl.BlockSpec(memory_space=pltpu.VMEM)
    smem = pl.BlockSpec(memory_space=pltpu.SMEM)
    specs = [smem if operand.dtype == jnp.int32 else vmem for operand in operands]
    for index in far:
        specs[index] = pl.BlockSpec(memory_space=pltpu.HBM)
    return pl.pallas_call(
        kernel,
        out_shape=out_shapes,
        in_specs=specs,
        out_specs=[smem if shape.dtype == jnp.int32 else vmem for shape in out_shapes],
        scratch_shapes=scratch,
        compiler_params=pltpu.CompilerParams(vmem_limit_bytes=room),
        cost_estimate=pl.CostEstimate(flops=flops, bytes_accessed=1, transcendentals=0),
    )(*operands)


def struct(shape, kind):
    return jax.ShapeDtypeStruct(shape, kind)


def pack(parts):
    packed = struct((len(parts),) + parts[0].shape, bf16)
    return call_kernel(pack_kernel, [packed], [], 1, parts)[0]


def gather_columns(rows, devices):
    depth = devices // (CORES * SQUARE)
    return pack([rows] + pass_layers([rows] * depth, devices))


def double_column(column, devices):
    half = column.shape[0]
    far = pass_on(column, half * CORES * SQUARE, devices)
    joined = struct((2 * half,) + column.shape[1:], bf16)
    return call_kernel(join_kernel, [joined], [], 1, [column, far])[0]


def gather_planes(column, devices):
    return pack([column] + pass_chips([column] * SQUARE, devices))


def add_cores(keep, other):
    parts = [struct(keep.shape[1:], bf16)] * SQUARE
    return call_kernel(add_cores_kernel, parts, [], 1, [keep, other])


def add_chips(parts, passed, flops=1):
    depth, padded, lanes = parts[0].shape
    halves = [struct((depth // 2, padded, lanes), bf16)] * 2
    return call_kernel(add_chips_kernel, halves, [], flops, [parts[0]] + passed)


def add_layers(keep, send, devices):
    half, padded, lanes = keep.shape
    while half > 1:
        other = pass_on(send, half * CORES * SQUARE, devices)
        half //= 2
        halves = [struct((half, padded, lanes), bf16)] * 2
        keep, send = call_kernel(add_layers_kernel, halves, [], 1, [keep, other])
    other = pass_on(send, CORES * SQUARE, devices)
    return keep[0].astype(f32) + other[0].astype(f32)


def shards(inputs, attn_blocks, mlp_blocks, image_id, bias_id, out_grad):
    token_rows = inputs.shape[0]
    devices = lax.axis_size("fsdp")
    depth = devices // (CORES * SQUARE)
    window = token_rows + 2 * HALO
    attn_flat = devices * attn_blocks.shape[1] // LANES
    mlp_flat = devices * mlp_blocks.shape[1] // LANES
    barrier = lax.optimization_barrier

    outside = [(i, i + 1) for i in range(1, devices - 1, 2)]
    outside = outside + [(b, a) for a, b in outside]
    tokens, inner, outer, meta = call_kernel(
        functools.partial(prepare_kernel, devices - 1),
        [
            struct((token_rows, WIDE), bf16),
            struct((HALO, WIDE), bf16),
            struct((HALO, WIDE), bf16),
            struct((8,), jnp.int32),
        ],
        [
            pltpu.VMEM((token_rows // LANES, LANES), jnp.int32),
            pltpu.VMEM((token_rows // LANES, LANES), jnp.int32),
            pltpu.SemaphoreType.DMA((4,)),
        ],
        1,
        [
            lax.axis_index("fsdp").astype(jnp.int32).reshape(1),
            image_id.reshape(-1, LANES),
            bias_id.reshape(-1, LANES),
            inputs,
            out_grad,
        ],
        (1, 2, 3, 4),
        60 * 1024 * 1024,
    )
    attn_rows = as_rows(attn_blocks)
    mlp_rows = as_rows(mlp_blocks)
    attn_column = gather_columns(attn_rows, devices)
    mlp_column = double_column(mlp_rows[None], devices)
    attn_column, mlp_column, inner, outer = barrier((attn_column, mlp_column, inner, outer))
    inner = pass_cores(inner, devices)
    outer = lax.ppermute(outer, "fsdp", outside)
    mlp_column, inner = barrier((mlp_column, inner))
    while mlp_column.shape[0] < depth:
        mlp_column = double_column(mlp_column, devices)
    attn_mine = gather_planes(attn_column, devices)
    mlp_column, attn_mine, inner, outer = barrier((mlp_column, attn_mine, inner, outer))
    mlp_passed = pass_chips([mlp_column] * SQUARE, devices)
    attn_other = pass_cores(attn_mine, devices)

    (
        middle, cotangent, inputs_span, normed, qkv, probability, context, classes_span,
        w_qkv, w_out, gain,
    ) = call_kernel(
        attend_kernel,
        [
            struct((SPAN, D), f32),
            struct((SPAN, D), bf16),
            struct((SPAN, D), bf16),
            struct((SPAN, D), bf16),
            struct((SPAN, 3 * D), bf16),
            struct((2 * HEADS, SLOT, SLOT), bf16),
            struct((SPAN, D), bf16),
            struct((SPAN, LANES), bf16),
            struct((D, 3 * D), bf16),
            struct((D, D), bf16),
            struct((1, D), f32),
        ],
        [pltpu.VMEM((attn_flat + 16, LANES), f32), pltpu.VMEM((window, WIDE), bf16)],
        1,
        [meta, inner, tokens, outer, attn_mine, attn_other],
    )
    mlp_passed, middle = barrier((mlp_passed, middle))
    mlp_mine = pack([mlp_column] + mlp_passed)
    mlp_other = pass_cores(mlp_mine, devices)
    feed_blocks = struct((SQUARE,) + mlp_column.shape, bf16)
    output, grad_middle, feed_keep, feed_send = call_kernel(
        feed_kernel,
        [struct((window, D), bf16), struct((SPAN, D), f32), feed_blocks, feed_blocks],
        [
            pltpu.VMEM((mlp_flat + 16, LANES), f32),
            pltpu.VMEM((D, FF), bf16),
            pltpu.VMEM((FF, D), bf16),
            pltpu.VMEM((SPAN, D), bf16),
        ],
        1,
        [meta, middle, cotangent, mlp_mine, mlp_other],
    )
    feed_parts = add_cores(feed_keep, pass_cores(feed_send, devices))
    grad_first, grad_w_out, grad_bias_out, grad_table, grad_context = call_kernel(
        attend_back_kernel,
        [
            struct((SLOT, 3 * D), bf16),
            struct((D, D), f32),
            struct((1, D), f32),
            struct((8, LANES), f32),
            struct((SPAN, D), bf16),
        ],
        [],
        1,
        [meta, grad_middle, qkv, probability, context, classes_span, w_out],
    )
    feed_parts, grad_first = barrier((feed_parts, grad_first))
    feed_passed = pass_chips(feed_parts, devices)
    attn_blocks_out = struct((SQUARE,) + attn_column.shape, bf16)
    own_output, own_grad, inner, outer, attn_keep, attn_send = call_kernel(
        inputs_back_kernel,
        [
            struct((token_rows, D), bf16),
            struct((token_rows, D), f32),
            struct((HALO, 2 * D), bf16),
            struct((HALO, 2 * D), bf16),
            attn_blocks_out,
            attn_blocks_out,
        ],
        [
            pltpu.VMEM((attn_flat + 16, LANES), f32),
            pltpu.VMEM((SLOT, 3 * D), bf16),
            pltpu.VMEM((SPAN, 3 * D), bf16),
            pltpu.VMEM((window, D), f32),
        ],
        1,
        [
            meta, grad_middle, output, inputs_span, normed, qkv, probability, classes_span,
            w_qkv, gain, grad_first, grad_w_out, grad_bias_out, grad_table, grad_context,
        ],
    )
    attn_other = pass_cores(attn_send, devices)
    feed_keep, feed_send = add_chips(feed_parts, feed_passed, 10**10)
    outer = lax.ppermute(outer, "fsdp", outside)
    attn_other, feed_keep, feed_send, outer = barrier((attn_other, feed_keep, feed_send, outer))
    attn_parts = list(add_cores(attn_keep, attn_other))
    attn_passed = pass_chips(attn_parts, devices)
    attn_keep, attn_send = add_chips(attn_parts, attn_passed)
    attn_keep, inner = barrier((attn_keep, inner))
    inner = pass_cores(inner, devices)
    feed_sum = add_layers(feed_keep, feed_send, devices)
    attn_sum = add_layers(attn_keep, attn_send, devices)
    output, grad_inputs = call_kernel(
        combine_kernel,
        [struct((token_rows, D), bf16), struct((token_rows, D), f32)],
        [],
        1,
        [meta, own_output, own_grad, inner, outer],
    )
    return (output, grad_inputs, as_block(attn_sum, attn_blocks), as_block(feed_sum, mlp_blocks))


def solution(mesh):
    return jax.shard_map(
        shards,
        mesh=mesh,
        in_specs=(
            P("fsdp", None),
            P("fsdp", None),
            P("fsdp", None),
            P("fsdp"),
            P("fsdp"),
            P("fsdp", None),
        ),
        out_specs=(P("fsdp", None), P("fsdp", None), P("fsdp", None), P("fsdp", None)),
        check_vma=False,
    )
```

```python
import functools
import math

import jax
import jax.numpy as jnp
from jax import lax
from jax.experimental import pallas as pl
from jax.experimental.pallas import tpu as pltpu
from jax.sharding import PartitionSpec as P

D = 384
FF = 1536
HEADS = 6
HEAD_DIM = 64
IMG = 197
NB = 16

LANES = 128
CORES = 2
SQUARE = 4
SLOT = 208
SPAN = 2 * SLOT
HALO = 112
WIDE = 2 * D + LANES
D_ROWS = D // LANES
FF_ROWS = FF // LANES
QKV_ROWS = 3 * D // LANES

GAIN_AT = 0
SHIFT_AT = D_ROWS
W_QKV_AT = 2 * D_ROWS
BIAS_QUERY_AT = W_QKV_AT + D * QKV_ROWS
BIAS_VALUE_AT = BIAS_QUERY_AT + D_ROWS
W_OUT_AT = BIAS_VALUE_AT + D_ROWS
BIAS_OUT_AT = W_OUT_AT + D * D_ROWS
TABLE_AT = BIAS_OUT_AT + D_ROWS
W_UP_AT = 2 * D_ROWS
BIAS_UP_AT = W_UP_AT + D * FF_ROWS
W_DOWN_AT = BIAS_UP_AT + FF_ROWS
BIAS_DOWN_AT = W_DOWN_AT + FF * D_ROWS
FEED_END = BIAS_DOWN_AT + D_ROWS

epsilon = 1e-06
score_scale = HEAD_DIM ** (-0.5)
masked_score = -1e30
f32 = jnp.float32
bf16 = jnp.bfloat16


def dot(left, right):
    return lax.dot_general(left, right, (((1,), (0,)), ((), ())), preferred_element_type=f32)


def dot_rows(left, right):
    return lax.dot_general(left, right, (((0,), (0,)), ((), ())), preferred_element_type=f32)


def dot_cols(left, right):
    return lax.dot_general(left, right, (((1,), (1,)), ((), ())), preferred_element_type=f32)


def pass_on(value, step, devices):
    return lax.ppermute(value, "fsdp", [(i, i ^ step) for i in range(devices)])


def pass_cores(value, devices):
    return pass_on(value, 1, devices)


def pass_chips(parts, devices):
    return [pass_on(part, q * CORES, devices) for q, part in enumerate(parts) if q]


def pass_layers(parts, devices):
    return [pass_on(part, k * CORES * SQUARE, devices) for k, part in enumerate(parts) if k]


def rounded(amount, step):
    return -(-amount // step) * step


def as_rows(block):
    rows = block.shape[1] // LANES
    return jnp.pad(block.reshape(rows, LANES), ((0, rounded(rows, 8) - rows), (0, 0)))


def as_block(part, like):
    width = like.shape[1]
    return part.astype(f32)[: width // LANES].reshape(1, width)


def block_row(meta_ref, step, spot, layer, rows):
    where = (meta_ref[5] ^ layer) * SQUARE + (meta_ref[6] ^ spot)
    return (where * CORES + (meta_ref[4] ^ step)) * rows


def lay_out_blocks(meta_ref, mine_ref, other_ref, flat_ref):
    spots, depth, padded, lanes = mine_ref.shape
    rows = flat_ref.shape[0] // (CORES * spots * depth)
    for step, block_ref in enumerate((mine_ref, other_ref)):
        for spot in range(spots):
            for layer in range(depth):
                base = block_row(meta_ref, step, spot, layer, rows)
                flat_ref[pl.ds(base, rows), :] = block_ref[spot, layer].astype(f32)[:rows]


def cut_blocks(meta_ref, flat_ref, keep_ref, send_ref):
    spots, depth, padded, lanes = keep_ref.shape
    rows = flat_ref.shape[0] // (CORES * spots * depth)
    for step, out_ref in enumerate((keep_ref, send_ref)):
        for spot in range(spots):
            for layer in range(depth):
                base = block_row(meta_ref, step, spot, layer, rows)
                out_ref[spot, layer] = flat_ref[pl.ds(base, padded), :].astype(bf16)


def pack_kernel(*refs):
    for layer, part_ref in enumerate(refs[:-1]):
        refs[-1][layer] = part_ref[...]


def join_kernel(near_ref, far_ref, joined_ref):
    half = near_ref.shape[0]
    joined_ref[:half] = near_ref[...]
    joined_ref[half:] = far_ref[...]


def add_cores_kernel(keep_ref, other_ref, *out_refs):
    for spot, out_ref in enumerate(out_refs):
        total = keep_ref[spot].astype(f32) + other_ref[spot].astype(f32)
        out_ref[...] = total.astype(bf16)


def add_chips_kernel(*refs):
    parts, (keep_ref, send_ref) = refs[:SQUARE], refs[SQUARE:]
    half = keep_ref.shape[0]
    for layer in range(2 * half):
        total = parts[0][layer].astype(f32)
        for part_ref in parts[1:]:
            total = total + part_ref[layer].astype(f32)
        if layer < half:
            keep_ref[layer] = total.astype(bf16)
        else:
            send_ref[layer - half] = total.astype(bf16)


def add_layers_kernel(keep_ref, other_ref, near_ref, send_ref):
    half = near_ref.shape[0]
    near_ref[...] = (keep_ref[:half].astype(f32) + other_ref[:half].astype(f32)).astype(bf16)
    send_ref[...] = (keep_ref[half:].astype(f32) + other_ref[half:].astype(f32)).astype(bf16)


def sixth(index):
    return (index * 43) >> 8


def head_mask():
    lane = lax.broadcasted_iota(jnp.int32, (8, LANES), 1)
    head = lax.broadcasted_iota(jnp.int32, (8, LANES), 0)
    inside = (lane - HEADS * sixth(lane) == head) & (lane < NB * HEADS)
    return jnp.where(inside, 1.0, 0.0)


def edge_rows(core, near_core, last):
    return pl.ds(pl.multiple_of(jnp.where(core == near_core, last, 0), 16), HALO)


def prepare_kernel(
    last_device, device_ref, image_hbm, bias_hbm, inputs_hbm, out_grad_hbm,
    tokens_ref, inner_ref, outer_ref, meta_ref,
    image_ref, bias_ref, semaphores,
):
    token_rows = tokens_ref.shape[0]
    moves = [
        pltpu.make_async_copy(source, target, semaphores.at[step])
        for step, (source, target) in enumerate(
            [
                (bias_hbm, bias_ref),
                (image_hbm, image_ref),
                (inputs_hbm, tokens_ref.at[:, 0:D]),
                (out_grad_hbm, tokens_ref.at[:, D : 2 * D]),
            ]
        )
    ]
    for move in moves:
        move.start()
    entry = sixth(lax.broadcasted_iota(jnp.int32, (LANES, LANES), 0))
    inside = entry < NB
    moves[0].wait()
    for step in range(token_rows // LANES):
        same = inside & (entry == bias_ref[step : step + 1])
        classes = jnp.transpose(jnp.where(same, 1.0, 0.0))
        tokens_ref[step * LANES : (step + 1) * LANES, 2 * D :] = classes.astype(bf16)
    moves[1].wait()
    images = image_ref[...]
    ends = jnp.sum(jnp.where(images == images[0:1, 0:1], 1, 0))
    device = device_ref[0]
    first, last = device == 0, device == last_device
    holds = first | (ends >= IMG // 2 + 1)
    start = jnp.where(first, 0, jnp.where(holds, ends - IMG, ends))
    stop = jnp.where(last, token_rows, token_rows + IMG)
    stop_one = jnp.where(holds, ends, jnp.minimum(ends + IMG, stop))
    has_next = (stop_one < stop) & (last | (stop_one + IMG // 2 < token_rows))
    stop_two = jnp.where(has_next, jnp.minimum(stop_one + IMG, stop), stop_one)
    meta_ref[0] = start + HALO
    meta_ref[1] = stop_one - start
    meta_ref[2] = stop_one + HALO
    meta_ref[3] = stop_two - stop_one
    meta_ref[4] = device & (CORES - 1)
    meta_ref[5] = device >> 3
    meta_ref[6] = (device >> 1) & (SQUARE - 1)
    meta_ref[7] = 0
    moves[2].wait()
    moves[3].wait()
    core = device & (CORES - 1)
    inner_ref[...] = tokens_ref[edge_rows(core, 0, token_rows - HALO)]
    outer_ref[...] = tokens_ref[edge_rows(core, 1, token_rows - HALO)]


def read_vector(flat_ref, at, amount):
    return jnp.concatenate([flat_ref[at + i : at + i + 1] for i in range(amount)], axis=1)


def write_vector(flat_ref, at, amount, value):
    for i in range(amount):
        flat_ref[at + i : at + i + 1] = value[:, i * LANES : (i + 1) * LANES]


def read_matrix(flat_ref, at, height, amount, out_ref):
    for i in range(amount):
        chunk = flat_ref[pl.ds(at + i, height, stride=amount), :]
        out_ref[:, i * LANES : (i + 1) * LANES] = chunk.astype(bf16)


def normalise(values):
    average = jnp.mean(values, axis=-1, keepdims=True)
    centred = values - average
    variance = jnp.mean(centred * centred, axis=-1, keepdims=True)
    inverse = lax.rsqrt(variance + epsilon)
    return (centred * inverse, inverse)


def norm_back(grad, unit, inverse, gain):
    scaled = grad * gain
    first = jnp.mean(scaled, axis=-1, keepdims=True)
    second = jnp.mean(scaled * unit, axis=-1, keepdims=True)
    return inverse * (scaled - first - unit * second)


def slot_mask(meta_ref, window, by_column):
    shape = (window, SPAN) if by_column else (SPAN, window)
    spot = lax.broadcasted_iota(jnp.int32, shape, 0 if by_column else 1)
    row = lax.broadcasted_iota(jnp.int32, shape, 1 if by_column else 0)
    start = jnp.where(row < SLOT, meta_ref[0], meta_ref[2] - SLOT)
    limit = jnp.where(row < SLOT, meta_ref[1], meta_ref[3] + SLOT)
    return jnp.where((spot == row + start) & (row < limit), 1.0, 0.0).astype(bf16)


def head_lanes(half):
    lane = lax.broadcasted_iota(jnp.int32, (1, LANES), 1)
    return (lane < HEAD_DIM) if half == 0 else (lane >= HEAD_DIM)


def attend_kernel(
    meta_ref, inner_ref, own_ref, outer_ref,
    mine_ref, other_ref,
    middle_ref, cotangent_ref, inputs_ref, normed_ref, qkv_ref, probability_ref,
    context_ref, classes_ref, w_qkv_ref, w_out_ref, gain_ref,
    flat_ref, window_ref,
):
    window = window_ref.shape[0]
    lay_out_blocks(meta_ref, mine_ref, other_ref, flat_ref)
    read_matrix(flat_ref, W_QKV_AT, D, QKV_ROWS, w_qkv_ref)
    read_matrix(flat_ref, W_OUT_AT, D, D_ROWS, w_out_ref)
    gain = read_vector(flat_ref, GAIN_AT, D_ROWS)
    shift = read_vector(flat_ref, SHIFT_AT, D_ROWS)
    gain_ref[...] = gain
    bias_query = read_vector(flat_ref, BIAS_QUERY_AT, D_ROWS)
    bias_value = read_vector(flat_ref, BIAS_VALUE_AT, D_ROWS)
    bias_out = read_vector(flat_ref, BIAS_OUT_AT, D_ROWS)
    table = (head_mask() * flat_ref[TABLE_AT : TABLE_AT + 1]).astype(bf16)

    own = own_ref.shape[0]
    window_ref[edge_rows(meta_ref[4], 0, HALO + own)] = inner_ref[...]
    window_ref[HALO : HALO + own] = own_ref[...]
    window_ref[edge_rows(meta_ref[4], 1, HALO + own)] = outer_ref[...]
    picked = dot(slot_mask(meta_ref, window, False), window_ref[...])
    inputs = picked[:, :D]
    inputs_ref[...] = inputs.astype(bf16)
    cotangent_ref[...] = picked[:, D : 2 * D].astype(bf16)
    classes_ref[...] = picked[:, 2 * D :].astype(bf16)

    unit, _ = normalise(inputs)
    normed_ref[...] = (unit * gain + shift).astype(bf16)
    normed = normed_ref[...]
    qkv_ref[:, :D] = (dot(normed, w_qkv_ref[:, :D]) + bias_query).astype(bf16)
    qkv_ref[:, D : 2 * D] = dot(normed, w_qkv_ref[:, D : 2 * D]).astype(bf16)
    qkv_ref[:, 2 * D :] = (dot(normed, w_qkv_ref[:, 2 * D :]) + bias_value).astype(bf16)

    for slot in range(2):
        rows = slice(slot * SLOT, (slot + 1) * SLOT)
        key = lax.broadcasted_iota(jnp.int32, (1, SLOT), 1)
        key_bias = dot_cols(table, classes_ref[rows])
        key_bias = jnp.where(key < meta_ref[2 * slot + 1], key_bias, masked_score)
        for pair in range(HEADS // 2):
            lanes = slice(pair * LANES, (pair + 1) * LANES)
            queries = qkv_ref[rows, lanes]
            keys = qkv_ref[rows, D + pair * LANES : D + (pair + 1) * LANES]
            values = qkv_ref[rows, 2 * D + pair * LANES : 2 * D + (pair + 1) * LANES]
            mixed = []
            for half in range(2):
                head = 2 * pair + half
                chosen = jnp.where(head_lanes(half), queries, jnp.zeros_like(queries))
                scores = dot_cols(chosen, keys) * score_scale + key_bias[head : head + 1]
                peak = jnp.max(scores, axis=-1, keepdims=True)
                weights = jnp.exp(scores - peak)
                total = jnp.sum(weights, axis=-1, keepdims=True)
                probability = (weights * (1.0 / total)).astype(bf16)
                probability_ref[slot * HEADS + head] = probability
                mixed.append(dot(probability, values))
            context_ref[rows, lanes] = jnp.where(head_lanes(0), mixed[0], mixed[1]).astype(bf16)
    middle_ref[...] = inputs + dot(context_ref[...], w_out_ref[...]) + bias_out


def feed_kernel(
    meta_ref, middle_ref, cotangent_ref,
    mine_ref, other_ref,
    output_ref, grad_middle_ref, keep_ref, send_ref,
    flat_ref, w_up_ref, w_down_ref, normed_ref,
):
    window = output_ref.shape[0]
    lay_out_blocks(meta_ref, mine_ref, other_ref, flat_ref)
    read_matrix(flat_ref, W_UP_AT, D, FF_ROWS, w_up_ref)
    read_matrix(flat_ref, W_DOWN_AT, FF, D_ROWS, w_down_ref)
    gain = read_vector(flat_ref, GAIN_AT, D_ROWS)
    shift = read_vector(flat_ref, SHIFT_AT, D_ROWS)
    bias_up = read_vector(flat_ref, BIAS_UP_AT, FF_ROWS)
    bias_down = read_vector(flat_ref, BIAS_DOWN_AT, D_ROWS)

    middle = middle_ref[...]
    cotangent = cotangent_ref[...]
    unit, inverse = normalise(middle)
    normed_ref[...] = (unit * gain + shift).astype(bf16)
    normed = normed_ref[...]
    output = middle + bias_down
    grad = jnp.zeros((SPAN, D), f32)
    slope = math.sqrt(2.0 / math.pi)
    for step in range(FF // D):
        cols = slice(step * D, (step + 1) * D)
        w_up = w_up_ref[:, cols]
        w_down = w_down_ref[cols]
        hidden = dot(normed, w_up) + bias_up[:, cols]
        square = hidden * hidden
        bend = jnp.tanh(slope * hidden * (1.0 + 0.044715 * square))
        half = 0.5 * (1.0 + bend)
        active = (hidden * half).astype(bf16)
        steep = half + 0.5 * hidden * (1.0 - bend * bend) * (
            slope * (1.0 + (3 * 0.044715) * square)
        )
        grad_hidden_wide = dot_cols(cotangent, w_down) * steep
        grad_hidden = grad_hidden_wide.astype(bf16)
        output = output + dot(active, w_down)
        grad = grad + dot_cols(grad_hidden, w_up)
        grad_down = dot_rows(active, cotangent)
        grad_up = dot_rows(normed, grad_hidden)
        grad_bias = jnp.sum(grad_hidden.astype(f32), axis=0, keepdims=True)
        write_vector(flat_ref, BIAS_UP_AT + step * D_ROWS, D_ROWS, grad_bias)
        for i in range(D_ROWS):
            lanes = slice(i * LANES, (i + 1) * LANES)
            flat_ref[pl.ds(W_UP_AT + step * D_ROWS + i, D, stride=FF_ROWS), :] = grad_up[:, lanes]
            flat_ref[pl.ds(W_DOWN_AT + step * D * D_ROWS + i, D, stride=D_ROWS), :] = grad_down[
                :, lanes
            ]
    output_ref[...] = dot(slot_mask(meta_ref, window, True), output.astype(bf16)).astype(bf16)
    grad_output = cotangent.astype(f32)
    write_vector(flat_ref, GAIN_AT, D_ROWS, jnp.sum(grad * unit, axis=0, keepdims=True))
    write_vector(flat_ref, SHIFT_AT, D_ROWS, jnp.sum(grad, axis=0, keepdims=True))
    write_vector(flat_ref, BIAS_DOWN_AT, D_ROWS, jnp.sum(grad_output, axis=0, keepdims=True))
    flat_ref[FEED_END:] = jnp.zeros((flat_ref.shape[0] - FEED_END, LANES), f32)
    grad_middle_ref[...] = grad_output + norm_back(grad, unit, inverse, gain)
    cut_blocks(meta_ref, flat_ref, keep_ref, send_ref)


def slot_back(
    slot, qkv_ref, probability_ref, classes_ref, grad_context_ref, grad_qkv_ref
):
    rows = slice(slot * SLOT, (slot + 1) * SLOT)
    key_sums = []
    for pair in range(HEADS // 2):
        lanes = slice(pair * LANES, (pair + 1) * LANES)
        key_lanes = slice(D + pair * LANES, D + (pair + 1) * LANES)
        value_lanes = slice(2 * D + pair * LANES, 2 * D + (pair + 1) * LANES)
        queries = qkv_ref[rows, lanes]
        keys = qkv_ref[rows, key_lanes]
        values = qkv_ref[rows, value_lanes]
        grad_context = grad_context_ref[rows, lanes]
        parts = []
        for half in range(2):
            head = 2 * pair + half
            chosen = jnp.where(head_lanes(half), grad_context, jnp.zeros_like(grad_context))
            grad_probs = dot_cols(chosen, values)
            narrow = probability_ref[slot * HEADS + head]
            probability = narrow.astype(f32)
            weighted = probability * grad_probs
            grad_scores = weighted - probability * jnp.sum(weighted, axis=-1, keepdims=True)
            key_sums.append(jnp.sum(grad_scores, axis=0, keepdims=True))
            grad_raw = (grad_scores * score_scale).astype(bf16)
            parts.append(
                (dot(grad_raw, keys), dot_rows(grad_raw, queries), dot_rows(narrow, grad_context))
            )
        low = head_lanes(0)
        for where, first, second in zip((lanes, key_lanes, value_lanes), *parts):
            grad_qkv_ref[:, where] = jnp.where(low, first, second).astype(bf16)
    sums = jnp.concatenate(key_sums + [jnp.zeros((8 - HEADS, SLOT), f32)], axis=0)
    sums_high = sums.astype(bf16)
    sums_low = (sums - sums_high.astype(f32)).astype(bf16)
    classes = classes_ref[rows]
    return dot(sums_high, classes) + dot(sums_low, classes)


def attend_back_kernel(
    meta_ref, grad_middle_ref, qkv_ref, probability_ref, context_ref, classes_ref, w_out_ref,
    grad_qkv_ref, grad_w_out_ref, grad_bias_out_ref, grad_table_ref, grad_context_ref,
):
    grad_branch = grad_middle_ref[...].astype(bf16)
    grad_bias_out_ref[...] = jnp.sum(grad_branch.astype(f32), axis=0, keepdims=True)
    grad_w_out_ref[...] = dot_rows(context_ref[...], grad_branch)
    grad_context_ref[...] = dot_cols(grad_branch, w_out_ref[...]).astype(bf16)
    grad_table_ref[...] = slot_back(
        0, qkv_ref, probability_ref, classes_ref, grad_context_ref, grad_qkv_ref
    )


def inputs_back_kernel(
    meta_ref, grad_middle_ref, output_ref, inputs_ref, normed_ref, qkv_ref, probability_ref,
    classes_ref, w_qkv_ref, gain_ref,
    grad_first_ref, grad_w_out_ref, grad_bias_out_ref, grad_table_ref, grad_context_ref,
    own_output_ref, own_grad_ref, inner_ref, outer_ref, keep_ref, send_ref,
    flat_ref, grad_second_ref, grad_qkv_ref, grad_inputs_ref,
):
    window = grad_inputs_ref.shape[0]
    grad_table = grad_table_ref[...] + slot_back(
        1, qkv_ref, probability_ref, classes_ref, grad_context_ref, grad_second_ref
    )
    grad_qkv_ref[:SLOT] = grad_first_ref[...]
    grad_qkv_ref[SLOT:] = grad_second_ref[...]
    flat_ref[TABLE_AT:] = jnp.zeros((flat_ref.shape[0] - TABLE_AT, LANES), f32)
    flat_ref[TABLE_AT : TABLE_AT + 1] = jnp.sum(grad_table * head_mask(), axis=0, keepdims=True)
    write_vector(flat_ref, BIAS_OUT_AT, D_ROWS, grad_bias_out_ref[...])
    for i in range(D_ROWS):
        flat_ref[pl.ds(W_OUT_AT + i, D, stride=D_ROWS), :] = grad_w_out_ref[
            :, i * LANES : (i + 1) * LANES
        ]
    grad_qkv = grad_qkv_ref[...]
    column_sums = jnp.sum(grad_qkv.astype(f32), axis=0, keepdims=True)
    write_vector(flat_ref, BIAS_QUERY_AT, D_ROWS, column_sums[:, :D])
    write_vector(flat_ref, BIAS_VALUE_AT, D_ROWS, column_sums[:, 2 * D :])
    normed = normed_ref[...]
    for part in range(3):
        grad_w = dot_rows(normed, grad_qkv_ref[:, part * D : (part + 1) * D])
        for i in range(D_ROWS):
            flat_ref[pl.ds(W_QKV_AT + part * D_ROWS + i, D, stride=QKV_ROWS), :] = grad_w[
                :, i * LANES : (i + 1) * LANES
            ]
    grad_normed = dot_cols(grad_qkv, w_qkv_ref[...])
    gain = gain_ref[...]
    unit, inverse = normalise(inputs_ref[...].astype(f32))
    write_vector(flat_ref, GAIN_AT, D_ROWS, jnp.sum(grad_normed * unit, axis=0, keepdims=True))
    write_vector(flat_ref, SHIFT_AT, D_ROWS, jnp.sum(grad_normed, axis=0, keepdims=True))
    grad_inputs = grad_middle_ref[...] + norm_back(grad_normed, unit, inverse, gain)
    high = grad_inputs.astype(bf16)
    low_part = (grad_inputs - high.astype(f32)).astype(bf16)
    back = slot_mask(meta_ref, window, True)
    grad_inputs_ref[...] = dot(back, high) + dot(back, low_part)
    own = slice(HALO, window - HALO)
    own_output_ref[...] = output_ref[own]
    own_grad_ref[...] = grad_inputs_ref[own]
    for near_core, edge_ref in enumerate((inner_ref, outer_ref)):
        edge = edge_rows(meta_ref[4], near_core, window - HALO)
        edge_ref[:, :D] = output_ref[edge]
        edge_ref[:, D:] = grad_inputs_ref[edge].astype(bf16)
    cut_blocks(meta_ref, flat_ref, keep_ref, send_ref)


def combine_kernel(
    meta_ref, own_output_ref, own_grad_ref, inner_ref, outer_ref, output_ref, grad_inputs_ref
):
    last = output_ref.shape[0] - HALO
    output_ref[HALO:last] = own_output_ref[HALO:last]
    grad_inputs_ref[HALO:last] = own_grad_ref[HALO:last]
    for near_core, edge_ref in enumerate((inner_ref, outer_ref)):
        edge = edge_rows(meta_ref[4], near_core, last)
        output_ref[edge] = (
            own_output_ref[edge].astype(f32) + edge_ref[:, :D].astype(f32)
        ).astype(bf16)
        grad_inputs_ref[edge] = own_grad_ref[edge] + edge_ref[:, D:].astype(f32)


def call_kernel(kernel, out_shapes, scratch, flops, operands, far=(), room=32 * 1024 * 1024):
    vmem = pl.BlockSpec(memory_space=pltpu.VMEM)
    smem = pl.BlockSpec(memory_space=pltpu.SMEM)
    specs = [smem if operand.dtype == jnp.int32 else vmem for operand in operands]
    for index in far:
        specs[index] = pl.BlockSpec(memory_space=pltpu.HBM)
    return pl.pallas_call(
        kernel,
        out_shape=out_shapes,
        in_specs=specs,
        out_specs=[smem if shape.dtype == jnp.int32 else vmem for shape in out_shapes],
        scratch_shapes=scratch,
        compiler_params=pltpu.CompilerParams(vmem_limit_bytes=room),
        cost_estimate=pl.CostEstimate(flops=flops, bytes_accessed=1, transcendentals=0),
    )(*operands)


def struct(shape, kind):
    return jax.ShapeDtypeStruct(shape, kind)


def pack(parts, flops=1):
    packed = struct((len(parts),) + parts[0].shape, bf16)
    return call_kernel(pack_kernel, [packed], [], flops, parts)[0]


def gather_columns(rows, devices):
    depth = devices // (CORES * SQUARE)
    return pack([rows] + pass_layers([rows] * depth, devices), 10**10)


def pass_column(column, devices):
    return pass_on(column, column.shape[0] * CORES * SQUARE, devices)


def join(near, far):
    joined = struct((2 * near.shape[0],) + near.shape[1:], bf16)
    return call_kernel(join_kernel, [joined], [], 1, [near, far])[0]


def add_cores(keep, other):
    parts = [struct(keep.shape[1:], bf16)] * SQUARE
    return call_kernel(add_cores_kernel, parts, [], 1, [keep, other])


def add_chips(parts, passed, flops=1):
    depth, padded, lanes = parts[0].shape
    halves = [struct((depth // 2, padded, lanes), bf16)] * 2
    return call_kernel(add_chips_kernel, halves, [], flops, [parts[0]] + passed)


def add_layers(keep, send, devices):
    half, padded, lanes = keep.shape
    while half > 1:
        other = pass_on(send, half * CORES * SQUARE, devices)
        half //= 2
        halves = [struct((half, padded, lanes), bf16)] * 2
        keep, send = call_kernel(add_layers_kernel, halves, [], 1, [keep, other])
    other = pass_on(send, CORES * SQUARE, devices)
    return keep[0].astype(f32) + other[0].astype(f32)


def shards(inputs, attn_blocks, mlp_blocks, image_id, bias_id, out_grad):
    token_rows = inputs.shape[0]
    devices = lax.axis_size("fsdp")
    depth = devices // (CORES * SQUARE)
    window = token_rows + 2 * HALO
    attn_flat = devices * attn_blocks.shape[1] // LANES
    mlp_flat = devices * mlp_blocks.shape[1] // LANES
    barrier = lax.optimization_barrier

    outside = [(i, i + 1) for i in range(1, devices - 1, 2)]
    outside = outside + [(b, a) for a, b in outside]
    tokens, inner, outer, meta = call_kernel(
        functools.partial(prepare_kernel, devices - 1),
        [
            struct((token_rows, WIDE), bf16),
            struct((HALO, WIDE), bf16),
            struct((HALO, WIDE), bf16),
            struct((8,), jnp.int32),
        ],
        [
            pltpu.VMEM((token_rows // LANES, LANES), jnp.int32),
            pltpu.VMEM((token_rows // LANES, LANES), jnp.int32),
            pltpu.SemaphoreType.DMA((4,)),
        ],
        1,
        [
            lax.axis_index("fsdp").astype(jnp.int32).reshape(1),
            image_id.reshape(-1, LANES),
            bias_id.reshape(-1, LANES),
            inputs,
            out_grad,
        ],
        (1, 2, 3, 4),
        60 * 1024 * 1024,
    )
    attn_rows = as_rows(attn_blocks)
    mlp_rows = as_rows(mlp_blocks)
    attn_column = gather_columns(attn_rows, devices)
    mlp_column = join(mlp_rows[None], pass_column(mlp_rows[None], devices))
    attn_column, mlp_column, inner, outer = barrier((attn_column, mlp_column, inner, outer))
    inner = pass_cores(inner, devices)
    inner, outer = barrier((inner, outer))
    outer = lax.ppermute(outer, "fsdp", outside)
    while 2 * mlp_column.shape[0] < depth:
        mlp_column = join(mlp_column, pass_column(mlp_column, devices))
    mlp_far = pass_column(mlp_column, devices)
    attn_passed = pass_chips([attn_column] * SQUARE, devices)
    attn_mine = pack([attn_column] + attn_passed, 10**10)
    attn_mine, outer, mlp_far = barrier((attn_mine, outer, mlp_far))
    mlp_column = join(mlp_column, mlp_far)
    mlp_column, attn_mine, inner, outer = barrier((mlp_column, attn_mine, inner, outer))
    mlp_passed = pass_chips([mlp_column] * SQUARE, devices)
    attn_other = pass_cores(attn_mine, devices)

    (
        middle, cotangent, inputs_span, normed, qkv, probability, context, classes_span,
        w_qkv, w_out, gain,
    ) = call_kernel(
        attend_kernel,
        [
            struct((SPAN, D), f32),
            struct((SPAN, D), bf16),
            struct((SPAN, D), bf16),
            struct((SPAN, D), bf16),
            struct((SPAN, 3 * D), bf16),
            struct((2 * HEADS, SLOT, SLOT), bf16),
            struct((SPAN, D), bf16),
            struct((SPAN, LANES), bf16),
            struct((D, 3 * D), bf16),
            struct((D, D), bf16),
            struct((1, D), f32),
        ],
        [pltpu.VMEM((attn_flat + 16, LANES), f32), pltpu.VMEM((window, WIDE), bf16)],
        1,
        [meta, inner, tokens, outer, attn_mine, attn_other],
    )
    mlp_passed, middle = barrier((mlp_passed, middle))
    mlp_mine = pack([mlp_column] + mlp_passed)
    mlp_other = pass_cores(mlp_mine, devices)
    feed_blocks = struct((SQUARE,) + mlp_column.shape, bf16)
    output, grad_middle, feed_keep, feed_send = call_kernel(
        feed_kernel,
        [struct((window, D), bf16), struct((SPAN, D), f32), feed_blocks, feed_blocks],
        [
            pltpu.VMEM((mlp_flat + 16, LANES), f32),
            pltpu.VMEM((D, FF), bf16),
            pltpu.VMEM((FF, D), bf16),
            pltpu.VMEM((SPAN, D), bf16),
        ],
        1,
        [meta, middle, cotangent, mlp_mine, mlp_other],
    )
    feed_parts = add_cores(feed_keep, pass_cores(feed_send, devices))
    grad_first, grad_w_out, grad_bias_out, grad_table, grad_context = call_kernel(
        attend_back_kernel,
        [
            struct((SLOT, 3 * D), bf16),
            struct((D, D), f32),
            struct((1, D), f32),
            struct((8, LANES), f32),
            struct((SPAN, D), bf16),
        ],
        [],
        1,
        [meta, grad_middle, qkv, probability, context, classes_span, w_out],
    )
    feed_parts, grad_first = barrier((feed_parts, grad_first))
    feed_passed = pass_chips(feed_parts, devices)
    attn_blocks_out = struct((SQUARE,) + attn_column.shape, bf16)
    own_output, own_grad, inner, outer, attn_keep, attn_send = call_kernel(
        inputs_back_kernel,
        [
            struct((token_rows, D), bf16),
            struct((token_rows, D), f32),
            struct((HALO, 2 * D), bf16),
            struct((HALO, 2 * D), bf16),
            attn_blocks_out,
            attn_blocks_out,
        ],
        [
            pltpu.VMEM((attn_flat + 16, LANES), f32),
            pltpu.VMEM((SLOT, 3 * D), bf16),
            pltpu.VMEM((SPAN, 3 * D), bf16),
            pltpu.VMEM((window, D), f32),
        ],
        1,
        [
            meta, grad_middle, output, inputs_span, normed, qkv, probability, classes_span,
            w_qkv, gain, grad_first, grad_w_out, grad_bias_out, grad_table, grad_context,
        ],
    )
    attn_other = pass_cores(attn_send, devices)
    feed_keep, feed_send = add_chips(feed_parts, feed_passed, 10**10)
    outer = lax.ppermute(outer, "fsdp", outside)
    attn_other, feed_keep, feed_send, outer = barrier((attn_other, feed_keep, feed_send, outer))
    attn_parts = list(add_cores(attn_keep, attn_other))
    attn_passed = pass_chips(attn_parts, devices)
    attn_keep, attn_send = add_chips(attn_parts, attn_passed)
    attn_keep, inner = barrier((attn_keep, inner))
    inner = pass_cores(inner, devices)
    feed_sum = add_layers(feed_keep, feed_send, devices)
    attn_sum = add_layers(attn_keep, attn_send, devices)
    output, grad_inputs = call_kernel(
        combine_kernel,
        [struct((token_rows, D), bf16), struct((token_rows, D), f32)],
        [],
        1,
        [meta, own_output, own_grad, inner, outer],
    )
    return (output, grad_inputs, as_block(attn_sum, attn_blocks), as_block(feed_sum, mlp_blocks))


def solution(mesh):
    return jax.shard_map(
        shards,
        mesh=mesh,
        in_specs=(
            P("fsdp", None),
            P("fsdp", None),
            P("fsdp", None),
            P("fsdp"),
            P("fsdp"),
            P("fsdp", None),
        ),
        out_specs=(P("fsdp", None), P("fsdp", None), P("fsdp", None), P("fsdp", None)),
        check_vma=False,
    )
```

```python
import functools
import math

import jax
import jax.numpy as jnp
from jax import lax
from jax.experimental import pallas as pl
from jax.experimental.pallas import tpu as pltpu
from jax.sharding import PartitionSpec as P

D = 384
FF = 1536
HEADS = 6
HEAD_DIM = 64
IMG = 197
NB = 16

LANES = 128
CORES = 2
SQUARE = 4
SLOT = 208
SPAN = 2 * SLOT
HALO = 112
WIDE = 2 * D + LANES
D_ROWS = D // LANES
FF_ROWS = FF // LANES
QKV_ROWS = 3 * D // LANES

GAIN_AT = 0
SHIFT_AT = D_ROWS
W_QKV_AT = 2 * D_ROWS
BIAS_QUERY_AT = W_QKV_AT + D * QKV_ROWS
BIAS_VALUE_AT = BIAS_QUERY_AT + D_ROWS
W_OUT_AT = BIAS_VALUE_AT + D_ROWS
BIAS_OUT_AT = W_OUT_AT + D * D_ROWS
TABLE_AT = BIAS_OUT_AT + D_ROWS
W_UP_AT = 2 * D_ROWS
BIAS_UP_AT = W_UP_AT + D * FF_ROWS
W_DOWN_AT = BIAS_UP_AT + FF_ROWS
BIAS_DOWN_AT = W_DOWN_AT + FF * D_ROWS
FEED_END = BIAS_DOWN_AT + D_ROWS

epsilon = 1e-06
score_scale = HEAD_DIM ** (-0.5)
masked_score = -1e30
f32 = jnp.float32
bf16 = jnp.bfloat16


def dot(left, right):
    return lax.dot_general(left, right, (((1,), (0,)), ((), ())), preferred_element_type=f32)


def dot_rows(left, right):
    return lax.dot_general(left, right, (((0,), (0,)), ((), ())), preferred_element_type=f32)


def dot_cols(left, right):
    return lax.dot_general(left, right, (((1,), (1,)), ((), ())), preferred_element_type=f32)


def pass_on(value, step, devices):
    return lax.ppermute(value, "fsdp", [(i, i ^ step) for i in range(devices)])


def pass_cores(value, devices):
    return pass_on(value, 1, devices)


def pass_chips(parts, devices):
    return [pass_on(part, q * CORES, devices) for q, part in enumerate(parts) if q]


def pass_layers(parts, devices):
    return [pass_on(part, k * CORES * SQUARE, devices) for k, part in enumerate(parts) if k]


def rounded(amount, step):
    return -(-amount // step) * step


def as_rows(block):
    rows = block.shape[1] // LANES
    return jnp.pad(block.reshape(rows, LANES), ((0, rounded(rows, 8) - rows), (0, 0)))


def as_block(part, like):
    width = like.shape[1]
    return part.astype(f32)[: width // LANES].reshape(1, width)


def block_row(meta_ref, step, spot, layer, rows):
    where = (meta_ref[5] ^ layer) * SQUARE + (meta_ref[6] ^ spot)
    return (where * CORES + (meta_ref[4] ^ step)) * rows


def lay_out_blocks(meta_ref, mine_ref, other_ref, flat_ref):
    spots, depth, padded, lanes = mine_ref.shape
    rows = flat_ref.shape[0] // (CORES * spots * depth)
    for step, block_ref in enumerate((mine_ref, other_ref)):
        for spot in range(spots):
            for layer in range(depth):
                base = block_row(meta_ref, step, spot, layer, rows)
                flat_ref[pl.ds(base, rows), :] = block_ref[spot, layer].astype(f32)[:rows]


def cut_blocks(meta_ref, flat_ref, keep_ref, send_ref):
    spots, depth, padded, lanes = keep_ref.shape
    rows = flat_ref.shape[0] // (CORES * spots * depth)
    for step, out_ref in enumerate((keep_ref, send_ref)):
        for spot in range(spots):
            for layer in range(depth):
                base = block_row(meta_ref, step, spot, layer, rows)
                out_ref[spot, layer] = flat_ref[pl.ds(base, padded), :].astype(bf16)


def pack_kernel(*refs):
    for layer, part_ref in enumerate(refs[:-1]):
        refs[-1][layer] = part_ref[...]


def join_kernel(near_ref, far_ref, joined_ref):
    half = near_ref.shape[0]
    joined_ref[:half] = near_ref[...]
    joined_ref[half:] = far_ref[...]


def add_cores_kernel(keep_ref, other_ref, *out_refs):
    for spot, out_ref in enumerate(out_refs):
        total = keep_ref[spot].astype(f32) + other_ref[spot].astype(f32)
        out_ref[...] = total.astype(bf16)


def add_chips_kernel(*refs):
    parts, (keep_ref, send_ref) = refs[:SQUARE], refs[SQUARE:]
    half = keep_ref.shape[0]
    for layer in range(2 * half):
        total = parts[0][layer].astype(f32)
        for part_ref in parts[1:]:
            total = total + part_ref[layer].astype(f32)
        if layer < half:
            keep_ref[layer] = total.astype(bf16)
        else:
            send_ref[layer - half] = total.astype(bf16)


def add_layers_kernel(keep_ref, other_ref, near_ref, send_ref):
    half = near_ref.shape[0]
    near_ref[...] = (keep_ref[:half].astype(f32) + other_ref[:half].astype(f32)).astype(bf16)
    send_ref[...] = (keep_ref[half:].astype(f32) + other_ref[half:].astype(f32)).astype(bf16)


def sixth(index):
    return (index * 43) >> 8


def head_mask():
    lane = lax.broadcasted_iota(jnp.int32, (8, LANES), 1)
    head = lax.broadcasted_iota(jnp.int32, (8, LANES), 0)
    inside = (lane - HEADS * sixth(lane) == head) & (lane < NB * HEADS)
    return jnp.where(inside, 1.0, 0.0)


def edge_rows(core, near_core, last):
    return pl.ds(pl.multiple_of(jnp.where(core == near_core, last, 0), 16), HALO)


def prepare_kernel(
    last_device, device_ref, image_hbm, bias_hbm, inputs_hbm, out_grad_hbm,
    tokens_ref, inner_ref, outer_ref, meta_ref,
    image_ref, bias_ref, semaphores,
):
    token_rows = tokens_ref.shape[0]
    moves = [
        pltpu.make_async_copy(source, target, semaphores.at[step])
        for step, (source, target) in enumerate(
            [
                (bias_hbm, bias_ref),
                (image_hbm, image_ref),
                (inputs_hbm, tokens_ref.at[:, 0:D]),
                (out_grad_hbm, tokens_ref.at[:, D : 2 * D]),
            ]
        )
    ]
    for move in moves:
        move.start()
    entry = sixth(lax.broadcasted_iota(jnp.int32, (LANES, LANES), 0))
    inside = entry < NB
    moves[0].wait()
    for step in range(token_rows // LANES):
        same = inside & (entry == bias_ref[step : step + 1])
        classes = jnp.transpose(jnp.where(same, 1.0, 0.0))
        tokens_ref[step * LANES : (step + 1) * LANES, 2 * D :] = classes.astype(bf16)
    moves[1].wait()
    images = image_ref[...]
    ends = jnp.sum(jnp.where(images == images[0:1, 0:1], 1, 0))
    device = device_ref[0]
    first, last = device == 0, device == last_device
    holds = first | (ends >= IMG // 2 + 1)
    start = jnp.where(first, 0, jnp.where(holds, ends - IMG, ends))
    stop = jnp.where(last, token_rows, token_rows + IMG)
    stop_one = jnp.where(holds, ends, jnp.minimum(ends + IMG, stop))
    has_next = (stop_one < stop) & (last | (stop_one + IMG // 2 < token_rows))
    stop_two = jnp.where(has_next, jnp.minimum(stop_one + IMG, stop), stop_one)
    meta_ref[0] = start + HALO
    meta_ref[1] = stop_one - start
    meta_ref[2] = stop_one + HALO
    meta_ref[3] = stop_two - stop_one
    meta_ref[4] = device & (CORES - 1)
    meta_ref[5] = device >> 3
    meta_ref[6] = (device >> 1) & (SQUARE - 1)
    meta_ref[7] = 0
    moves[2].wait()
    moves[3].wait()
    core = device & (CORES - 1)
    inner_ref[...] = tokens_ref[edge_rows(core, 0, token_rows - HALO)]
    outer_ref[...] = tokens_ref[edge_rows(core, 1, token_rows - HALO)]


def read_vector(flat_ref, at, amount):
    return jnp.concatenate([flat_ref[at + i : at + i + 1] for i in range(amount)], axis=1)


def write_vector(flat_ref, at, amount, value):
    for i in range(amount):
        flat_ref[at + i : at + i + 1] = value[:, i * LANES : (i + 1) * LANES]


def read_matrix(flat_ref, at, height, amount, out_ref):
    for i in range(amount):
        chunk = flat_ref[pl.ds(at + i, height, stride=amount), :]
        out_ref[:, i * LANES : (i + 1) * LANES] = chunk.astype(bf16)


def normalise(values):
    average = jnp.mean(values, axis=-1, keepdims=True)
    centred = values - average
    variance = jnp.mean(centred * centred, axis=-1, keepdims=True)
    inverse = lax.rsqrt(variance + epsilon)
    return (centred * inverse, inverse)


def norm_back(grad, unit, inverse, gain):
    scaled = grad * gain
    first = jnp.mean(scaled, axis=-1, keepdims=True)
    second = jnp.mean(scaled * unit, axis=-1, keepdims=True)
    return inverse * (scaled - first - unit * second)


def slot_mask(meta_ref, window, by_column):
    shape = (window, SPAN) if by_column else (SPAN, window)
    spot = lax.broadcasted_iota(jnp.int32, shape, 0 if by_column else 1)
    row = lax.broadcasted_iota(jnp.int32, shape, 1 if by_column else 0)
    start = jnp.where(row < SLOT, meta_ref[0], meta_ref[2] - SLOT)
    limit = jnp.where(row < SLOT, meta_ref[1], meta_ref[3] + SLOT)
    return jnp.where((spot == row + start) & (row < limit), 1.0, 0.0).astype(bf16)


def head_lanes(half):
    lane = lax.broadcasted_iota(jnp.int32, (1, LANES), 1)
    return (lane < HEAD_DIM) if half == 0 else (lane >= HEAD_DIM)


def attend_kernel(
    meta_ref, inner_ref, own_ref, outer_ref,
    mine_ref, other_ref,
    middle_ref, cotangent_ref, inputs_ref, normed_ref, qkv_ref, probability_ref,
    context_ref, classes_ref, w_qkv_ref, w_out_ref, gain_ref,
    flat_ref, window_ref,
):
    window = window_ref.shape[0]
    lay_out_blocks(meta_ref, mine_ref, other_ref, flat_ref)
    read_matrix(flat_ref, W_QKV_AT, D, QKV_ROWS, w_qkv_ref)
    read_matrix(flat_ref, W_OUT_AT, D, D_ROWS, w_out_ref)
    gain = read_vector(flat_ref, GAIN_AT, D_ROWS)
    shift = read_vector(flat_ref, SHIFT_AT, D_ROWS)
    gain_ref[...] = gain
    bias_query = read_vector(flat_ref, BIAS_QUERY_AT, D_ROWS)
    bias_value = read_vector(flat_ref, BIAS_VALUE_AT, D_ROWS)
    bias_out = read_vector(flat_ref, BIAS_OUT_AT, D_ROWS)
    table = (head_mask() * flat_ref[TABLE_AT : TABLE_AT + 1]).astype(bf16)

    own = own_ref.shape[0]
    window_ref[edge_rows(meta_ref[4], 0, HALO + own)] = inner_ref[...]
    window_ref[HALO : HALO + own] = own_ref[...]
    window_ref[edge_rows(meta_ref[4], 1, HALO + own)] = outer_ref[...]
    picked = dot(slot_mask(meta_ref, window, False), window_ref[...])
    inputs = picked[:, :D]
    inputs_ref[...] = inputs.astype(bf16)
    cotangent_ref[...] = picked[:, D : 2 * D].astype(bf16)
    classes_ref[...] = picked[:, 2 * D :].astype(bf16)

    unit, _ = normalise(inputs)
    normed_ref[...] = (unit * gain + shift).astype(bf16)
    normed = normed_ref[...]
    qkv_ref[:, :D] = (dot(normed, w_qkv_ref[:, :D]) + bias_query).astype(bf16)
    qkv_ref[:, D : 2 * D] = dot(normed, w_qkv_ref[:, D : 2 * D]).astype(bf16)
    qkv_ref[:, 2 * D :] = (dot(normed, w_qkv_ref[:, 2 * D :]) + bias_value).astype(bf16)

    for slot in range(2):
        rows = slice(slot * SLOT, (slot + 1) * SLOT)
        key = lax.broadcasted_iota(jnp.int32, (1, SLOT), 1)
        key_bias = dot_cols(table, classes_ref[rows])
        key_bias = jnp.where(key < meta_ref[2 * slot + 1], key_bias, masked_score)
        for pair in range(HEADS // 2):
            lanes = slice(pair * LANES, (pair + 1) * LANES)
            queries = qkv_ref[rows, lanes]
            keys = qkv_ref[rows, D + pair * LANES : D + (pair + 1) * LANES]
            values = qkv_ref[rows, 2 * D + pair * LANES : 2 * D + (pair + 1) * LANES]
            mixed = []
            for half in range(2):
                head = 2 * pair + half
                chosen = jnp.where(head_lanes(half), queries, jnp.zeros_like(queries))
                scores = dot_cols(chosen, keys) * score_scale + key_bias[head : head + 1]
                peak = jnp.max(scores, axis=-1, keepdims=True)
                weights = jnp.exp(scores - peak)
                total = jnp.sum(weights, axis=-1, keepdims=True)
                probability = (weights * (1.0 / total)).astype(bf16)
                probability_ref[slot * HEADS + head] = probability
                mixed.append(dot(probability, values))
            context_ref[rows, lanes] = jnp.where(head_lanes(0), mixed[0], mixed[1]).astype(bf16)
    middle_ref[...] = inputs + dot(context_ref[...], w_out_ref[...]) + bias_out


def feed_kernel(
    meta_ref, middle_ref, cotangent_ref,
    mine_ref, other_ref,
    output_ref, grad_middle_ref, keep_ref, send_ref,
    flat_ref, w_up_ref, w_down_ref, normed_ref,
):
    window = output_ref.shape[0]
    lay_out_blocks(meta_ref, mine_ref, other_ref, flat_ref)
    read_matrix(flat_ref, W_UP_AT, D, FF_ROWS, w_up_ref)
    read_matrix(flat_ref, W_DOWN_AT, FF, D_ROWS, w_down_ref)
    gain = read_vector(flat_ref, GAIN_AT, D_ROWS)
    shift = read_vector(flat_ref, SHIFT_AT, D_ROWS)
    bias_up = read_vector(flat_ref, BIAS_UP_AT, FF_ROWS)
    bias_down = read_vector(flat_ref, BIAS_DOWN_AT, D_ROWS)

    middle = middle_ref[...]
    cotangent = cotangent_ref[...]
    unit, inverse = normalise(middle)
    normed_ref[...] = (unit * gain + shift).astype(bf16)
    normed = normed_ref[...]
    output = middle + bias_down
    grad = jnp.zeros((SPAN, D), f32)
    slope = math.sqrt(2.0 / math.pi)
    for step in range(FF // D):
        cols = slice(step * D, (step + 1) * D)
        w_up = w_up_ref[:, cols]
        w_down = w_down_ref[cols]
        hidden = dot(normed, w_up) + bias_up[:, cols]
        square = hidden * hidden
        bend = jnp.tanh(slope * hidden * (1.0 + 0.044715 * square))
        half = 0.5 * (1.0 + bend)
        active = (hidden * half).astype(bf16)
        steep = half + 0.5 * hidden * (1.0 - bend * bend) * (
            slope * (1.0 + (3 * 0.044715) * square)
        )
        grad_hidden_wide = dot_cols(cotangent, w_down) * steep
        grad_hidden = grad_hidden_wide.astype(bf16)
        output = output + dot(active, w_down)
        grad = grad + dot_cols(grad_hidden, w_up)
        grad_down = dot_rows(active, cotangent)
        grad_up = dot_rows(normed, grad_hidden)
        grad_bias = jnp.sum(grad_hidden.astype(f32), axis=0, keepdims=True)
        write_vector(flat_ref, BIAS_UP_AT + step * D_ROWS, D_ROWS, grad_bias)
        for i in range(D_ROWS):
            lanes = slice(i * LANES, (i + 1) * LANES)
            flat_ref[pl.ds(W_UP_AT + step * D_ROWS + i, D, stride=FF_ROWS), :] = grad_up[:, lanes]
            flat_ref[pl.ds(W_DOWN_AT + step * D * D_ROWS + i, D, stride=D_ROWS), :] = grad_down[
                :, lanes
            ]
    output_ref[...] = dot(slot_mask(meta_ref, window, True), output.astype(bf16)).astype(bf16)
    grad_output = cotangent.astype(f32)
    write_vector(flat_ref, GAIN_AT, D_ROWS, jnp.sum(grad * unit, axis=0, keepdims=True))
    write_vector(flat_ref, SHIFT_AT, D_ROWS, jnp.sum(grad, axis=0, keepdims=True))
    write_vector(flat_ref, BIAS_DOWN_AT, D_ROWS, jnp.sum(grad_output, axis=0, keepdims=True))
    flat_ref[FEED_END:] = jnp.zeros((flat_ref.shape[0] - FEED_END, LANES), f32)
    grad_middle_ref[...] = grad_output + norm_back(grad, unit, inverse, gain)
    cut_blocks(meta_ref, flat_ref, keep_ref, send_ref)


def slot_back(
    slot, qkv_ref, probability_ref, classes_ref, grad_context_ref, grad_qkv_ref
):
    rows = slice(slot * SLOT, (slot + 1) * SLOT)
    key_sums = []
    for pair in range(HEADS // 2):
        lanes = slice(pair * LANES, (pair + 1) * LANES)
        key_lanes = slice(D + pair * LANES, D + (pair + 1) * LANES)
        value_lanes = slice(2 * D + pair * LANES, 2 * D + (pair + 1) * LANES)
        queries = qkv_ref[rows, lanes]
        keys = qkv_ref[rows, key_lanes]
        values = qkv_ref[rows, value_lanes]
        grad_context = grad_context_ref[rows, lanes]
        parts = []
        for half in range(2):
            head = 2 * pair + half
            chosen = jnp.where(head_lanes(half), grad_context, jnp.zeros_like(grad_context))
            grad_probs = dot_cols(chosen, values)
            narrow = probability_ref[slot * HEADS + head]
            probability = narrow.astype(f32)
            weighted = probability * grad_probs
            grad_scores = weighted - probability * jnp.sum(weighted, axis=-1, keepdims=True)
            key_sums.append(jnp.sum(grad_scores, axis=0, keepdims=True))
            grad_raw = (grad_scores * score_scale).astype(bf16)
            parts.append(
                (dot(grad_raw, keys), dot_rows(grad_raw, queries), dot_rows(narrow, grad_context))
            )
        low = head_lanes(0)
        for where, first, second in zip((lanes, key_lanes, value_lanes), *parts):
            grad_qkv_ref[:, where] = jnp.where(low, first, second).astype(bf16)
    sums = jnp.concatenate(key_sums + [jnp.zeros((8 - HEADS, SLOT), f32)], axis=0)
    sums_high = sums.astype(bf16)
    sums_low = (sums - sums_high.astype(f32)).astype(bf16)
    classes = classes_ref[rows]
    return dot(sums_high, classes) + dot(sums_low, classes)


def attend_back_kernel(
    meta_ref, grad_middle_ref, qkv_ref, probability_ref, context_ref, classes_ref, w_out_ref,
    grad_qkv_ref, grad_w_out_ref, grad_bias_out_ref, grad_table_ref, grad_context_ref,
):
    grad_branch = grad_middle_ref[...].astype(bf16)
    grad_bias_out_ref[...] = jnp.sum(grad_branch.astype(f32), axis=0, keepdims=True)
    grad_w_out_ref[...] = dot_rows(context_ref[...], grad_branch)
    grad_context_ref[...] = dot_cols(grad_branch, w_out_ref[...]).astype(bf16)
    grad_table_ref[...] = slot_back(
        0, qkv_ref, probability_ref, classes_ref, grad_context_ref, grad_qkv_ref
    )


def inputs_back_kernel(
    meta_ref, grad_middle_ref, output_ref, inputs_ref, normed_ref, qkv_ref, probability_ref,
    classes_ref, w_qkv_ref, gain_ref,
    grad_first_ref, grad_w_out_ref, grad_bias_out_ref, grad_table_ref, grad_context_ref,
    own_output_ref, own_grad_ref, inner_ref, outer_ref, keep_ref, send_ref,
    flat_ref, grad_second_ref, grad_qkv_ref, grad_inputs_ref,
):
    window = grad_inputs_ref.shape[0]
    grad_table = grad_table_ref[...] + slot_back(
        1, qkv_ref, probability_ref, classes_ref, grad_context_ref, grad_second_ref
    )
    grad_qkv_ref[:SLOT] = grad_first_ref[...]
    grad_qkv_ref[SLOT:] = grad_second_ref[...]
    flat_ref[TABLE_AT:] = jnp.zeros((flat_ref.shape[0] - TABLE_AT, LANES), f32)
    flat_ref[TABLE_AT : TABLE_AT + 1] = jnp.sum(grad_table * head_mask(), axis=0, keepdims=True)
    write_vector(flat_ref, BIAS_OUT_AT, D_ROWS, grad_bias_out_ref[...])
    for i in range(D_ROWS):
        flat_ref[pl.ds(W_OUT_AT + i, D, stride=D_ROWS), :] = grad_w_out_ref[
            :, i * LANES : (i + 1) * LANES
        ]
    grad_qkv = grad_qkv_ref[...]
    column_sums = jnp.sum(grad_qkv.astype(f32), axis=0, keepdims=True)
    write_vector(flat_ref, BIAS_QUERY_AT, D_ROWS, column_sums[:, :D])
    write_vector(flat_ref, BIAS_VALUE_AT, D_ROWS, column_sums[:, 2 * D :])
    normed = normed_ref[...]
    for part in range(3):
        grad_w = dot_rows(normed, grad_qkv_ref[:, part * D : (part + 1) * D])
        for i in range(D_ROWS):
            flat_ref[pl.ds(W_QKV_AT + part * D_ROWS + i, D, stride=QKV_ROWS), :] = grad_w[
                :, i * LANES : (i + 1) * LANES
            ]
    grad_normed = dot_cols(grad_qkv, w_qkv_ref[...])
    gain = gain_ref[...]
    unit, inverse = normalise(inputs_ref[...].astype(f32))
    write_vector(flat_ref, GAIN_AT, D_ROWS, jnp.sum(grad_normed * unit, axis=0, keepdims=True))
    write_vector(flat_ref, SHIFT_AT, D_ROWS, jnp.sum(grad_normed, axis=0, keepdims=True))
    grad_inputs = grad_middle_ref[...] + norm_back(grad_normed, unit, inverse, gain)
    high = grad_inputs.astype(bf16)
    low_part = (grad_inputs - high.astype(f32)).astype(bf16)
    back = slot_mask(meta_ref, window, True)
    grad_inputs_ref[...] = dot(back, high) + dot(back, low_part)
    own = slice(HALO, window - HALO)
    own_output_ref[...] = output_ref[own]
    own_grad_ref[...] = grad_inputs_ref[own]
    for near_core, edge_ref in enumerate((inner_ref, outer_ref)):
        edge = edge_rows(meta_ref[4], near_core, window - HALO)
        edge_ref[:, :D] = output_ref[edge]
        edge_ref[:, D:] = grad_inputs_ref[edge].astype(bf16)
    cut_blocks(meta_ref, flat_ref, keep_ref, send_ref)


def combine_kernel(
    meta_ref, own_output_ref, own_grad_ref, inner_ref, outer_ref, output_ref, grad_inputs_ref
):
    last = output_ref.shape[0] - HALO
    output_ref[HALO:last] = own_output_ref[HALO:last]
    grad_inputs_ref[HALO:last] = own_grad_ref[HALO:last]
    for near_core, edge_ref in enumerate((inner_ref, outer_ref)):
        edge = edge_rows(meta_ref[4], near_core, last)
        output_ref[edge] = (
            own_output_ref[edge].astype(f32) + edge_ref[:, :D].astype(f32)
        ).astype(bf16)
        grad_inputs_ref[edge] = own_grad_ref[edge] + edge_ref[:, D:].astype(f32)


def call_kernel(kernel, out_shapes, scratch, flops, operands, far=(), room=32 * 1024 * 1024):
    vmem = pl.BlockSpec(memory_space=pltpu.VMEM)
    smem = pl.BlockSpec(memory_space=pltpu.SMEM)
    specs = [smem if operand.dtype == jnp.int32 else vmem for operand in operands]
    for index in far:
        specs[index] = pl.BlockSpec(memory_space=pltpu.HBM)
    return pl.pallas_call(
        kernel,
        out_shape=out_shapes,
        in_specs=specs,
        out_specs=[smem if shape.dtype == jnp.int32 else vmem for shape in out_shapes],
        scratch_shapes=scratch,
        compiler_params=pltpu.CompilerParams(vmem_limit_bytes=room),
        cost_estimate=pl.CostEstimate(flops=flops, bytes_accessed=1, transcendentals=0),
    )(*operands)


def struct(shape, kind):
    return jax.ShapeDtypeStruct(shape, kind)


def pack(parts, flops=1):
    packed = struct((len(parts),) + parts[0].shape, bf16)
    return call_kernel(pack_kernel, [packed], [], flops, parts)[0]


def gather_columns(rows, devices):
    depth = devices // (CORES * SQUARE)
    return pack([rows] + pass_layers([rows] * depth, devices), 10**10)


def pass_column(column, devices):
    return pass_on(column, column.shape[0] * CORES * SQUARE, devices)


def join(near, far):
    joined = struct((2 * near.shape[0],) + near.shape[1:], bf16)
    return call_kernel(join_kernel, [joined], [], 1, [near, far])[0]


def add_cores(keep, other):
    parts = [struct(keep.shape[1:], bf16)] * SQUARE
    return call_kernel(add_cores_kernel, parts, [], 1, [keep, other])


def add_chips(parts, passed, flops=1):
    depth, padded, lanes = parts[0].shape
    halves = [struct((depth // 2, padded, lanes), bf16)] * 2
    return call_kernel(add_chips_kernel, halves, [], flops, [parts[0]] + passed)


def add_layers(keep, send, devices):
    half, padded, lanes = keep.shape
    while half > 1:
        other = pass_on(send, half * CORES * SQUARE, devices)
        half //= 2
        halves = [struct((half, padded, lanes), bf16)] * 2
        keep, send = call_kernel(add_layers_kernel, halves, [], 1, [keep, other])
    return (keep, pass_on(send, CORES * SQUARE, devices))


def add_last(keep, other):
    return keep[0].astype(f32) + other[0].astype(f32)


def shards(inputs, attn_blocks, mlp_blocks, image_id, bias_id, out_grad):
    token_rows = inputs.shape[0]
    devices = lax.axis_size("fsdp")
    depth = devices // (CORES * SQUARE)
    window = token_rows + 2 * HALO
    attn_flat = devices * attn_blocks.shape[1] // LANES
    mlp_flat = devices * mlp_blocks.shape[1] // LANES
    barrier = lax.optimization_barrier

    outside = [(i, i + 1) for i in range(1, devices - 1, 2)]
    outside = outside + [(b, a) for a, b in outside]
    tokens, inner, outer, meta = call_kernel(
        functools.partial(prepare_kernel, devices - 1),
        [
            struct((token_rows, WIDE), bf16),
            struct((HALO, WIDE), bf16),
            struct((HALO, WIDE), bf16),
            struct((8,), jnp.int32),
        ],
        [
            pltpu.VMEM((token_rows // LANES, LANES), jnp.int32),
            pltpu.VMEM((token_rows // LANES, LANES), jnp.int32),
            pltpu.SemaphoreType.DMA((4,)),
        ],
        1,
        [
            lax.axis_index("fsdp").astype(jnp.int32).reshape(1),
            image_id.reshape(-1, LANES),
            bias_id.reshape(-1, LANES),
            inputs,
            out_grad,
        ],
        (1, 2, 3, 4),
        60 * 1024 * 1024,
    )
    attn_rows = as_rows(attn_blocks)
    mlp_rows = as_rows(mlp_blocks)
    attn_column = gather_columns(attn_rows, devices)
    mlp_column = join(mlp_rows[None], pass_column(mlp_rows[None], devices))
    attn_column, mlp_column, inner, outer = barrier((attn_column, mlp_column, inner, outer))
    inner = pass_cores(inner, devices)
    inner, outer = barrier((inner, outer))
    outer = lax.ppermute(outer, "fsdp", outside)
    while 2 * mlp_column.shape[0] < depth:
        mlp_column = join(mlp_column, pass_column(mlp_column, devices))
    mlp_far = pass_column(mlp_column, devices)
    attn_passed = pass_chips([attn_column] * SQUARE, devices)
    attn_mine = pack([attn_column] + attn_passed, 10**10)
    attn_mine, outer, mlp_far = barrier((attn_mine, outer, mlp_far))
    mlp_column = join(mlp_column, mlp_far)
    mlp_column, attn_mine, inner, outer = barrier((mlp_column, attn_mine, inner, outer))
    mlp_passed = pass_chips([mlp_column] * SQUARE, devices)
    attn_other = pass_cores(attn_mine, devices)

    (
        middle, cotangent, inputs_span, normed, qkv, probability, context, classes_span,
        w_qkv, w_out, gain,
    ) = call_kernel(
        attend_kernel,
        [
            struct((SPAN, D), f32),
            struct((SPAN, D), bf16),
            struct((SPAN, D), bf16),
            struct((SPAN, D), bf16),
            struct((SPAN, 3 * D), bf16),
            struct((2 * HEADS, SLOT, SLOT), bf16),
            struct((SPAN, D), bf16),
            struct((SPAN, LANES), bf16),
            struct((D, 3 * D), bf16),
            struct((D, D), bf16),
            struct((1, D), f32),
        ],
        [pltpu.VMEM((attn_flat + 16, LANES), f32), pltpu.VMEM((window, WIDE), bf16)],
        1,
        [meta, inner, tokens, outer, attn_mine, attn_other],
    )
    mlp_passed, middle = barrier((mlp_passed, middle))
    mlp_mine = pack([mlp_column] + mlp_passed)
    mlp_other = pass_cores(mlp_mine, devices)
    feed_blocks = struct((SQUARE,) + mlp_column.shape, bf16)
    output, grad_middle, feed_keep, feed_send = call_kernel(
        feed_kernel,
        [struct((window, D), bf16), struct((SPAN, D), f32), feed_blocks, feed_blocks],
        [
            pltpu.VMEM((mlp_flat + 16, LANES), f32),
            pltpu.VMEM((D, FF), bf16),
            pltpu.VMEM((FF, D), bf16),
            pltpu.VMEM((SPAN, D), bf16),
        ],
        1,
        [meta, middle, cotangent, mlp_mine, mlp_other],
    )
    feed_parts = add_cores(feed_keep, pass_cores(feed_send, devices))
    grad_first, grad_w_out, grad_bias_out, grad_table, grad_context = call_kernel(
        attend_back_kernel,
        [
            struct((SLOT, 3 * D), bf16),
            struct((D, D), f32),
            struct((1, D), f32),
            struct((8, LANES), f32),
            struct((SPAN, D), bf16),
        ],
        [],
        1,
        [meta, grad_middle, qkv, probability, context, classes_span, w_out],
    )
    feed_parts, grad_first = barrier((feed_parts, grad_first))
    feed_passed = pass_chips(feed_parts, devices)
    attn_blocks_out = struct((SQUARE,) + attn_column.shape, bf16)
    own_output, own_grad, inner, outer, attn_keep, attn_send = call_kernel(
        inputs_back_kernel,
        [
            struct((token_rows, D), bf16),
            struct((token_rows, D), f32),
            struct((HALO, 2 * D), bf16),
            struct((HALO, 2 * D), bf16),
            attn_blocks_out,
            attn_blocks_out,
        ],
        [
            pltpu.VMEM((attn_flat + 16, LANES), f32),
            pltpu.VMEM((SLOT, 3 * D), bf16),
            pltpu.VMEM((SPAN, 3 * D), bf16),
            pltpu.VMEM((window, D), f32),
        ],
        1,
        [
            meta, grad_middle, output, inputs_span, normed, qkv, probability, classes_span,
            w_qkv, gain, grad_first, grad_w_out, grad_bias_out, grad_table, grad_context,
        ],
    )
    attn_other = pass_cores(attn_send, devices)
    feed_keep, feed_send = add_chips(feed_parts, feed_passed, 10**10)
    outer = lax.ppermute(outer, "fsdp", outside)
    attn_other, feed_keep, feed_send, outer = barrier((attn_other, feed_keep, feed_send, outer))
    attn_parts = list(add_cores(attn_keep, attn_other))
    attn_passed = pass_chips(attn_parts, devices)
    attn_keep, attn_send = add_chips(attn_parts, attn_passed)
    attn_keep, inner = barrier((attn_keep, inner))
    inner = pass_cores(inner, devices)
    feed_keep, feed_other = add_layers(feed_keep, feed_send, devices)
    attn_keep, attn_other = add_layers(attn_keep, attn_send, devices)
    output, grad_inputs = call_kernel(
        combine_kernel,
        [struct((token_rows, D), bf16), struct((token_rows, D), f32)],
        [],
        1,
        [meta, own_output, own_grad, inner, outer],
    )
    attn_other, output, grad_inputs = barrier((attn_other, output, grad_inputs))
    attn_sum = add_last(attn_keep, attn_other)
    feed_sum = add_last(feed_keep, feed_other)
    return (output, grad_inputs, as_block(attn_sum, attn_blocks), as_block(feed_sum, mlp_blocks))


def solution(mesh):
    return jax.shard_map(
        shards,
        mesh=mesh,
        in_specs=(
            P("fsdp", None),
            P("fsdp", None),
            P("fsdp", None),
            P("fsdp"),
            P("fsdp"),
            P("fsdp", None),
        ),
        out_specs=(P("fsdp", None), P("fsdp", None), P("fsdp", None), P("fsdp", None)),
        check_vma=False,
    )
```
